32 devices in a mesh: seq: 32 (over z, y, x, core).
Axes of the slice: x: 2, y: 2, z: 4, core: 2. Of those that a mesh axis runs over, the one named last changes fastest.
Arguments:
- tokens: bfloat16 [16384, 1024], P('seq'), may hold values from -6 to 6
- out_grad: bfloat16 [16384, 1024], P('seq'), may hold values from -6 to 6
- caption_states: bfloat16 [512, 1024], replicated, may hold values from -6 to 6
- query_weight: bfloat16 [1024, 1024], replicated, may hold values from -0.1875 to 0.1875
- key_weight: bfloat16 [1024, 1024], replicated, may hold values from -0.1875 to 0.1875
- value_weight: bfloat16 [1024, 1024], replicated, may hold values from -0.1875 to 0.1875
- output_weight: bfloat16 [1024, 1024], replicated, may hold values from -0.75 to 0.75
- cross_query: bfloat16 [1024, 1024], replicated, may hold values from -0.1875 to 0.1875
- cross_key: bfloat16 [1024, 1024], replicated, may hold values from -0.1875 to 0.1875
- cross_value: bfloat16 [1024, 1024], replicated, may hold values from -0.1875 to 0.1875
- cross_output: bfloat16 [1024, 1024], replicated, may hold values from -0.5 to 0.5
- up_weight: bfloat16 [1024, 4096], replicated, may hold values from -0.1875 to 0.1875
- down_weight: bfloat16 [4096, 1024], replicated, may hold values from -0.09375 to 0.09375
- attn_gain: float32 [1024], replicated, may hold values from 0.5 to 1.5
- attn_bias: float32 [1024], replicated, may hold values from -1.5 to 1.5
- cross_gain: float32 [1024], replicated, may hold values from 0.5 to 1.5
- cross_bias: float32 [1024], replicated, may hold values from -1.5 to 1.5
- mlp_gain: float32 [1024], replicated, may hold values from 0.5 to 1.5
- mlp_bias: float32 [1024], replicated, may hold values from -1.5 to 1.5
- item_ids: int32 [16384], replicated, may hold values from 0 to 23, never falling along the last dimension, each value on 1 to 1024 neighbouring positions
- caption_segments: int32 [4, 128], replicated, may hold values from 0 to 3, never falling along the last dimension, each value on 1 to 64 neighbouring positions
- item_rows: int32 [24], replicated, may hold values from 0 to 3
- item_segments: int32 [24], replicated, may hold values from 0 to 3
Outputs:
- block_output: bfloat16 [16384, 1024], P('seq')
- input_grad: float32 [16384, 1024], P('seq')
- caption_grad: float32 [512, 1024], P('seq')
- query_weight_grad: float32 [1024, 1024], P('seq')
- key_weight_grad: float32 [1024, 1024], P('seq')
- value_weight_grad: float32 [1024, 1024], P('seq')
- output_weight_grad: float32 [1024, 1024], P('seq')
- cross_query_grad: float32 [1024, 1024], P('seq')
- cross_key_grad: float32 [1024, 1024], P('seq')
- cross_value_grad: float32 [1024, 1024], P('seq')
- cross_output_grad: float32 [1024, 1024], P('seq')
- up_weight_grad: float32 [1024, 4096], P('seq')
- down_weight_grad: float32 [4096, 1024], P('seq')
- attn_gain_grad: float32 [1024], P('seq')
- attn_bias_grad: float32 [1024], P('seq')
- cross_gain_grad: float32 [1024], P('seq')
- cross_bias_grad: float32 [1024], P('seq')
- mlp_gain_grad: float32 [1024], P('seq')
- mlp_bias_grad: float32 [1024], P('seq')
The draws below stay inside these ranges and needn't reach their ends.
Inputs may be any that keep to these rules, and one draw needn't show every extreme that they name: `item_ids`: item ids never fall along the stream; each item holds 1 to 1024 consecutive tokens, and one holds exactly 1024. `caption_segments`: within each caption row the ids never fall; every caption has 1 to 64 tokens.
All inputs are finite; a program needn't handle non-finite values.
Results may differ from the reference program's by a relative error of at most 0.017.
Values may be sent and summed in bfloat16 or wider, within the bound.
A program may use at most 256 MiB of HBM per device.

```python
import math
import jax
import jax.numpy as jnp
import numpy as np
from jax import lax

D = 1024
HEADS = 16
HEAD = 64
FF = 4096
ITEM_LEN = 1024
CAP_LEN = 128
CAP_SEGS = 4
TOKENS = 16384
ITEMS = 24
CAP_ROWS = 4
TEXT = 512


def place_ends(array, own_key, low, high):
    longest = array.shape.index(max(array.shape))
    spots = []
    for shift in (0, 1):
        where = [jax.random.randint(jax.random.fold_in(own_key, axis), (), 0, length) for axis, length in enumerate(array.shape)]
        where[longest] = (where[longest] + shift) % array.shape[longest]
        spots.append(tuple(where))
    return array.at[spots[0]].set(low).at[spots[1]].set(high)


def level_of(rng, dims, shards, smallest, largest):
    loudness, own = 1.0, jax.random.fold_in(rng, 6)
    for dim, blocks in shards:
        draws = jnp.exp(jax.random.uniform(jax.random.fold_in(own, dim), (blocks,), jnp.float32, smallest / len(shards), largest / len(shards)))
        loudness = loudness * jnp.repeat(draws, dims[dim] // blocks).reshape([-1 if axis == dim else 1 for axis in range(len(dims))])
    return loudness


def split_up(number_of, total, most, lean):
    portions = [(1 << 20) // math.isqrt(standing ** lean) + 1 for standing in range(2, number_of + 1)]
    spare, counts = total - most - (number_of - 1), [1] * (number_of - 1)
    while spare > 0:
        movable = [i for i in range(number_of - 1) if counts[i] < most]
        whole, left = sum([portions[i] for i in movable]), spare
        for i in movable:
            more = min(most - counts[i], max(1, left * portions[i] // whole), spare)
            counts[i] = counts[i] + more
            spare = spare - more
    return np.array([most] + counts)


def uneven(stream_key, amount, total, most, skew):
    if amount == 2:
        one = jax.random.randint(stream_key, (), max(1, total - most), min(most, total - 1) + 1)
        return jnp.stack([one, total - one])
    tallies = jnp.asarray(split_up(amount, total, most, skew), jnp.int32)
    pairs = (amount - 1) // 2
    source_of, sink = tallies[1:1 + 2 * pairs:2], tallies[2:2 + 2 * pairs:2]
    room = jnp.minimum(source_of - 1, most - sink)
    passed = jax.random.randint(jax.random.fold_in(stream_key, 1), (pairs,), 0, 1 << 20) % (room + 1)
    tallies = tallies.at[1:1 + 2 * pairs:2].set(source_of - passed).at[2:2 + 2 * pairs:2].set(sink + passed)
    return tallies[jax.random.permutation(jax.random.fold_in(stream_key, 2), amount)]


def gaussian(own_key, dims, deviation, bound, shards=(), kind=jnp.bfloat16):
    values = deviation * jax.random.normal(own_key, dims, jnp.float32)
    if shards:
        values = values * level_of(own_key, dims, shards, -0.22, 0.18)
    return jnp.clip(values, -bound, bound).astype(kind)


def setup_inputs(seed: int = 0) -> dict:
    seeds = jax.random.split(jax.random.key(seed), 24)
    tokens = gaussian(seeds[0], (TOKENS, D), 1.0, 6.0, ((0, 32),))
    out_grad = gaussian(seeds[1], (TOKENS, D), 1.0, 6.0, ((0, 32),))
    caption_states = gaussian(seeds[2], (TEXT, D), 1.0, 6.0)
    query_weight = gaussian(seeds[3], (D, D), D ** -0.5, 0.1875)
    key_weight = gaussian(seeds[4], (D, D), D ** -0.5, 0.1875)
    value_weight = gaussian(seeds[5], (D, D), D ** -0.5, 0.1875)
    output_weight = gaussian(seeds[6], (D, D), (D // 16) ** -0.5, 0.75)
    cross_query = gaussian(seeds[7], (D, D), D ** -0.5, 0.1875)
    cross_key = gaussian(seeds[8], (D, D), D ** -0.5, 0.1875)
    cross_value = gaussian(seeds[9], (D, D), D ** -0.5, 0.1875)
    cross_output = gaussian(seeds[10], (D, D), (D // 8) ** -0.5, 0.5)
    up_weight = gaussian(seeds[11], (D, FF), D ** -0.5, 0.1875)
    down_weight = gaussian(seeds[12], (FF, D), FF ** -0.5, 0.09375)
    attn_gain = jnp.clip(1.0 + 0.1 * jax.random.normal(seeds[13], (D,), jnp.float32), 0.5, 1.5)
    attn_bias = gaussian(seeds[14], (D,), 0.3, 1.5, (), jnp.float32)
    cross_gain = jnp.clip(1.0 + 0.1 * jax.random.normal(seeds[15], (D,), jnp.float32), 0.5, 1.5)
    cross_bias = gaussian(seeds[16], (D,), 0.3, 1.5, (), jnp.float32)
    mlp_gain = jnp.clip(1.0 + 0.1 * jax.random.normal(seeds[17], (D,), jnp.float32), 0.5, 1.5)
    mlp_bias = gaussian(seeds[18], (D,), 0.3, 1.5, (), jnp.float32)
    item_ids = jnp.searchsorted(jnp.cumsum(uneven(seeds[19], ITEMS, TOKENS, ITEM_LEN, 0)), jnp.arange(TOKENS), side="right").astype(jnp.int32)
    caption_segments = jax.vmap(lambda own: jnp.searchsorted(jnp.cumsum(uneven(own, CAP_SEGS, CAP_LEN, CAP_LEN // 2, 0)), jnp.arange(CAP_LEN), side="right"))(jax.random.split(seeds[20], CAP_ROWS)).reshape((CAP_ROWS, CAP_LEN)).astype(jnp.int32)
    item_rows = place_ends(jax.random.randint(seeds[21], (ITEMS,), 0, CAP_ROWS), jax.random.fold_in(seeds[21], 1), 0, CAP_ROWS - 1).astype(jnp.int32)
    item_segments = place_ends(jax.random.randint(seeds[22], (ITEMS,), 0, CAP_SEGS), jax.random.fold_in(seeds[22], 1), 0, CAP_SEGS - 1).astype(jnp.int32)
    return dict(tokens=tokens, out_grad=out_grad, caption_states=caption_states, query_weight=query_weight, key_weight=key_weight, value_weight=value_weight, output_weight=output_weight, cross_query=cross_query, cross_key=cross_key, cross_value=cross_value, cross_output=cross_output, up_weight=up_weight, down_weight=down_weight, attn_gain=attn_gain, attn_bias=attn_bias, cross_gain=cross_gain, cross_bias=cross_bias, mlp_gain=mlp_gain, mlp_bias=mlp_bias, item_ids=item_ids, caption_segments=caption_segments, item_rows=item_rows, item_segments=item_segments)


@jax.custom_vjp
def low(v):
    return lax.optimization_barrier(v.astype(jnp.bfloat16)).astype(jnp.float32)

@jax.custom_vjp
def low_back(v):
    return v

def low_keep(v):
    return (low(v), None)

def low_pass(kept, grad):
    return (grad,)

def back_keep(v):
    return (v, None)

def back_low(kept, grad):
    return (low(grad),)
low.defvjp(low_keep, low_pass)
low_back.defvjp(back_keep, back_low)
EPS = 1e-05
NEG = -1e+30
HIGH = lax.Precision.HIGHEST

def rounded(value):
    return low_back(low(value))

def layer_norm(value, gain, bias):
    mean = lax.optimization_barrier(jnp.mean(value, axis=-1, keepdims=True))
    centred = value - mean
    spread = lax.optimization_barrier(jnp.mean(centred * centred, axis=-1, keepdims=True))
    return centred * lax.rsqrt(spread + EPS) * gain + bias

def attend(queries, keys, values, allowed):
    scores = jnp.einsum('qhd,khd->hqk', queries, keys, precision=HIGH) * HEAD ** (-0.5)
    scores = low_back(scores)
    masked = jnp.where(allowed[None], scores, NEG)
    probs = low(jax.nn.softmax(masked, axis=-1))
    result = jnp.einsum('hqk,khd->qhd', probs, values, precision=HIGH)
    return rounded(result)

def self_attention(queries, keys, values, item_ids):
    blocks = TOKENS // ITEM_LEN
    query_heads = queries.reshape(TOKENS, HEADS, HEAD)
    pad = jnp.zeros((ITEM_LEN, D), jnp.float32)
    key_heads = jnp.concatenate([pad, keys], 0).reshape(-1, HEADS, HEAD)
    value_heads = jnp.concatenate([pad, values], 0).reshape(-1, HEADS, HEAD)
    id_padded = jnp.concatenate([jnp.full((ITEM_LEN,), -1, dtype=jnp.int32), item_ids.astype(jnp.int32)], 0)

    def one_block(number):
        start = (number * ITEM_LEN).astype(jnp.int32)
        block_q = lax.dynamic_slice_in_dim(query_heads, start, ITEM_LEN, 0)
        block_k = lax.dynamic_slice_in_dim(key_heads, start, 2 * ITEM_LEN, 0)
        block_v = lax.dynamic_slice_in_dim(value_heads, start, 2 * ITEM_LEN, 0)
        query_pos = start + jnp.arange(ITEM_LEN, dtype=jnp.int32)
        key_pos = start - ITEM_LEN + jnp.arange(2 * ITEM_LEN, dtype=jnp.int32)
        query_item = lax.dynamic_slice_in_dim(item_ids.astype(jnp.int32), start, ITEM_LEN, 0)
        key_item = lax.dynamic_slice_in_dim(id_padded, start, 2 * ITEM_LEN, 0)
        allowed = (key_pos[None, :] >= 0) & (key_pos[None, :] <= query_pos[:, None]) & (key_item[None, :] == query_item[:, None])
        return attend(block_q, block_k, block_v, allowed)
    outputs = lax.map(jax.checkpoint(one_block), jnp.arange(blocks, dtype=jnp.int32))
    return outputs.reshape(TOKENS, D)

def cross_attention(queries, keys, values, item_ids, caption_segments, item_rows, item_segments):
    blocks = TOKENS // ITEM_LEN
    query_heads = queries.reshape(TOKENS, HEADS, HEAD)
    key_heads = keys.reshape(TEXT, HEADS, HEAD)
    value_heads = values.reshape(TEXT, HEADS, HEAD)
    query_row = item_rows[item_ids]
    query_seg = item_segments[item_ids]
    key_row = jnp.arange(TEXT, dtype=jnp.int32) // CAP_LEN
    key_seg = caption_segments.reshape(-1).astype(jnp.int32)

    def one_block(number):
        start = (number * ITEM_LEN).astype(jnp.int32)
        block_q = lax.dynamic_slice_in_dim(query_heads, start, ITEM_LEN, 0)
        row_here = lax.dynamic_slice_in_dim(query_row.astype(jnp.int32), start, ITEM_LEN, 0)
        seg_here = lax.dynamic_slice_in_dim(query_seg.astype(jnp.int32), start, ITEM_LEN, 0)
        allowed = (key_row[None, :] == row_here[:, None]) & (key_seg[None, :] == seg_here[:, None])
        return attend(block_q, key_heads, value_heads, allowed)
    outputs = lax.map(jax.checkpoint(one_block), jnp.arange(blocks, dtype=jnp.int32))
    return outputs.reshape(TOKENS, D)

def reference(tokens, out_grad, caption_states, query_weight, key_weight, value_weight, output_weight, cross_query, cross_key, cross_value, cross_output, up_weight, down_weight, attn_gain, attn_bias, cross_gain, cross_bias, mlp_gain, mlp_bias, item_ids, caption_segments, item_rows, item_segments):
    floats = tuple((a.astype(jnp.float32) for a in (tokens, caption_states, query_weight, key_weight, value_weight, output_weight, cross_query, cross_key, cross_value, cross_output, up_weight, down_weight, attn_gain, attn_bias, cross_gain, cross_bias, mlp_gain, mlp_bias)))

    def forward(inputs, text, wq, wk, wv, wo, cq, ck, cv, co, wup, wdown, gone, bone, gtwo, btwo, gthree, bthree):
        normed_one = low(layer_norm(inputs, gone, bone))
        queries = rounded(jnp.dot(normed_one, wq, precision=HIGH))
        keys = rounded(jnp.dot(normed_one, wk, precision=HIGH))
        values = rounded(jnp.dot(normed_one, wv, precision=HIGH))
        self_att = self_attention(queries, keys, values, item_ids)
        after_one = inputs + low_back(jnp.dot(self_att, wo, precision=HIGH))
        normed_two = low(layer_norm(after_one, gtwo, btwo))
        cross_q = rounded(jnp.dot(normed_two, cq, precision=HIGH))
        text_keys = rounded(jnp.dot(text, ck, precision=HIGH))
        text_values = rounded(jnp.dot(text, cv, precision=HIGH))
        cross_att = cross_attention(cross_q, text_keys, text_values, item_ids, caption_segments, item_rows, item_segments)
        after_two = after_one + low_back(jnp.dot(cross_att, co, precision=HIGH))
        normed_three = low(layer_norm(after_two, gthree, bthree))
        hidden_pre = low_back(jnp.dot(normed_three, wup, precision=HIGH))
        hidden = low(jax.nn.gelu(hidden_pre))
        return after_two + low_back(jnp.dot(hidden, wdown, precision=HIGH))
    result, pullback = jax.vjp(forward, *floats)
    grads = pullback(out_grad.astype(jnp.float32))
    return (result.astype(jnp.bfloat16), grads[0], grads[1], grads[2], grads[3], grads[4], grads[5], grads[6], grads[7], grads[8], grads[9], grads[10], grads[11], grads[12], grads[13], grads[14], grads[15], grads[16], grads[17])
```

```python
import functools

import jax
import jax.numpy as jnp
from jax import lax
from jax.experimental import pallas as pl
from jax.experimental.pallas import tpu as pltpu
from jax.sharding import PartitionSpec as P

HEADS = 16
REACH = 2
EPS = 1e-05
NEG = -1e30
TILE = 256
LANES = 128
AXIS = "seq"
F32 = jnp.float32
BF16 = jnp.bfloat16

NT = (((1,), (1,)), ((), ()))
TN = (((0,), (0,)), ((), ()))


def head_lanes(value, half):
    lane = lax.broadcasted_iota(jnp.int32, value.shape, 1)
    keep = (lane < LANES // 2) if half == 0 else (lane >= LANES // 2)
    return jnp.where(keep, value, jnp.zeros_like(value))


def forward_kernel(causal, sizes, ends, n_ref, qid_ref, kid_ref, q_ref, k_ref, v_ref, o_ref, lse_ref, bias_ref):
    tile = pl.program_id(1)
    span = bias_ref.shape[2]

    @pl.when(pl.program_id(0) == 0)
    def _():
        last = ends[0] + tile * ends[1]
        kid = kid_ref[tile]
        qid = qid_ref[...]
        allowed = kid == qid
        if causal:
            kpos = lax.broadcasted_iota(jnp.int32, (TILE, span), 1)
            qpos = lax.broadcasted_iota(jnp.int32, (TILE, span), 0) + (span - TILE)
            allowed = allowed & (kpos <= qpos)
        bias_ref[tile] = jnp.where(allowed, 0.0, NEG)

    def run(size):
        start = pl.multiple_of(ends[0] + tile * ends[1] - size, TILE)
        keys = k_ref[pl.ds(start, size), :]
        values = v_ref[pl.ds(start, size), :]
        query = q_ref[...] * jnp.asarray(0.125, BF16)
        outs = []
        lses = []
        for half in range(2):
            scores = lax.dot_general(head_lanes(query, half), keys, NT, preferred_element_type=F32)
            scores = scores + bias_ref[tile, :, span - size :]
            row_max = jnp.max(scores, axis=1, keepdims=True)
            weights = jnp.exp(scores - row_max)
            summed = jnp.sum(weights, axis=1, keepdims=True)
            out = jnp.dot(weights.astype(BF16), values, preferred_element_type=F32)
            outs.append(out / summed)
            lses.append(row_max + jnp.log(summed))
        lane = lax.broadcasted_iota(jnp.int32, (TILE, LANES), 1)
        o_ref[...] = jnp.where(lane < LANES // 2, outs[0], outs[1]).astype(BF16)
        lse_ref[0] = jnp.where(lane < LANES // 2, lses[0], lses[1])

    if len(sizes) == 1:
        run(sizes[0])
    else:
        number = n_ref[tile]
        for size in sizes:
            pl.when(number == size // TILE)(functools.partial(run, size))


def attend_forward(queries, keys, values, qid, kid, numbers, causal, sizes, ends):
    rows, width = queries.shape
    tiles = rows // TILE
    pairs = width // LANES
    key_rows = keys.shape[0]
    span = max(sizes)
    flops = 4 * rows * span * width
    return pl.pallas_call(
        functools.partial(forward_kernel, causal, sizes, ends),
        grid_spec=pltpu.PrefetchScalarGridSpec(
            num_scalar_prefetch=1,
            grid=(pairs, tiles),
            in_specs=[
                pl.BlockSpec((TILE, 1), lambda h, t, n: (t, 0)),
                pl.BlockSpec((tiles, 1, span), lambda h, t, n: (0, 0, 0)),
                pl.BlockSpec((TILE, LANES), lambda h, t, n: (t, h)),
                pl.BlockSpec((key_rows, LANES), lambda h, t, n: (0, h)),
                pl.BlockSpec((key_rows, LANES), lambda h, t, n: (0, h)),
            ],
            out_specs=[
                pl.BlockSpec((TILE, LANES), lambda h, t, n: (t, h)),
                pl.BlockSpec((1, TILE, LANES), lambda h, t, n: (h, t, 0)),
            ],
            scratch_shapes=[pltpu.VMEM((tiles, TILE, span), F32)],
        ),
        out_shape=[
            jax.ShapeDtypeStruct((rows, width), BF16),
            jax.ShapeDtypeStruct((pairs, rows, LANES), F32),
        ],
        compiler_params=pltpu.CompilerParams(vmem_limit_bytes=48 << 20),
        cost_estimate=pl.CostEstimate(flops=4 * flops, bytes_accessed=8 << 20, transcendentals=rows * span * HEADS),
    )(numbers, qid, kid, queries, keys, values)


def backward_kernel(
    causal, sizes, ends, n_ref, qid_ref, kid_ref, q_ref, k_ref, v_ref, g_ref, o_ref, lse_ref,
    dq_ref, dk_ref, dv_ref, bias_ref, dk_sum, dv_sum,
):
    tile = pl.program_id(1)
    tiles = pl.num_programs(1)
    span = bias_ref.shape[1]

    @pl.when(pl.program_id(0) == 0)
    def _():
        kid = kid_ref[tile]
        qid = qid_ref[...]
        allowed = kid == qid
        if causal:
            kpos = lax.broadcasted_iota(jnp.int32, (span, TILE), 0)
            qpos = lax.broadcasted_iota(jnp.int32, (span, TILE), 1) + (span - TILE)
            allowed = allowed & (kpos <= qpos)
        bias_ref[tile] = jnp.where(allowed, 0.0, NEG)

    @pl.when(tile == 0)
    def _():
        dk_sum[...] = jnp.zeros_like(dk_sum)
        dv_sum[...] = jnp.zeros_like(dv_sum)

    def run(size):
        start = pl.multiple_of(ends[0] + tile * ends[1] - size, TILE)
        window = pl.ds(start, size)
        keys = k_ref[window, :]
        values = v_ref[window, :]
        query = q_ref[...] * jnp.asarray(0.125, BF16)
        grad = g_ref[...]
        inner = grad.astype(F32) * o_ref[...].astype(F32)
        lse_rows = jnp.transpose(lse_ref[0])
        inner_rows = jnp.transpose(inner)
        half_lanes = LANES // 2
        parts_dq = []
        dk = None
        dv = None
        for half in range(2):
            head_q = head_lanes(query, half)
            head_g = head_lanes(grad, half)
            lse = lse_rows[half * half_lanes : half * half_lanes + 1, :]
            delta = jnp.sum(inner_rows[half * half_lanes : (half + 1) * half_lanes, :], axis=0, keepdims=True)
            scores = lax.dot_general(keys, head_q, NT, preferred_element_type=F32)
            probs = jnp.exp(scores + bias_ref[tile, span - size :, :] - lse)
            grad_probs = lax.dot_general(values, head_g, NT, preferred_element_type=F32)
            grad_scores = (probs * (grad_probs - delta)).astype(BF16)
            probs = probs.astype(BF16)
            part_k = jnp.dot(grad_scores, head_q, preferred_element_type=F32)
            part_v = jnp.dot(probs, head_g, preferred_element_type=F32)
            dk = part_k if dk is None else dk + part_k
            dv = part_v if dv is None else dv + part_v
            parts_dq.append(lax.dot_general(grad_scores, keys, TN, preferred_element_type=F32))
        lane = lax.broadcasted_iota(jnp.int32, (TILE, LANES), 1)
        dq_ref[...] = (jnp.where(lane < half_lanes, parts_dq[0], parts_dq[1]) * 0.125).astype(BF16)
        dk_sum[window, :] += dk
        dv_sum[window, :] += dv

    if len(sizes) == 1:
        run(sizes[0])
    else:
        number = n_ref[tile]
        for size in sizes:
            pl.when(number == size // TILE)(functools.partial(run, size))

    @pl.when(tile == tiles - 1)
    def _():
        dk_ref[...] = dk_sum[...].astype(BF16)
        dv_ref[...] = dv_sum[...].astype(BF16)


def attend_backward(queries, keys, values, grad, out, lse, qid, kid, numbers, causal, sizes, ends):
    rows, width = queries.shape
    tiles = rows // TILE
    pairs = width // LANES
    key_rows = keys.shape[0]
    span = max(sizes)
    flops = 10 * rows * span * width
    near = pl.BlockSpec((TILE, LANES), lambda h, t, n: (t, h))
    wide = pl.BlockSpec((key_rows, LANES), lambda h, t, n: (0, h))
    return pl.pallas_call(
        functools.partial(backward_kernel, causal, sizes, ends),
        grid_spec=pltpu.PrefetchScalarGridSpec(
            num_scalar_prefetch=1,
            grid=(pairs, tiles),
            in_specs=[
                pl.BlockSpec((1, TILE), lambda h, t, n: (0, t)),
                pl.BlockSpec((tiles, span, 1), lambda h, t, n: (0, 0, 0)),
                near,
                wide,
                wide,
                near,
                near,
                pl.BlockSpec((1, TILE, LANES), lambda h, t, n: (h, t, 0)),
            ],
            out_specs=[near, wide, wide],
            scratch_shapes=[
                pltpu.VMEM((tiles, span, TILE), F32),
                pltpu.VMEM((key_rows, LANES), F32),
                pltpu.VMEM((key_rows, LANES), F32),
            ],
        ),
        out_shape=[
            jax.ShapeDtypeStruct((rows, width), BF16),
            jax.ShapeDtypeStruct((key_rows, width), BF16),
            jax.ShapeDtypeStruct((key_rows, width), BF16),
        ],
        compiler_params=pltpu.CompilerParams(vmem_limit_bytes=48 << 20),
        cost_estimate=pl.CostEstimate(flops=4 * flops, bytes_accessed=12 << 20, transcendentals=rows * span * HEADS),
    )(numbers, qid, kid, queries, keys, values, grad, out, lse)


def factors(count):
    return {32: (4, 2, 2, 2), 128: (4, 4, 4, 2)}.get(count, (count,))


def coordinates(count):
    sizes = factors(count)
    left = lax.axis_index(AXIS)
    places = []
    for size in reversed(sizes):
        places.insert(0, lax.rem(left, size))
        left = lax.div(left, size)
    return places


def peers_along(count, axis, step):
    sizes = factors(count)
    stride = 1
    for size in sizes[axis + 1 :]:
        stride *= size
    size = sizes[axis]
    pairs = []
    for device in range(count):
        place = (device // stride) % size
        pairs.append((device, device + ((place + step) % size - place) * stride))
    return pairs


def take(value, place, axis):
    return lax.dynamic_slice_in_dim(value, place, 1, axis)


def total(terms):
    summed = terms[0].astype(F32)
    for term in terms[1:]:
        summed = summed + term.astype(F32)
    return summed


def reduce_scatter(value, order, kind, count):
    sizes = factors(count)
    places = coordinates(count)
    rows, width = value.shape
    terms = [value.reshape(*sizes, rows // count, width)]
    for axis in order:
        size = sizes[axis]
        arrived = []
        for step in range(1, size):
            other = lax.rem(places[axis] + step, size)
            sent = total([take(term, other, axis) for term in terms]).astype(kind)
            arrived.append(lax.ppermute(sent, AXIS, peers_along(count, axis, step)))
        terms = [take(term, places[axis], axis) for term in terms] + arrived
    return total(terms).reshape(rows // count, width)


def all_gather(value, order, count):
    sizes = factors(count)
    places = coordinates(count)
    rows, width = value.shape
    held = value.reshape(*([1] * len(sizes)), rows, width)
    for axis in order:
        size = sizes[axis]
        shape = list(held.shape)
        shape[axis] = size
        gathered = lax.dynamic_update_slice_in_dim(jnp.zeros(shape, held.dtype), held, places[axis], axis)
        for step in range(1, size):
            arrived = lax.ppermute(held, AXIS, peers_along(count, axis, step))
            source = lax.rem(places[axis] + size - step, size)
            gathered = lax.dynamic_update_slice_in_dim(gathered, arrived, source, axis)
        held = gathered
    return held.reshape(rows * count, width)


def matmul(left, right):
    return jnp.dot(left, right, preferred_element_type=F32)


def left_product(left, right):
    return lax.dot_general(left, right, TN, preferred_element_type=F32)


def right_product(left, right):
    return lax.dot_general(left, right, NT, preferred_element_type=F32)


def normalise(value):
    mean = jnp.mean(value, axis=-1, keepdims=True)
    centred = value - mean
    scale = lax.rsqrt(jnp.mean(centred * centred, axis=-1, keepdims=True) + EPS)
    return centred * scale, scale


def norm_back(grad, unit, scale, gain):
    scaled = grad * gain
    return scale * (
        scaled
        - jnp.mean(scaled, axis=-1, keepdims=True)
        - unit * jnp.mean(scaled * unit, axis=-1, keepdims=True)
    )


GELU_A = 0.7978845608028654
GELU_B = 0.044715


def gelu_and_slope(value):
    square = value * value
    bend = jnp.tanh(GELU_A * (value + GELU_B * value * square))
    gate = 0.5 * (1.0 + bend)
    slope = gate + value * 0.5 * (1.0 - bend * bend) * (GELU_A * (1.0 + 3.0 * GELU_B * square))
    return value * gate, slope


def body(
    tokens, out_grad, caption_states,
    query_weight, key_weight, value_weight, output_weight,
    cross_query, cross_key, cross_value, cross_output,
    up_weight, down_weight,
    attn_gain, attn_bias, cross_gain, cross_bias, mlp_gain, mlp_bias,
    item_ids, caption_segments, item_rows, item_segments,
):
    device = lax.axis_index(AXIS)
    count = lax.axis_size(AXIS)
    rows = tokens.shape[0]
    tiles = rows // TILE
    odd = lax.rem(device, 2) == 1
    swap = [(i, i ^ 1) for i in range(count)]
    ahead = [(i, i + 2) for i in range(count - 2)]
    behind = [(i + 2, i) for i in range(count - 2)]

    block_two = lax.ppermute(tokens, AXIS, ahead)
    block_one = lax.ppermute(jnp.where(odd, block_two, tokens), AXIS, swap)
    near_tokens = jnp.concatenate([block_two, block_one, tokens], 0)

    all_ids = jnp.concatenate([jnp.full((REACH * rows,), -1, jnp.int32), item_ids])
    near_ids = lax.dynamic_slice_in_dim(all_ids, device * rows, (REACH + 1) * rows)
    own_ids = near_ids[REACH * rows :]
    near_rows = (REACH + 1) * rows
    span = REACH * rows + TILE
    windows = jnp.stack([near_ids[t * TILE : t * TILE + span] for t in range(tiles)])
    firsts = own_ids[::TILE]
    before = jnp.sum((near_ids[None, :] < firsts[:, None]).astype(jnp.int32), axis=1)
    lasts = REACH * rows + TILE * (1 + jnp.arange(tiles, dtype=jnp.int32))
    numbers = lasts // TILE - before // TILE
    numbers = jnp.clip(numbers, 1, span // TILE)
    self_sizes = tuple(TILE * (i + 1) for i in range(span // TILE))
    self_ends = (REACH * rows + TILE, TILE)

    text = caption_states.shape[0]
    caption_len = caption_segments.shape[1]
    member = own_ids[:, None] == jnp.arange(item_rows.shape[0], dtype=jnp.int32)[None, :]
    codes = item_rows * caption_len + item_segments
    query_code = jnp.sum(jnp.where(member, codes[None, :], 0), axis=1)
    key_code = (jnp.arange(text, dtype=jnp.int32) // caption_len) * caption_len + caption_segments.reshape(-1)
    text_code = jnp.broadcast_to(key_code[None], (tiles, text))
    no_numbers = jnp.zeros((tiles,), jnp.int32)
    text_ends = (text, 0)

    inputs = tokens.astype(F32)
    near_unit, near_scale = normalise(near_tokens.astype(F32))
    near_low = (near_unit * attn_gain + attn_bias).astype(BF16)
    low_one = near_low[REACH * rows :]
    queries = matmul(low_one, query_weight).astype(BF16)
    near_keys = matmul(near_low, key_weight).astype(BF16)
    near_values = matmul(near_low, value_weight).astype(BF16)
    self_att, self_lse = attend_forward(
        queries, near_keys, near_values, own_ids[:, None], windows[:, None, :], numbers, True, self_sizes, self_ends
    )
    after_one = inputs + matmul(self_att, output_weight)
    unit_two, scale_two = normalise(after_one)
    low_two = (unit_two * cross_gain + cross_bias).astype(BF16)
    cross_q = matmul(low_two, cross_query).astype(BF16)
    text_keys = matmul(caption_states, cross_key).astype(BF16)
    text_values = matmul(caption_states, cross_value).astype(BF16)
    cross_att, cross_lse = attend_forward(
        cross_q, text_keys, text_values, query_code[:, None], text_code[:, None, :], no_numbers, False, (text,), text_ends
    )
    after_two = after_one + matmul(cross_att, cross_output)
    unit_three, scale_three = normalise(after_two)
    low_three = (unit_three * mlp_gain + mlp_bias).astype(BF16)
    hidden_pre = matmul(low_three, up_weight)
    hidden, slope = gelu_and_slope(hidden_pre)
    hidden_low = hidden.astype(BF16)
    block_output = (after_two + matmul(hidden_low, down_weight)).astype(BF16)

    grad_pre = (slope * right_product(out_grad, down_weight)).astype(BF16)
    down_grad = left_product(hidden_low, out_grad).astype(BF16)
    up_grad = left_product(low_three, grad_pre).astype(BF16)
    z_, y_, x_, c_ = 0, 1, 2, 3
    one_way = (c_, x_, y_, z_) if len(factors(count)) == 4 else (0,)
    other_way = (c_, y_, x_, z_) if len(factors(count)) == 4 else (0,)
    down_out = reduce_scatter(down_grad, one_way, BF16, count)
    up_out = reduce_scatter(up_grad, other_way, BF16, count)
    grad_three = right_product(grad_pre, up_weight)
    mlp_gain_grad = jnp.sum(grad_three * unit_three, axis=0)
    mlp_bias_grad = jnp.sum(grad_three, axis=0)
    grad_two = out_grad.astype(F32) + norm_back(grad_three, unit_three, scale_three, mlp_gain)
    grad_two_low = grad_two.astype(BF16)

    cross_output_grad = left_product(cross_att, grad_two_low).astype(BF16)
    grad_cross = right_product(grad_two_low, cross_output).astype(BF16)
    grad_cq, grad_tk, grad_tv = attend_backward(
        cross_q, text_keys, text_values, grad_cross, cross_att, cross_lse,
        query_code[None, :], text_code[:, :, None], no_numbers, False, (text,), text_ends,
    )
    own_text = reduce_scatter(jnp.concatenate([grad_tk, grad_tv], 1), one_way, BF16, count).astype(BF16)
    width = grad_tk.shape[1]
    caption_grad = right_product(own_text[:, :width], cross_key) + right_product(own_text[:, width:], cross_value)
    all_text = all_gather(own_text, one_way[::-1], count)
    share = width // count
    caption_part = lax.dynamic_slice_in_dim(caption_states, device * share, share, 1)
    text_weight_grads = left_product(caption_part, all_text)
    cross_key_grad = text_weight_grads[:, :width]
    cross_value_grad = text_weight_grads[:, width:]
    cross_query_grad = left_product(low_two, grad_cq).astype(BF16)
    grad_norm_two = right_product(grad_cq, cross_query)
    cross_gain_grad = jnp.sum(grad_norm_two * unit_two, axis=0)
    cross_bias_grad = jnp.sum(grad_norm_two, axis=0)
    grad_one = grad_two + norm_back(grad_norm_two, unit_two, scale_two, cross_gain)
    grad_one_low = grad_one.astype(BF16)

    output_weight_grad = left_product(self_att, grad_one_low).astype(BF16)
    middle = reduce_scatter(
        jnp.concatenate([cross_output_grad, cross_query_grad, output_weight_grad], 1), other_way, BF16, count
    )
    grad_self = right_product(grad_one_low, output_weight).astype(BF16)
    grad_q, grad_k, grad_v = attend_backward(
        queries, near_keys, near_values, grad_self, self_att, self_lse,
        own_ids[None, :], windows[:, :, None], numbers, True, self_sizes, self_ends,
    )
    grad_near = right_product(grad_k, key_weight) + right_product(grad_v, value_weight)
    grad_own = grad_near[REACH * rows :] + right_product(grad_q, query_weight)
    to_two = grad_near[:rows]
    to_one = grad_near[rows : REACH * rows].astype(BF16)
    from_swap = lax.ppermute(to_one, AXIS, swap).astype(F32)
    to_two = (to_two + jnp.where(odd, from_swap, 0.0)).astype(BF16)
    from_two = lax.ppermute(to_two, AXIS, behind).astype(F32)
    near_sum = jnp.concatenate([grad_near[: REACH * rows], grad_own], 0)
    attn_gain_grad = jnp.sum(near_sum * near_unit, axis=0)
    attn_bias_grad = jnp.sum(near_sum, axis=0)
    grad_norm_one = grad_own + from_two + jnp.where(odd, 0.0, from_swap)
    unit_one = near_unit[REACH * rows :]
    input_grad = grad_one + norm_back(grad_norm_one, unit_one, near_scale[REACH * rows :], attn_gain)
    query_grad = left_product(low_one, grad_q).astype(BF16)
    key_grad = left_product(near_low, grad_k).astype(BF16)
    value_grad = left_product(near_low, grad_v).astype(BF16)
    late = reduce_scatter(jnp.concatenate([query_grad, key_grad, value_grad], 1), one_way, BF16, count)
    vectors = jnp.stack(
        [attn_gain_grad, attn_bias_grad, cross_gain_grad, cross_bias_grad, mlp_gain_grad, mlp_bias_grad], 1
    )
    small = reduce_scatter(vectors, one_way, F32, count)
    return (
        block_output,
        input_grad,
        caption_grad,
        late[:, :width],
        late[:, width : 2 * width],
        late[:, 2 * width :],
        middle[:, 2 * width :],
        middle[:, width : 2 * width],
        cross_key_grad,
        cross_value_grad,
        middle[:, :width],
        up_out,
        down_out,
        small[:, 0],
        small[:, 1],
        small[:, 2],
        small[:, 3],
        small[:, 4],
        small[:, 5],
    )


def solution(mesh):
    split = P(AXIS, None)
    return jax.shard_map(
        body,
        mesh=mesh,
        in_specs=(split, split) + (P(),) * 21,
        out_specs=(split,) * 13 + (P(AXIS),) * 6,
        check_vma=False,
    )
```

```python
import functools

import jax
import jax.numpy as jnp
from jax import lax
from jax.experimental import pallas as pl
from jax.experimental.pallas import tpu as pltpu
from jax.sharding import PartitionSpec as P

HEADS = 16
REACH = 2
EPS = 1e-05
NEG = -1e30
TILE = 256
LANES = 128
AXIS = "seq"
F32 = jnp.float32
BF16 = jnp.bfloat16

NT = (((1,), (1,)), ((), ()))
TN = (((0,), (0,)), ((), ()))


def head_lanes(value, half):
    lane = lax.broadcasted_iota(jnp.int32, value.shape, 1)
    keep = (lane < LANES // 2) if half == 0 else (lane >= LANES // 2)
    return jnp.where(keep, value, jnp.zeros_like(value))


def forward_kernel(causal, sizes, ends, n_ref, qid_ref, kid_ref, q_ref, k_ref, v_ref, o_ref, lse_ref, bias_ref):
    tile = pl.program_id(1)
    span = bias_ref.shape[2]

    @pl.when(pl.program_id(0) == 0)
    def _():
        last = ends[0] + tile * ends[1]
        kid = kid_ref[tile]
        qid = qid_ref[...]
        allowed = kid == qid
        if causal:
            kpos = lax.broadcasted_iota(jnp.int32, (TILE, span), 1)
            qpos = lax.broadcasted_iota(jnp.int32, (TILE, span), 0) + (span - TILE)
            allowed = allowed & (kpos <= qpos)
        bias_ref[tile] = jnp.where(allowed, 0.0, NEG)

    def run(size):
        start = pl.multiple_of(ends[0] + tile * ends[1] - size, TILE)
        keys = k_ref[pl.ds(start, size), :]
        values = v_ref[pl.ds(start, size), :]
        query = q_ref[...] * jnp.asarray(0.125, BF16)
        outs = []
        lses = []
        for half in range(2):
            scores = lax.dot_general(head_lanes(query, half), keys, NT, preferred_element_type=F32)
            scores = scores + bias_ref[tile, :, span - size :]
            row_max = jnp.max(scores, axis=1, keepdims=True)
            weights = jnp.exp(scores - row_max)
            summed = jnp.sum(weights, axis=1, keepdims=True)
            out = jnp.dot(weights.astype(BF16), values, preferred_element_type=F32)
            outs.append(out / summed)
            lses.append(row_max + jnp.log(summed))
        lane = lax.broadcasted_iota(jnp.int32, (TILE, LANES), 1)
        o_ref[...] = jnp.where(lane < LANES // 2, outs[0], outs[1]).astype(BF16)
        lse_ref[0] = jnp.where(lane < LANES // 2, lses[0], lses[1])

    if len(sizes) == 1:
        run(sizes[0])
    else:
        number = n_ref[tile]
        for size in sizes:
            pl.when(number == size // TILE)(functools.partial(run, size))


def attend_forward(queries, keys, values, qid, kid, numbers, causal, sizes, ends):
    rows, width = queries.shape
    tiles = rows // TILE
    pairs = width // LANES
    key_rows = keys.shape[0]
    span = max(sizes)
    flops = 4 * rows * span * width
    return pl.pallas_call(
        functools.partial(forward_kernel, causal, sizes, ends),
        grid_spec=pltpu.PrefetchScalarGridSpec(
            num_scalar_prefetch=1,
            grid=(pairs, tiles),
            in_specs=[
                pl.BlockSpec((TILE, 1), lambda h, t, n: (t, 0)),
                pl.BlockSpec((tiles, 1, span), lambda h, t, n: (0, 0, 0)),
                pl.BlockSpec((TILE, LANES), lambda h, t, n: (t, h)),
                pl.BlockSpec((key_rows, LANES), lambda h, t, n: (0, h)),
                pl.BlockSpec((key_rows, LANES), lambda h, t, n: (0, h)),
            ],
            out_specs=[
                pl.BlockSpec((TILE, LANES), lambda h, t, n: (t, h)),
                pl.BlockSpec((1, TILE, LANES), lambda h, t, n: (h, t, 0)),
            ],
            scratch_shapes=[pltpu.VMEM((tiles, TILE, span), F32)],
        ),
        out_shape=[
            jax.ShapeDtypeStruct((rows, width), BF16),
            jax.ShapeDtypeStruct((pairs, rows, LANES), F32),
        ],
        compiler_params=pltpu.CompilerParams(vmem_limit_bytes=48 << 20),
        cost_estimate=pl.CostEstimate(flops=4 * flops, bytes_accessed=8 << 20, transcendentals=rows * span * HEADS),
    )(numbers, qid, kid, queries, keys, values)


def backward_kernel(
    causal, sizes, ends, n_ref, qid_ref, kid_ref, q_ref, k_ref, v_ref, g_ref, o_ref, lse_ref,
    dq_ref, dk_ref, dv_ref, bias_ref, dk_sum, dv_sum,
):
    tile = pl.program_id(1)
    tiles = pl.num_programs(1)
    span = bias_ref.shape[1]

    @pl.when(pl.program_id(0) == 0)
    def _():
        kid = kid_ref[tile]
        qid = qid_ref[...]
        allowed = kid == qid
        if causal:
            kpos = lax.broadcasted_iota(jnp.int32, (span, TILE), 0)
            qpos = lax.broadcasted_iota(jnp.int32, (span, TILE), 1) + (span - TILE)
            allowed = allowed & (kpos <= qpos)
        bias_ref[tile] = jnp.where(allowed, 0.0, NEG)

    @pl.when(tile == 0)
    def _():
        dk_sum[...] = jnp.zeros_like(dk_sum)
        dv_sum[...] = jnp.zeros_like(dv_sum)

    def run(size):
        start = pl.multiple_of(ends[0] + tile * ends[1] - size, TILE)
        window = pl.ds(start, size)
        keys = k_ref[window, :]
        values = v_ref[window, :]
        query = q_ref[...] * jnp.asarray(0.125, BF16)
        grad = g_ref[...]
        inner = grad.astype(F32) * o_ref[...].astype(F32)
        lse_rows = jnp.transpose(lse_ref[0])
        inner_rows = jnp.transpose(inner)
        half_lanes = LANES // 2
        parts_dq = []
        dk = None
        dv = None
        for half in range(2):
            head_q = head_lanes(query, half)
            head_g = head_lanes(grad, half)
            lse = lse_rows[half * half_lanes : half * half_lanes + 1, :]
            delta = jnp.sum(inner_rows[half * half_lanes : (half + 1) * half_lanes, :], axis=0, keepdims=True)
            scores = lax.dot_general(keys, head_q, NT, preferred_element_type=F32)
            probs = jnp.exp(scores + bias_ref[tile, span - size :, :] - lse)
            grad_probs = lax.dot_general(values, head_g, NT, preferred_element_type=F32)
            grad_scores = (probs * (grad_probs - delta)).astype(BF16)
            probs = probs.astype(BF16)
            part_k = jnp.dot(grad_scores, head_q, preferred_element_type=F32)
            part_v = jnp.dot(probs, head_g, preferred_element_type=F32)
            dk = part_k if dk is None else dk + part_k
            dv = part_v if dv is None else dv + part_v
            parts_dq.append(lax.dot_general(grad_scores, keys, TN, preferred_element_type=F32))
        lane = lax.broadcasted_iota(jnp.int32, (TILE, LANES), 1)
        dq_ref[...] = (jnp.where(lane < half_lanes, parts_dq[0], parts_dq[1]) * 0.125).astype(BF16)
        dk_sum[window, :] += dk
        dv_sum[window, :] += dv

    if len(sizes) == 1:
        run(sizes[0])
    else:
        number = n_ref[tile]
        for size in sizes:
            pl.when(number == size // TILE)(functools.partial(run, size))

    @pl.when(tile == tiles - 1)
    def _():
        dk_ref[...] = dk_sum[...].astype(BF16)
        dv_ref[...] = dv_sum[...].astype(BF16)


def attend_backward(queries, keys, values, grad, out, lse, qid, kid, numbers, causal, sizes, ends):
    rows, width = queries.shape
    tiles = rows // TILE
    pairs = width // LANES
    key_rows = keys.shape[0]
    span = max(sizes)
    flops = 10 * rows * span * width
    near = pl.BlockSpec((TILE, LANES), lambda h, t, n: (t, h))
    wide = pl.BlockSpec((key_rows, LANES), lambda h, t, n: (0, h))
    return pl.pallas_call(
        functools.partial(backward_kernel, causal, sizes, ends),
        grid_spec=pltpu.PrefetchScalarGridSpec(
            num_scalar_prefetch=1,
            grid=(pairs, tiles),
            in_specs=[
                pl.BlockSpec((1, TILE), lambda h, t, n: (0, t)),
                pl.BlockSpec((tiles, span, 1), lambda h, t, n: (0, 0, 0)),
                near,
                wide,
                wide,
                near,
                near,
                pl.BlockSpec((1, TILE, LANES), lambda h, t, n: (h, t, 0)),
            ],
            out_specs=[near, wide, wide],
            scratch_shapes=[
                pltpu.VMEM((tiles, span, TILE), F32),
                pltpu.VMEM((key_rows, LANES), F32),
                pltpu.VMEM((key_rows, LANES), F32),
            ],
        ),
        out_shape=[
            jax.ShapeDtypeStruct((rows, width), BF16),
            jax.ShapeDtypeStruct((key_rows, width), BF16),
            jax.ShapeDtypeStruct((key_rows, width), BF16),
        ],
        compiler_params=pltpu.CompilerParams(vmem_limit_bytes=48 << 20),
        cost_estimate=pl.CostEstimate(flops=4 * flops, bytes_accessed=12 << 20, transcendentals=rows * span * HEADS),
    )(numbers, qid, kid, queries, keys, values, grad, out, lse)


def factors(count):
    return {32: (4, 2, 2, 2), 128: (4, 4, 4, 2)}.get(count, (count,))


def coordinates(count):
    sizes = factors(count)
    left = lax.axis_index(AXIS)
    places = []
    for size in reversed(sizes):
        places.insert(0, lax.rem(left, size))
        left = lax.div(left, size)
    return places


def peers_along(count, axis, step):
    sizes = factors(count)
    stride = 1
    for size in sizes[axis + 1 :]:
        stride *= size
    size = sizes[axis]
    pairs = []
    for device in range(count):
        place = (device // stride) % size
        pairs.append((device, device + ((place + step) % size - place) * stride))
    return pairs


def take(value, place, axis):
    return lax.dynamic_slice_in_dim(value, place, 1, axis)


def total(terms):
    summed = terms[0].astype(F32)
    for term in terms[1:]:
        summed = summed + term.astype(F32)
    return summed


def reduce_scatter(value, order, kind, count):
    sizes = factors(count)
    places = coordinates(count)
    rows, width = value.shape
    terms = [value.reshape(*sizes, rows // count, width)]
    for axis in order:
        size = sizes[axis]
        arrived = []
        for step in range(1, size):
            other = lax.rem(places[axis] + step, size)
            sent = total([take(term, other, axis) for term in terms]).astype(kind)
            arrived.append(lax.ppermute(sent, AXIS, peers_along(count, axis, step)))
        terms = [take(term, places[axis], axis) for term in terms] + arrived
    return total(terms).reshape(rows // count, width)


def all_gather(value, order, count):
    sizes = factors(count)
    places = coordinates(count)
    rows, width = value.shape
    held = value.reshape(*([1] * len(sizes)), rows, width)
    for axis in order:
        size = sizes[axis]
        shape = list(held.shape)
        shape[axis] = size
        gathered = lax.dynamic_update_slice_in_dim(jnp.zeros(shape, held.dtype), held, places[axis], axis)
        for step in range(1, size):
            arrived = lax.ppermute(held, AXIS, peers_along(count, axis, step))
            source = lax.rem(places[axis] + size - step, size)
            gathered = lax.dynamic_update_slice_in_dim(gathered, arrived, source, axis)
        held = gathered
    return held.reshape(rows * count, width)


MESH = pl.DeviceIdType.MESH
BLOCK = 32
WIDE = 1024


def places32():
    me = lax.axis_index(AXIS)
    core = lax.rem(me, 2)
    x = lax.rem(lax.div(me, 2), 2)
    y = lax.rem(lax.div(me, 4), 2)
    z = lax.div(me, 8)
    return me, core, x, y, z


def chunk_of(ref, first_row, first_col, y, x, core):
    return ref.at[:, y, x, core, pl.ds(first_row, BLOCK), pl.ds(first_col, WIDE)]


def reduce_kernel(chunks, n_in, n_out, *refs):
    total = len(chunks)
    ins = refs[:n_in]
    vec_in = refs[n_in]
    outs = refs[n_in + 1 : n_in + 1 + n_out]
    vec_out = refs[n_in + 1 + n_out]
    (own, r0, r1, r2, r3, v0, v1, v2, v3, own_sem, s0, d0, s1, d1, s2, d2, s3, d3, vs, vd) = refs[n_in + n_out + 2 :]
    me, core, x, y, z = places32()
    sibling = me + 1 - 2 * core
    x_peer = me + 2 - 4 * x
    y_peer = me + 4 - 8 * y
    z_other = [lax.rem(z + m, 4) for m in range(1, 4)]
    z_peers = [me + 8 * (o - z) for o in z_other]

    barrier = pltpu.get_barrier_semaphore()
    for peer in (sibling, x_peer, y_peer, *z_peers):
        pl.semaphore_signal(barrier, inc=1, device_id=(peer,), device_id_type=MESH)
    pl.semaphore_wait(barrier, 6)

    def remote(src, dst, send, recv, peer):
        return pltpu.make_async_remote_copy(
            src_ref=src, dst_ref=dst, send_sem=send, recv_sem=recv, device_id=(peer,), device_id_type=MESH
        )

    vec = remote(vec_in.at[1 - core], v0, vs.at[0], vd.at[0], sibling)
    vec.start()
    for c, (number, row, col, *_) in enumerate(chunks):
        for f in range(2):
            for s in range(2):
                yy, xx = (s, f) if c % 2 == 0 else (f, s)
                remote(
                    chunk_of(ins[number], row, col, yy, xx, 1 - core), r0.at[c, f, s], s0.at[c], d0.at[c], sibling
                ).start()
                pltpu.make_async_copy(
                    chunk_of(ins[number], row, col, yy, xx, core), own.at[c, f, s], own_sem.at[c]
                ).start()

    def along(c):
        even = lax.rem(c, 2) == 0
        return (
            jnp.where(even, x, y),
            jnp.where(even, x_peer, y_peer),
            jnp.where(even, y, x),
            jnp.where(even, y_peer, x_peer),
        )

    def add_blocks(count, dst, src):
        @pl.loop(0, count)
        def _(i):
            dst(i)[...] = dst(i)[...] + src(i)[...]

    def first(c):
        f, fp, _, _ = along(c)
        pltpu.make_async_copy(own.at[c], own.at[c], own_sem.at[c]).wait()
        remote(r0.at[c], r0.at[c], s0.at[c], d0.at[c], sibling).wait_recv()
        add_blocks(
            16, lambda i: r0.at[c, i // 8, (i // 4) % 2, i % 4], lambda i: own.at[c, i // 8, (i // 4) % 2, i % 4]
        )
        remote(r0.at[c, 1 - f], r1.at[c], s1.at[c], d1.at[c], fp).start()

    def second(c):
        f, fp, s, sp = along(c)
        remote(r0.at[c, 1 - f], r1.at[c], s1.at[c], d1.at[c], fp).wait_recv()
        add_blocks(8, lambda i: r1.at[c, i // 4, i % 4], lambda i: r0.at[c, f, i // 4, i % 4])
        remote(r1.at[c, 1 - s], r2.at[c], s2.at[c], d2.at[c], sp).start()

    def third(c):
        _, _, s, sp = along(c)
        remote(r1.at[c, 1 - s], r2.at[c], s2.at[c], d2.at[c], sp).wait_recv()
        add_blocks(4, lambda i: r2.at[c, i], lambda i: r1.at[c, s, i])
        for m in range(3):
            remote(r2.at[c, z_other[m]], r3.at[c, m], s3.at[c, m], d3.at[c, m], z_peers[m]).start()

    @pl.loop(0, total + 4)
    def _(k):
        @pl.when(k < total)
        def _():
            first(k)

        @pl.when((k >= 2) & (k < total + 2))
        def _():
            second(k - 2)

        @pl.when(k >= 4)
        def _():
            third(k - 4)

    vec.wait()
    v0[...] += vec_in[core]
    step = remote(v0.at[1 - x], v1, vs.at[1], vd.at[1], x_peer)
    step.start()
    step.wait()
    v1[...] += v0[x]
    step = remote(v1.at[1 - y], v2, vs.at[2], vd.at[2], y_peer)
    step.start()
    step.wait()
    v2[...] += v1[y]
    steps = [remote(v2.at[z_other[m]], v3.at[m], vs.at[3 + m], vd.at[3 + m], z_peers[m]) for m in range(3)]
    for step in steps:
        step.start()
    for step in steps:
        step.wait()
    vec_out[...] = v2[z] + v3[0] + v3[1] + v3[2]

    for c, (_, _, _, number, rows, row, col) in enumerate(chunks):
        for m in range(3):
            remote(r2.at[c, z_other[m]], r3.at[c, m], s3.at[c, m], d3.at[c, m], z_peers[m]).wait()
        summed = r2[c, z].astype(F32) + r3[c, 0].astype(F32) + r3[c, 1].astype(F32) + r3[c, 2].astype(F32)
        outs[number][row : row + rows, col : col + WIDE] = summed[:rows]

    @pl.loop(0, total)
    def _(c):
        f, fp, s, sp = along(c)
        remote(r0.at[c], r0.at[c], s0.at[c], d0.at[c], sibling).wait_send()
        remote(r0.at[c, 1 - f], r1.at[c], s1.at[c], d1.at[c], fp).wait_send()
        remote(r1.at[c, 1 - s], r2.at[c], s2.at[c], d2.at[c], sp).wait_send()


def reduce_all(arrays, vectors):
    ins = []
    chunks = []
    shapes = []
    for array, rows in arrays:
        height = array.shape[0] // 32
        cols = array.shape[1]
        number = len(ins)
        ins.append(array.reshape(4, 2, 2, 2, height, cols))
        shapes.append((rows, cols))
        for row in range(0, height, BLOCK):
            for col in range(0, cols, WIDE):
                chunks.append((number, row, col, number, min(BLOCK, rows - row), row, col))
    total = len(chunks)
    kinds = vectors.shape[0]
    vec = jnp.pad(vectors.reshape(kinds, 32, 32).transpose(1, 0, 2), ((0, 0), (0, 8 - kinds), (0, LANES - 32)))
    vec = vec.reshape(4, 2, 2, 2, 8, LANES).transpose(3, 2, 1, 0, 4, 5)
    vmem = pl.BlockSpec(memory_space=pltpu.VMEM)
    dma = pltpu.SemaphoreType.DMA
    results = pl.pallas_call(
        functools.partial(reduce_kernel, chunks, len(ins), len(ins)),
        in_specs=[pl.BlockSpec(memory_space=pl.ANY)] * len(ins) + [vmem],
        out_specs=[vmem] * (len(ins) + 1),
        out_shape=[jax.ShapeDtypeStruct(shape, F32) for shape in shapes] + [jax.ShapeDtypeStruct((8, LANES), F32)],
        scratch_shapes=[
            pltpu.VMEM((total, 2, 2, 4, BLOCK, WIDE), BF16),
            pltpu.VMEM((total, 2, 2, 4, BLOCK, WIDE), BF16),
            pltpu.VMEM((total, 2, 4, BLOCK, WIDE), BF16),
            pltpu.VMEM((total, 4, BLOCK, WIDE), BF16),
            pltpu.VMEM((total, 3, BLOCK, WIDE), BF16),
            pltpu.VMEM((2, 2, 4, 8, LANES), F32),
            pltpu.VMEM((2, 4, 8, LANES), F32),
            pltpu.VMEM((4, 8, LANES), F32),
            pltpu.VMEM((3, 8, LANES), F32),
            dma((total,)), dma((total,)), dma((total,)), dma((total,)), dma((total,)), dma((total,)), dma((total,)),
            dma((total, 3)), dma((total, 3)), dma((6,)), dma((6,)),
        ],
        compiler_params=pltpu.CompilerParams(collective_id=0, has_side_effects=True, vmem_limit_bytes=62 << 20),
        cost_estimate=pl.CostEstimate(flops=1 << 20, bytes_accessed=64 << 20, transcendentals=0),
    )(*ins, vec)
    return results[:-1], results[-1][:kinds, :32]


def matmul(left, right):
    return jnp.dot(left, right, preferred_element_type=F32)


def left_product(left, right):
    return lax.dot_general(left, right, TN, preferred_element_type=F32)


def right_product(left, right):
    return lax.dot_general(left, right, NT, preferred_element_type=F32)


def normalise(value):
    mean = jnp.mean(value, axis=-1, keepdims=True)
    centred = value - mean
    scale = lax.rsqrt(jnp.mean(centred * centred, axis=-1, keepdims=True) + EPS)
    return centred * scale, scale


def norm_back(grad, unit, scale, gain):
    scaled = grad * gain
    return scale * (
        scaled
        - jnp.mean(scaled, axis=-1, keepdims=True)
        - unit * jnp.mean(scaled * unit, axis=-1, keepdims=True)
    )


GELU_A = 0.7978845608028654
GELU_B = 0.044715


def gelu_and_slope(value):
    square = value * value
    bend = jnp.tanh(GELU_A * (value + GELU_B * value * square))
    gate = 0.5 * (1.0 + bend)
    slope = gate + value * 0.5 * (1.0 - bend * bend) * (GELU_A * (1.0 + 3.0 * GELU_B * square))
    return value * gate, slope


def body(
    tokens, out_grad, caption_states,
    query_weight, key_weight, value_weight, output_weight,
    cross_query, cross_key, cross_value, cross_output,
    up_weight, down_weight,
    attn_gain, attn_bias, cross_gain, cross_bias, mlp_gain, mlp_bias,
    item_ids, caption_segments, item_rows, item_segments,
):
    device = lax.axis_index(AXIS)
    count = lax.axis_size(AXIS)
    rows = tokens.shape[0]
    tiles = rows // TILE
    odd = lax.rem(device, 2) == 1
    swap = [(i, i ^ 1) for i in range(count)]
    ahead = [(i, i + 2) for i in range(count - 2)]
    behind = [(i + 2, i) for i in range(count - 2)]

    block_two = lax.ppermute(tokens, AXIS, ahead)
    block_one = lax.ppermute(jnp.where(odd, block_two, tokens), AXIS, swap)
    near_tokens = jnp.concatenate([block_two, block_one, tokens], 0)

    all_ids = jnp.concatenate([jnp.full((REACH * rows,), -1, jnp.int32), item_ids])
    near_ids = lax.dynamic_slice_in_dim(all_ids, device * rows, (REACH + 1) * rows)
    own_ids = near_ids[REACH * rows :]
    near_rows = (REACH + 1) * rows
    span = REACH * rows + TILE
    windows = jnp.stack([near_ids[t * TILE : t * TILE + span] for t in range(tiles)])
    firsts = own_ids[::TILE]
    before = jnp.sum((near_ids[None, :] < firsts[:, None]).astype(jnp.int32), axis=1)
    lasts = REACH * rows + TILE * (1 + jnp.arange(tiles, dtype=jnp.int32))
    numbers = lasts // TILE - before // TILE
    numbers = jnp.clip(numbers, 1, span // TILE)
    self_sizes = tuple(TILE * (i + 1) for i in range(span // TILE))
    self_ends = (REACH * rows + TILE, TILE)

    text = caption_states.shape[0]
    caption_len = caption_segments.shape[1]
    member = own_ids[:, None] == jnp.arange(item_rows.shape[0], dtype=jnp.int32)[None, :]
    codes = item_rows * caption_len + item_segments
    query_code = jnp.sum(jnp.where(member, codes[None, :], 0), axis=1)
    key_code = (jnp.arange(text, dtype=jnp.int32) // caption_len) * caption_len + caption_segments.reshape(-1)
    text_code = jnp.broadcast_to(key_code[None], (tiles, text))
    no_numbers = jnp.zeros((tiles,), jnp.int32)
    text_ends = (text, 0)

    inputs = tokens.astype(F32)
    near_unit, near_scale = normalise(near_tokens.astype(F32))
    near_low = (near_unit * attn_gain + attn_bias).astype(BF16)
    low_one = near_low[REACH * rows :]
    queries = matmul(low_one, query_weight).astype(BF16)
    near_keys = matmul(near_low, key_weight).astype(BF16)
    near_values = matmul(near_low, value_weight).astype(BF16)
    self_att, self_lse = attend_forward(
        queries, near_keys, near_values, own_ids[:, None], windows[:, None, :], numbers, True, self_sizes, self_ends
    )
    after_one = inputs + matmul(self_att, output_weight)
    unit_two, scale_two = normalise(after_one)
    low_two = (unit_two * cross_gain + cross_bias).astype(BF16)
    cross_q = matmul(low_two, cross_query).astype(BF16)
    text_keys = matmul(caption_states, cross_key).astype(BF16)
    text_values = matmul(caption_states, cross_value).astype(BF16)
    cross_att, cross_lse = attend_forward(
        cross_q, text_keys, text_values, query_code[:, None], text_code[:, None, :], no_numbers, False, (text,), text_ends
    )
    after_two = after_one + matmul(cross_att, cross_output)
    unit_three, scale_three = normalise(after_two)
    low_three = (unit_three * mlp_gain + mlp_bias).astype(BF16)
    hidden_pre = matmul(low_three, up_weight)
    hidden, slope = gelu_and_slope(hidden_pre)
    hidden_low = hidden.astype(BF16)
    block_output = (after_two + matmul(hidden_low, down_weight)).astype(BF16)

    grad_pre = (slope * right_product(out_grad, down_weight)).astype(BF16)
    down_grad = left_product(hidden_low, out_grad).astype(BF16)
    up_grad = left_product(low_three, grad_pre).astype(BF16)
    z_, y_, x_, c_ = 0, 1, 2, 3
    one_way = (c_, x_, y_, z_) if len(factors(count)) == 4 else (0,)
    other_way = (c_, y_, x_, z_) if len(factors(count)) == 4 else (0,)
    fused = count == 32
    grad_three = right_product(grad_pre, up_weight)
    mlp_gain_grad = jnp.sum(grad_three * unit_three, axis=0)
    mlp_bias_grad = jnp.sum(grad_three, axis=0)
    grad_two = out_grad.astype(F32) + norm_back(grad_three, unit_three, scale_three, mlp_gain)
    grad_two_low = grad_two.astype(BF16)

    cross_output_grad = left_product(cross_att, grad_two_low).astype(BF16)
    grad_cross = right_product(grad_two_low, cross_output).astype(BF16)
    grad_cq, grad_tk, grad_tv = attend_backward(
        cross_q, text_keys, text_values, grad_cross, cross_att, cross_lse,
        query_code[None, :], text_code[:, :, None], no_numbers, False, (text,), text_ends,
    )
    width = grad_tk.shape[1]
    cross_key_grad = left_product(caption_states, grad_tk).astype(BF16)
    cross_value_grad = left_product(caption_states, grad_tv).astype(BF16)
    caption_grad = (right_product(grad_tk, cross_key) + right_product(grad_tv, cross_value)).astype(BF16)
    cross_query_grad = left_product(low_two, grad_cq).astype(BF16)
    grad_norm_two = right_product(grad_cq, cross_query)
    cross_gain_grad = jnp.sum(grad_norm_two * unit_two, axis=0)
    cross_bias_grad = jnp.sum(grad_norm_two, axis=0)
    grad_one = grad_two + norm_back(grad_norm_two, unit_two, scale_two, cross_gain)
    grad_one_low = grad_one.astype(BF16)

    output_weight_grad = left_product(self_att, grad_one_low).astype(BF16)
    grad_self = right_product(grad_one_low, output_weight).astype(BF16)
    grad_q, grad_k, grad_v = attend_backward(
        queries, near_keys, near_values, grad_self, self_att, self_lse,
        own_ids[None, :], windows[:, :, None], numbers, True, self_sizes, self_ends,
    )
    grad_near = right_product(grad_k, key_weight) + right_product(grad_v, value_weight)
    grad_own = grad_near[REACH * rows :] + right_product(grad_q, query_weight)
    to_two = grad_near[:rows]
    to_one = grad_near[rows : REACH * rows].astype(BF16)
    from_swap = lax.ppermute(to_one, AXIS, swap).astype(F32)
    to_two = (to_two + jnp.where(odd, from_swap, 0.0)).astype(BF16)
    from_two = lax.ppermute(to_two, AXIS, behind).astype(F32)
    near_sum = jnp.concatenate([grad_near[: REACH * rows], grad_own], 0)
    attn_gain_grad = jnp.sum(near_sum * near_unit, axis=0)
    attn_bias_grad = jnp.sum(near_sum, axis=0)
    grad_norm_one = grad_own + from_two + jnp.where(odd, 0.0, from_swap)
    unit_one = near_unit[REACH * rows :]
    input_grad = grad_one + norm_back(grad_norm_one, unit_one, near_scale[REACH * rows :], attn_gain)
    query_grad = left_product(low_one, grad_q).astype(BF16)
    key_grad = left_product(near_low, grad_k).astype(BF16)
    value_grad = left_product(near_low, grad_v).astype(BF16)
    grads = [
        down_grad, up_grad, cross_output_grad, cross_query_grad, cross_key_grad, cross_value_grad,
        output_weight_grad, query_grad, key_grad, value_grad,
    ]
    vectors = jnp.stack(
        [attn_gain_grad, attn_bias_grad, cross_gain_grad, cross_bias_grad, mlp_gain_grad, mlp_bias_grad]
    )
    if fused:
        share = text // count
        caption_blocks = jnp.pad(caption_grad.reshape(count, share, width), ((0, 0), (0, BLOCK - share), (0, 0)))
        arrays = [(grad, grad.shape[0] // count) for grad in grads]
        arrays.append((caption_blocks.reshape(count * BLOCK, width), share))
        sums, small = reduce_all(arrays, vectors)
    else:
        sums = [
            reduce_scatter(grad, one_way if i % 2 else other_way, BF16, count)
            for i, grad in enumerate([*grads, caption_grad])
        ]
        small = reduce_scatter(vectors.T, one_way, F32, count).T
    (down_out, up_out, cross_output_out, cross_query_out, cross_key_out, cross_value_out,
     output_out, query_out, key_out, value_out, caption_out) = sums
    return (
        block_output, input_grad, caption_out,
        query_out, key_out, value_out, output_out,
        cross_query_out, cross_key_out, cross_value_out, cross_output_out,
        up_out, down_out,
        small[0], small[1], small[2], small[3], small[4], small[5],
    )


def solution(mesh):
    split = P(AXIS, None)
    return jax.shard_map(
        body,
        mesh=mesh,
        in_specs=(split, split) + (P(),) * 21,
        out_specs=(split,) * 13 + (P(AXIS),) * 6,
        check_vma=False,
    )
```

```python
import functools

import jax
import jax.numpy as jnp
from jax import lax
from jax.experimental import pallas as pl
from jax.experimental.pallas import tpu as pltpu
from jax.sharding import PartitionSpec as P

HEADS = 16
REACH = 2
EPS = 1e-05
NEG = -1e30
TILE = 256
LANES = 128
AXIS = "seq"
F32 = jnp.float32
BF16 = jnp.bfloat16

NT = (((1,), (1,)), ((), ()))
TN = (((0,), (0,)), ((), ()))


def head_lanes(value, half):
    lane = lax.broadcasted_iota(jnp.int32, value.shape, 1)
    keep = (lane < LANES // 2) if half == 0 else (lane >= LANES // 2)
    return jnp.where(keep, value, jnp.zeros_like(value))


def forward_kernel(causal, sizes, ends, n_ref, qid_ref, kid_ref, q_ref, k_ref, v_ref, o_ref, lse_ref, bias_ref):
    tile = pl.program_id(1)
    span = bias_ref.shape[2]

    @pl.when(pl.program_id(0) == 0)
    def _():
        last = ends[0] + tile * ends[1]
        kid = kid_ref[tile]
        qid = qid_ref[...]
        allowed = kid == qid
        if causal:
            kpos = lax.broadcasted_iota(jnp.int32, (TILE, span), 1)
            qpos = lax.broadcasted_iota(jnp.int32, (TILE, span), 0) + (span - TILE)
            allowed = allowed & (kpos <= qpos)
        bias_ref[tile] = jnp.where(allowed, 0.0, NEG)

    def run(size):
        start = pl.multiple_of(ends[0] + tile * ends[1] - size, TILE)
        keys = k_ref[pl.ds(start, size), :]
        values = v_ref[pl.ds(start, size), :]
        query = q_ref[...] * jnp.asarray(0.125, BF16)
        outs = []
        lses = []
        for half in range(2):
            scores = lax.dot_general(head_lanes(query, half), keys, NT, preferred_element_type=F32)
            scores = scores + bias_ref[tile, :, span - size :]
            row_max = jnp.max(scores, axis=1, keepdims=True)
            weights = jnp.exp(scores - row_max)
            summed = jnp.sum(weights, axis=1, keepdims=True)
            out = jnp.dot(weights.astype(BF16), values, preferred_element_type=F32)
            outs.append(out / summed)
            lses.append(row_max + jnp.log(summed))
        lane = lax.broadcasted_iota(jnp.int32, (TILE, LANES), 1)
        o_ref[...] = jnp.where(lane < LANES // 2, outs[0], outs[1]).astype(BF16)
        for half in range(2):
            lse_ref[0, half : half + 1, :] = jnp.transpose(jnp.broadcast_to(lses[half], (TILE, LANES)))[:1]

    if len(sizes) == 1:
        run(sizes[0])
    else:
        number = n_ref[tile]
        for size in sizes:
            pl.when(number == size // TILE)(functools.partial(run, size))


def attend_forward(queries, keys, values, qid, kid, numbers, causal, sizes, ends):
    rows, width = queries.shape
    tiles = rows // TILE
    pairs = width // LANES
    key_rows = keys.shape[0]
    span = max(sizes)
    flops = 4 * rows * span * width
    return pl.pallas_call(
        functools.partial(forward_kernel, causal, sizes, ends),
        grid_spec=pltpu.PrefetchScalarGridSpec(
            num_scalar_prefetch=1,
            grid=(pairs, tiles),
            in_specs=[
                pl.BlockSpec((TILE, 1), lambda h, t, n: (t, 0)),
                pl.BlockSpec((tiles, 1, span), lambda h, t, n: (0, 0, 0)),
                pl.BlockSpec((TILE, LANES), lambda h, t, n: (t, h)),
                pl.BlockSpec((key_rows, LANES), lambda h, t, n: (0, h)),
                pl.BlockSpec((key_rows, LANES), lambda h, t, n: (0, h)),
            ],
            out_specs=[
                pl.BlockSpec((TILE, LANES), lambda h, t, n: (t, h)),
                pl.BlockSpec((1, 2, TILE), lambda h, t, n: (h, 0, t)),
            ],
            scratch_shapes=[pltpu.VMEM((tiles, TILE, span), F32)],
        ),
        out_shape=[
            jax.ShapeDtypeStruct((rows, width), BF16),
            jax.ShapeDtypeStruct((pairs, 2, rows), F32),
        ],
        compiler_params=pltpu.CompilerParams(vmem_limit_bytes=48 << 20),
        cost_estimate=pl.CostEstimate(flops=4 * flops, bytes_accessed=8 << 20, transcendentals=rows * span * HEADS),
    )(numbers, qid, kid, queries, keys, values)


def backward_kernel(
    causal, sizes, ends, n_ref, qid_ref, kid_ref, q_ref, k_ref, v_ref, g_ref, o_ref, lse_ref,
    dq_ref, dk_ref, dv_ref, bias_ref, dk_sum, dv_sum,
):
    tile = pl.program_id(1)
    tiles = pl.num_programs(1)
    span = bias_ref.shape[1]

    @pl.when(pl.program_id(0) == 0)
    def _():
        kid = kid_ref[tile]
        qid = qid_ref[...]
        allowed = kid == qid
        if causal:
            kpos = lax.broadcasted_iota(jnp.int32, (span, TILE), 0)
            qpos = lax.broadcasted_iota(jnp.int32, (span, TILE), 1) + (span - TILE)
            allowed = allowed & (kpos <= qpos)
        bias_ref[tile] = jnp.where(allowed, 0.0, NEG)

    @pl.when(tile == 0)
    def _():
        dk_sum[...] = jnp.zeros_like(dk_sum)
        dv_sum[...] = jnp.zeros_like(dv_sum)

    def run(size):
        start = pl.multiple_of(ends[0] + tile * ends[1] - size, TILE)
        window = pl.ds(start, size)
        keys = k_ref[window, :]
        values = v_ref[window, :]
        query = q_ref[...] * jnp.asarray(0.125, BF16)
        grad = g_ref[...]
        inner = grad.astype(F32) * o_ref[...].astype(F32)
        inner_rows = jnp.transpose(inner)
        half_lanes = LANES // 2
        parts_dq = []
        dk = None
        dv = None
        for half in range(2):
            head_q = head_lanes(query, half)
            head_g = head_lanes(grad, half)
            lse = lse_ref[0, half : half + 1, :]
            delta = jnp.sum(inner_rows[half * half_lanes : (half + 1) * half_lanes, :], axis=0, keepdims=True)
            scores = lax.dot_general(keys, head_q, NT, preferred_element_type=F32)
            probs = jnp.exp(scores + bias_ref[tile, span - size :, :] - lse)
            grad_probs = lax.dot_general(values, head_g, NT, preferred_element_type=F32)
            grad_scores = (probs * (grad_probs - delta)).astype(BF16)
            probs = probs.astype(BF16)
            part_k = jnp.dot(grad_scores, head_q, preferred_element_type=F32)
            part_v = jnp.dot(probs, head_g, preferred_element_type=F32)
            dk = part_k if dk is None else dk + part_k
            dv = part_v if dv is None else dv + part_v
            parts_dq.append(lax.dot_general(grad_scores, keys, TN, preferred_element_type=F32))
        lane = lax.broadcasted_iota(jnp.int32, (TILE, LANES), 1)
        dq_ref[...] = (jnp.where(lane < half_lanes, parts_dq[0], parts_dq[1]) * 0.125).astype(BF16)
        dk_sum[window, :] += dk
        dv_sum[window, :] += dv

    if len(sizes) == 1:
        run(sizes[0])
    else:
        number = n_ref[tile]
        for size in sizes:
            pl.when(number == size // TILE)(functools.partial(run, size))

    @pl.when(tile == tiles - 1)
    def _():
        dk_ref[...] = dk_sum[...].astype(BF16)
        dv_ref[...] = dv_sum[...].astype(BF16)


def attend_backward(queries, keys, values, grad, out, lse, qid, kid, numbers, causal, sizes, ends):
    rows, width = queries.shape
    tiles = rows // TILE
    pairs = width // LANES
    key_rows = keys.shape[0]
    span = max(sizes)
    flops = 10 * rows * span * width
    near = pl.BlockSpec((TILE, LANES), lambda h, t, n: (t, h))
    wide = pl.BlockSpec((key_rows, LANES), lambda h, t, n: (0, h))
    return pl.pallas_call(
        functools.partial(backward_kernel, causal, sizes, ends),
        grid_spec=pltpu.PrefetchScalarGridSpec(
            num_scalar_prefetch=1,
            grid=(pairs, tiles),
            in_specs=[
                pl.BlockSpec((1, TILE), lambda h, t, n: (0, t)),
                pl.BlockSpec((tiles, span, 1), lambda h, t, n: (0, 0, 0)),
                near,
                wide,
                wide,
                near,
                near,
                pl.BlockSpec((1, 2, TILE), lambda h, t, n: (h, 0, t)),
            ],
            out_specs=[near, wide, wide],
            scratch_shapes=[
                pltpu.VMEM((tiles, span, TILE), F32),
                pltpu.VMEM((key_rows, LANES), F32),
                pltpu.VMEM((key_rows, LANES), F32),
            ],
        ),
        out_shape=[
            jax.ShapeDtypeStruct((rows, width), BF16),
            jax.ShapeDtypeStruct((key_rows, width), BF16),
            jax.ShapeDtypeStruct((key_rows, width), BF16),
        ],
        compiler_params=pltpu.CompilerParams(vmem_limit_bytes=48 << 20),
        cost_estimate=pl.CostEstimate(flops=4 * flops, bytes_accessed=12 << 20, transcendentals=rows * span * HEADS),
    )(numbers, qid, kid, queries, keys, values, grad, out, lse)


def factors(count):
    return {32: (4, 2, 2, 2), 128: (4, 4, 4, 2)}.get(count, (count,))


def coordinates(count):
    sizes = factors(count)
    left = lax.axis_index(AXIS)
    places = []
    for size in reversed(sizes):
        places.insert(0, lax.rem(left, size))
        left = lax.div(left, size)
    return places


def peers_along(count, axis, step):
    sizes = factors(count)
    stride = 1
    for size in sizes[axis + 1 :]:
        stride *= size
    size = sizes[axis]
    pairs = []
    for device in range(count):
        place = (device // stride) % size
        pairs.append((device, device + ((place + step) % size - place) * stride))
    return pairs


def take(value, place, axis):
    return lax.dynamic_slice_in_dim(value, place, 1, axis)


def total(terms):
    summed = terms[0].astype(F32)
    for term in terms[1:]:
        summed = summed + term.astype(F32)
    return summed


def reduce_scatter(value, order, kind, count):
    sizes = factors(count)
    places = coordinates(count)
    rows, width = value.shape
    terms = [value.reshape(*sizes, rows // count, width)]
    for axis in order:
        size = sizes[axis]
        arrived = []
        for step in range(1, size):
            other = lax.rem(places[axis] + step, size)
            sent = total([take(term, other, axis) for term in terms]).astype(kind)
            arrived.append(lax.ppermute(sent, AXIS, peers_along(count, axis, step)))
        terms = [take(term, places[axis], axis) for term in terms] + arrived
    return total(terms).reshape(rows // count, width)


def all_gather(value, order, count):
    sizes = factors(count)
    places = coordinates(count)
    rows, width = value.shape
    held = value.reshape(*([1] * len(sizes)), rows, width)
    for axis in order:
        size = sizes[axis]
        shape = list(held.shape)
        shape[axis] = size
        gathered = lax.dynamic_update_slice_in_dim(jnp.zeros(shape, held.dtype), held, places[axis], axis)
        for step in range(1, size):
            arrived = lax.ppermute(held, AXIS, peers_along(count, axis, step))
            source = lax.rem(places[axis] + size - step, size)
            gathered = lax.dynamic_update_slice_in_dim(gathered, arrived, source, axis)
        held = gathered
    return held.reshape(rows * count, width)


MESH = pl.DeviceIdType.MESH
BLOCK = 32
WIDE = 1024


def places32():
    me = lax.axis_index(AXIS)
    core = lax.rem(me, 2)
    x = lax.rem(lax.div(me, 2), 2)
    y = lax.rem(lax.div(me, 4), 2)
    z = lax.div(me, 8)
    return me, core, x, y, z


SLOTS = 2
LANDINGS = 9
HALF = LANES // 2


def chunk_of(ref, first_row, first_col, y, x, core):
    return ref.at[:, y, x, core, pl.ds(first_row, BLOCK), pl.ds(first_col, WIDE)]


def normalise_rows(value):
    mean = jnp.mean(value, axis=-1, keepdims=True)
    centred = value - mean
    scale = lax.rsqrt(jnp.mean(centred * centred, axis=-1, keepdims=True) + EPS)
    return centred * scale, scale


IN_HBM = (
    "queries", "near_keys", "near_values", "self_att", "grad_self", "near_low", "near_tokens", "grad_one",
    "query_weight", "key_weight", "value_weight",
)
IN_VMEM = ("vectors", "starts", "self_lse", "attn_gain")
SCRATCH = (
    "arena", "sums", "accum_k", "accum_v", "back_one", "back_two", "vec", "vec_in",
    "tiles", "r0", "r1", "r2", "r3",
    "load", "own_sem", "s0", "d0", "s1", "d1", "s2", "d2", "s3", "d3", "vs", "vd", "bs", "bd", "credit",
)


def layer_kernel(chunks, rows, n_in, n_out, *refs):
    total = len(chunks)
    made = total - 3
    ins = refs[:n_in]
    refs = refs[n_in:]
    hbm = dict(zip(IN_HBM, refs))
    refs = refs[len(IN_HBM) :]
    near = dict(zip(IN_VMEM, refs))
    refs = refs[len(IN_VMEM) :]
    outs = refs[:n_out]
    vec_out, input_grad = refs[n_out : n_out + 2]
    held = dict(zip(SCRATCH, refs[n_out + 2 :]))
    arena, tiles = held["arena"], held["tiles"]
    r0, r1, r2, r3 = held["r0"], held["r1"], held["r2"], held["r3"]
    s0, d0, s1, d1, s2, d2, s3, d3 = (held[name] for name in ("s0", "d0", "s1", "d1", "s2", "d2", "s3", "d3"))
    own_sem, credit, load = held["own_sem"], held["credit"], held["load"]
    sums = held["sums"]
    vec = held["vec"]

    me, core, x, y, z = places32()
    sibling = me + 1 - 2 * core
    x_peer = me + 2 - 4 * x
    y_peer = me + 4 - 8 * y
    z_other = [lax.rem(z + m, 4) for m in range(1, 4)]
    z_peers = [me + 8 * (o - z) for o in z_other]
    has_before = me >= 2
    has_after = me < 30

    barrier = pltpu.get_barrier_semaphore()
    for peer in (sibling, x_peer, y_peer, *z_peers):
        pl.semaphore_signal(barrier, inc=1, device_id=(peer,), device_id_type=MESH)

    @pl.when(has_before)
    def _():
        pl.semaphore_signal(barrier, inc=1, device_id=(me - 2,), device_id_type=MESH)

    @pl.when(has_after)
    def _():
        pl.semaphore_signal(barrier, inc=1, device_id=(me + 2,), device_id_type=MESH)

    def fetch(name, place, number, at=None, dst=None):
        source = hbm[name] if at is None else at
        target = arena.at[pl.ds(place, source.shape[0])] if dst is None else dst
        return pltpu.make_async_copy(source, target, load.at[number])

    q_at, k_at, v_at, g_at, o_at = 0, rows, 4 * rows, 7 * rows, 8 * rows
    low_at = 9 * rows
    wq_at, wk_at, wv_at = 12 * rows, 14 * rows, 7 * rows

    first_loads = [
        fetch("queries", q_at, 0), fetch("near_keys", k_at, 1), fetch("near_values", v_at, 2),
        fetch("grad_self", g_at, 3), fetch("self_att", o_at, 4), fetch("near_low", low_at, 5),
        fetch("query_weight", wq_at, 6), fetch("key_weight", wk_at, 7),
    ]
    for copy in first_loads:
        copy.start()

    pl.semaphore_wait(barrier, 6 + jnp.where(has_before, 1, 0) + jnp.where(has_after, 1, 0))

    def remote(src, dst, send, recv, peer):
        return pltpu.make_async_remote_copy(
            src_ref=src, dst_ref=dst, send_sem=send, recv_sem=recv, device_id=(peer,), device_id_type=MESH
        )

    def along(c):
        even = lax.rem(c, 2) == 0
        return (
            jnp.where(even, x, y),
            jnp.where(even, x_peer, y_peer),
            jnp.where(even, y, x),
            jnp.where(even, y_peer, x_peer),
        )

    def add_blocks(count, dst, src):
        @pl.loop(0, count)
        def _(i):
            dst(i)[...] = dst(i)[...] + src(i)[...]

    def take_credit(c):
        if c >= LANDINGS:
            pl.semaphore_wait(credit, 1)

    def stage(c):
        number, row, col = chunks[c][:3]
        take_credit(c)
        for f in range(2):
            for s in range(2):
                yy, xx = (s, f) if c % 2 == 0 else (f, s)
                remote(
                    chunk_of(ins[number], row, col, yy, xx, 1 - core), r0.at[c % LANDINGS, f, s], s0.at[c], d0.at[c],
                    sibling,
                ).start()
                pltpu.make_async_copy(
                    chunk_of(ins[number], row, col, yy, xx, core), tiles.at[c % SLOTS, core, f, s], own_sem.at[c]
                ).start()

    def make(c, left_at, right_at, depth):
        take_credit(c)

        @pl.loop(0, 4)
        def _(zz):
            left = arena[pl.ds(left_at, depth), pl.ds(pl.multiple_of(zz * TILE, TILE), TILE)]
            for part in range(2):
                cols = slice(part * (WIDE // 2), (part + 1) * (WIDE // 2))
                result = lax.dot_general(left, arena[pl.ds(right_at, depth), cols], TN, preferred_element_type=F32)
                result = result.astype(BF16)
                for block in range(8):
                    yy, xx, cc = block // 4, (block // 2) % 2, block % 2
                    f, s = (xx, yy) if c % 2 == 0 else (yy, xx)
                    tiles[c % SLOTS, cc, f, s, zz, :, cols] = result[block * BLOCK : (block + 1) * BLOCK]

        remote(tiles.at[c % SLOTS, 1 - core], r0.at[c % LANDINGS], s0.at[c], d0.at[c], sibling).start()

    def first(c):
        f, fp, _, _ = along(c)
        slot, place = c % SLOTS, c % LANDINGS
        if c < made:
            pltpu.make_async_copy(tiles.at[slot, core], tiles.at[slot, core], own_sem.at[c]).wait()
        copy = remote(tiles.at[slot, 1 - core], r0.at[place], s0.at[c], d0.at[c], sibling)
        copy.wait_recv()
        add_blocks(
            16,
            lambda i: r0.at[place, i // 8, (i // 4) % 2, i % 4],
            lambda i: tiles.at[slot, core, i // 8, (i // 4) % 2, i % 4],
        )
        remote(r0.at[place, 1 - f], r1.at[c], s1.at[c], d1.at[c], fp).start()
        copy.wait_send()

    def second(c):
        f, fp, s, sp = along(c)
        place = lax.rem(c, LANDINGS)
        copy = remote(r0.at[place, 1 - f], r1.at[c], s1.at[c], d1.at[c], fp)
        copy.wait_recv()
        add_blocks(8, lambda i: r1.at[c, i // 4, i % 4], lambda i: r0.at[place, f, i // 4, i % 4])
        remote(r1.at[c, 1 - s], r2.at[c], s2.at[c], d2.at[c], sp).start()
        copy.wait_send()

        @pl.when(c < total - LANDINGS)
        def _():
            pl.semaphore_signal(credit, inc=1, device_id=(sibling,), device_id_type=MESH)

    def third(c):
        _, _, s, sp = along(c)
        copy = remote(r1.at[c, 1 - s], r2.at[c], s2.at[c], d2.at[c], sp)
        copy.wait_recv()
        add_blocks(4, lambda i: r2.at[c, i], lambda i: r1.at[c, s, i])
        for m in range(3):
            remote(r2.at[c, z_other[m]], r3.at[c, m], s3.at[c, m], d3.at[c, m], z_peers[m]).start()
        copy.wait_send()

    def last(c):
        number, height, row, col = chunks[c][3:]
        for m in range(3):
            remote(r2.at[c, z_other[m]], r3.at[c, m], s3.at[c, m], d3.at[c, m], z_peers[m]).wait()
        summed = r2[c, z].astype(F32) + r3[c, 0].astype(F32) + r3[c, 1].astype(F32) + r3[c, 2].astype(F32)
        outs[number][row : row + height, col : col + WIDE] = summed[:height]

    stage(0)
    stage(1)
    for c in range(made):
        first(c)
        if c >= 5:
            second(c - 5)
        if c + SLOTS < made:
            stage(c + SLOTS)

    for copy in first_loads[:5]:
        copy.wait()
    half_lanes = LANES // 2
    span = 2 * rows + TILE

    def self_step(i):
        h, t = lax.div(i, 2), lax.rem(i, 2)
        lanes = pl.ds(pl.multiple_of(h * LANES, LANES), LANES)
        own = pl.multiple_of(t * TILE, TILE)
        mine = pl.ds(q_at + own, TILE)
        keys = arena[pl.ds(k_at + own, span), lanes]
        values = arena[pl.ds(v_at + own, span), lanes]
        query = arena[mine, lanes] * jnp.asarray(0.125, BF16)
        grad = arena[pl.ds(g_at + own, TILE), lanes]
        inner = jnp.transpose(grad.astype(F32) * arena[pl.ds(o_at + own, TILE), lanes].astype(F32))
        kpos = lax.broadcasted_iota(jnp.int32, (span, TILE), 0)
        qpos = lax.broadcasted_iota(jnp.int32, (TILE, TILE), 1)
        dpos = lax.broadcasted_iota(jnp.int32, (TILE, TILE), 0)
        start = near["starts"][:, pl.ds(own, TILE)] - own
        allowed = kpos >= start
        allowed = jnp.concatenate([allowed[: span - TILE], allowed[span - TILE :] & (dpos <= qpos)], 0)

        @pl.when(t == 0)
        def _():
            held["accum_k"][span:] = jnp.zeros((3 * rows - span, LANES), F32)
            held["accum_v"][span:] = jnp.zeros((3 * rows - span, LANES), F32)
            held["accum_k"][:span] = jnp.zeros((span, LANES), F32)
            held["accum_v"][:span] = jnp.zeros((span, LANES), F32)

        parts = []
        dk = None
        dv = None
        for half in range(2):
            head_q = head_lanes(query, half)
            head_g = head_lanes(grad, half)
            lse = near["self_lse"][h, half : half + 1, pl.ds(own, TILE)]
            delta = jnp.sum(inner[half * half_lanes : (half + 1) * half_lanes], axis=0, keepdims=True)
            scores = lax.dot_general(keys, head_q, NT, preferred_element_type=F32)
            probs = jnp.where(allowed, jnp.exp(jnp.where(allowed, scores - lse, 0.0)), 0.0)
            grad_probs = lax.dot_general(values, head_g, NT, preferred_element_type=F32)
            grad_scores = (probs * (grad_probs - delta)).astype(BF16)
            probs = probs.astype(BF16)
            part_k = jnp.dot(grad_scores, head_q, preferred_element_type=F32)
            part_v = jnp.dot(probs, head_g, preferred_element_type=F32)
            dk = part_k if dk is None else dk + part_k
            dv = part_v if dv is None else dv + part_v
            parts.append(lax.dot_general(grad_scores, keys, TN, preferred_element_type=F32))
        lane = lax.broadcasted_iota(jnp.int32, (TILE, LANES), 1)
        arena[mine, lanes] = (jnp.where(lane < half_lanes, parts[0], parts[1]) * 0.125).astype(BF16)
        window = pl.ds(own, span)
        held["accum_k"][window] += dk
        held["accum_v"][window] += dv

        @pl.when(t == 1)
        def _():
            arena[pl.ds(k_at, 3 * rows), lanes] = held["accum_k"][...].astype(BF16)
            arena[pl.ds(v_at, 3 * rows), lanes] = held["accum_v"][...].astype(BF16)

    @pl.loop(0, 16)
    def _(i):
        self_step(i)
        step = lax.div(i, 2)

        @pl.when(lax.rem(i, 2) == 0)
        def _():
            third(step)

        @pl.when((lax.rem(i, 2) == 1) & (step + made - 5 < made))
        def _():
            second(step + made - 5)

    value_weight = fetch("value_weight", wv_at, 3)
    value_weight.start()
    for copy in first_loads[5:]:
        copy.wait()
    own_low = low_at + 2 * rows
    make(made, own_low, q_at, rows)

    def norm_grad(j):
        @pl.loop(0, 4)
        def _(n):
            cols = pl.ds(pl.multiple_of(n * TILE, TILE), TILE)
            result = lax.dot_general(
                arena[pl.ds(k_at + j * rows, rows), :], arena[pl.ds(wk_at + n * TILE, TILE), :], NT,
                preferred_element_type=F32,
            )
            result += lax.dot_general(
                arena[pl.ds(v_at + j * rows, rows), :], arena[pl.ds(wv_at + n * TILE, TILE), :], NT,
                preferred_element_type=F32,
            )
            if j == 2:
                result += lax.dot_general(
                    arena[pl.ds(q_at, rows), :], arena[pl.ds(wq_at + n * TILE, TILE), :], NT,
                    preferred_element_type=F32,
                )
            sums[0, :, cols] = result

    vec[...] = near["vectors"][...]

    STEP = 64

    def gains(j, token_at):
        @pl.loop(0, rows // STEP)
        def _(i):
            here = pl.ds(pl.multiple_of(i * STEP, STEP), STEP)
            unit, _ = normalise_rows(arena[pl.ds(token_at + i * STEP, STEP), :].astype(F32))
            grad = sums[0, here, :]
            vec[0:1] += jnp.sum(grad * unit, axis=0, keepdims=True)
            vec[1:2] += jnp.sum(grad, axis=0, keepdims=True)

    value_weight.wait()
    norm_grad(1)
    first(made)
    make(made + 1, low_at, k_at, 3 * rows)
    third(8)
    first(made + 1)
    make(made + 2, low_at, v_at, 3 * rows)
    third(9)
    first(made + 2)
    token_copy = fetch("near_tokens", low_at, 5)
    token_copy.start()
    grad_copy = pltpu.make_async_copy(hbm["grad_one"], sums.at[1], load.at[0])
    grad_copy.start()
    token_copy.wait()
    back_one, back_two = held["back_one"], held["back_two"]
    bs, bd = held["bs"], held["bd"]
    gains(1, low_at + rows)

    def as_low(dst, extra):
        @pl.loop(0, rows // STEP)
        def _(i):
            here = pl.ds(pl.multiple_of(i * STEP, STEP), STEP)
            value = sums[0, here, :]
            if extra is not None:
                value = value + jnp.where(core == 1, extra[here, :].astype(F32), 0.0)
            dst[here, :] = value.astype(BF16)

    as_low(back_one.at[0], None)
    swap = remote(back_one.at[0], back_one.at[1], bs.at[0], bd.at[0], sibling)
    swap.start()
    norm_grad(0)
    gains(0, low_at)
    swap.wait()
    as_low(back_two.at[0], back_one.at[1])
    send_back = remote(back_two.at[0], back_two.at[1], bs.at[1], bd.at[1], me - 2)

    @pl.when(has_before)
    def _():
        send_back.start()

    norm_grad(2)
    gains(2, low_at + 2 * rows)

    vs, vd = held["vs"], held["vd"]
    vec_in = held["vec_in"]

    def vec_step(number, peer, slot):
        step = remote(vec, vec_in.at[slot], vs.at[number], vd.at[number], peer)
        step.start()
        return step

    step = vec_step(0, sibling, 0)
    step.wait()
    vec[...] += vec_in[0]
    step = vec_step(1, x_peer, 1)
    for c in range(10, made):
        third(c)
    step.wait()
    vec[...] += vec_in[1]
    step = vec_step(2, y_peer, 2)
    for c in range(made, total):
        second(c)
    step.wait()
    vec[...] += vec_in[2]
    steps = [vec_step(3 + m, z_peers[m], 3 + m) for m in range(3)]

    grad_copy.wait()

    @pl.when(has_before)
    def _():
        send_back.wait_send()

    @pl.when(has_after)
    def _():
        send_back.wait_recv()

    gain = near["attn_gain"][...]

    @pl.loop(0, rows // STEP)
    def _(i):
        here = pl.ds(pl.multiple_of(i * STEP, STEP), STEP)
        unit, scale = normalise_rows(arena[pl.ds(low_at + 2 * rows + i * STEP, STEP), :].astype(F32))
        grad = sums[0, here, :]
        grad = grad + jnp.where(core == 0, back_one[1, here, :].astype(F32), 0.0)
        grad = grad + jnp.where(has_after, back_two[1, here, :].astype(F32), 0.0)
        scaled = grad * gain
        back = scale * (
            scaled - jnp.mean(scaled, axis=-1, keepdims=True) - unit * jnp.mean(scaled * unit, axis=-1, keepdims=True)
        )
        sums[1, here, :] += back

    out_copy = pltpu.make_async_copy(sums.at[1], input_grad, load.at[0])
    out_copy.start()

    for c in range(made, total):
        third(c)
    for step in steps:
        step.wait()
    vec_out[...] = vec[...] + vec_in[3] + vec_in[4] + vec_in[5]
    for c in range(total):
        last(c)
    out_copy.wait()


def layer_tail(arrays, hbm, vmem, rows):
    ins = []
    chunks = []
    shapes = []
    for array, height_out in arrays:
        height = array.shape[0] // 32
        cols = array.shape[1]
        number = len(ins)
        ins.append(array.reshape(4, 2, 2, 2, height, cols))
        shapes.append((height_out, cols))
        for row in range(0, height, BLOCK):
            for col in range(0, cols, WIDE):
                chunks.append((number, row, col, number, min(BLOCK, height_out - row), row, col))
    for i in range(3):
        chunks.append((None, 0, 0, len(shapes), BLOCK, 0, 0))
        shapes.append((BLOCK, WIDE))
    total = len(chunks)
    local = pl.BlockSpec(memory_space=pltpu.VMEM)
    anywhere = pl.BlockSpec(memory_space=pl.ANY)
    dma = pltpu.SemaphoreType.DMA
    width = hbm["queries"].shape[1]
    scratch = dict(
        arena=pltpu.VMEM((16 * rows, width), BF16),
        sums=pltpu.VMEM((2, rows, width), F32),
        accum_k=pltpu.VMEM((3 * rows, LANES), F32),
        accum_v=pltpu.VMEM((3 * rows, LANES), F32),
        back_one=pltpu.VMEM((2, rows, width), BF16),
        back_two=pltpu.VMEM((2, rows, width), BF16),
        vec=pltpu.VMEM((8, width), F32),
        vec_in=pltpu.VMEM((6, 8, width), F32),
        tiles=pltpu.VMEM((SLOTS, 2, 2, 2, 4, BLOCK, WIDE), BF16),
        r0=pltpu.VMEM((LANDINGS, 2, 2, 4, BLOCK, WIDE), BF16),
        r1=pltpu.VMEM((total, 2, 4, BLOCK, WIDE), BF16),
        r2=pltpu.VMEM((total, 4, BLOCK, WIDE), BF16),
        r3=pltpu.VMEM((total, 3, BLOCK, WIDE), BF16),
        load=dma((8,)), own_sem=dma((total,)), s0=dma((total,)), d0=dma((total,)), s1=dma((total,)), d1=dma((total,)),
        s2=dma((total,)), d2=dma((total,)), s3=dma((total, 3)), d3=dma((total, 3)), vs=dma((6,)), vd=dma((6,)),
        bs=dma((2,)), bd=dma((2,)), credit=pltpu.SemaphoreType.REGULAR,
    )
    results = pl.pallas_call(
        functools.partial(layer_kernel, chunks, rows, len(ins), len(shapes)),
        in_specs=[anywhere] * (len(ins) + len(IN_HBM)) + [local] * len(IN_VMEM),
        out_specs=[local] * (len(shapes) + 1) + [anywhere],
        out_shape=[jax.ShapeDtypeStruct(shape, F32) for shape in shapes]
        + [jax.ShapeDtypeStruct((8, width), F32), jax.ShapeDtypeStruct((rows, width), F32)],
        scratch_shapes=[scratch[name] for name in SCRATCH],
        compiler_params=pltpu.CompilerParams(collective_id=0, has_side_effects=True, vmem_limit_bytes=63 << 20),
        cost_estimate=pl.CostEstimate(flops=1 << 34, bytes_accessed=64 << 20, transcendentals=0),
    )(*ins, *[hbm[name] for name in IN_HBM], *[vmem[name] for name in IN_VMEM])
    return results[:-2], results[-2], results[-1]


def matmul(left, right):
    return jnp.dot(left, right, preferred_element_type=F32)


def left_product(left, right):
    return lax.dot_general(left, right, TN, preferred_element_type=F32)


def right_product(left, right):
    return lax.dot_general(left, right, NT, preferred_element_type=F32)


def normalise(value):
    mean = jnp.mean(value, axis=-1, keepdims=True)
    centred = value - mean
    scale = lax.rsqrt(jnp.mean(centred * centred, axis=-1, keepdims=True) + EPS)
    return centred * scale, scale


def norm_back(grad, unit, scale, gain):
    scaled = grad * gain
    return scale * (
        scaled
        - jnp.mean(scaled, axis=-1, keepdims=True)
        - unit * jnp.mean(scaled * unit, axis=-1, keepdims=True)
    )


GELU_A = 0.7978845608028654
GELU_B = 0.044715


def gelu_and_slope(value):
    square = value * value
    bend = jnp.tanh(GELU_A * (value + GELU_B * value * square))
    gate = 0.5 * (1.0 + bend)
    slope = gate + value * 0.5 * (1.0 - bend * bend) * (GELU_A * (1.0 + 3.0 * GELU_B * square))
    return value * gate, slope


def body(
    tokens, out_grad, caption_states,
    query_weight, key_weight, value_weight, output_weight,
    cross_query, cross_key, cross_value, cross_output,
    up_weight, down_weight,
    attn_gain, attn_bias, cross_gain, cross_bias, mlp_gain, mlp_bias,
    item_ids, caption_segments, item_rows, item_segments,
):
    device = lax.axis_index(AXIS)
    count = lax.axis_size(AXIS)
    rows = tokens.shape[0]
    tiles = rows // TILE
    odd = lax.rem(device, 2) == 1
    swap = [(i, i ^ 1) for i in range(count)]
    ahead = [(i, i + 2) for i in range(count - 2)]
    behind = [(i + 2, i) for i in range(count - 2)]

    block_two = lax.ppermute(tokens, AXIS, ahead)
    block_one = lax.ppermute(jnp.where(odd, block_two, tokens), AXIS, swap)
    near_tokens = jnp.concatenate([block_two, block_one, tokens], 0)

    all_ids = jnp.concatenate([jnp.full((REACH * rows,), -1, jnp.int32), item_ids])
    near_ids = lax.dynamic_slice_in_dim(all_ids, device * rows, (REACH + 1) * rows)
    own_ids = near_ids[REACH * rows :]
    near_rows = (REACH + 1) * rows
    span = REACH * rows + TILE
    windows = jnp.stack([near_ids[t * TILE : t * TILE + span] for t in range(tiles)])
    firsts = own_ids[::TILE]
    before = jnp.sum((near_ids[None, :] < firsts[:, None]).astype(jnp.int32), axis=1)
    lasts = REACH * rows + TILE * (1 + jnp.arange(tiles, dtype=jnp.int32))
    numbers = lasts // TILE - before // TILE
    numbers = jnp.clip(numbers, 1, span // TILE)
    self_sizes = tuple(TILE * (i + 1) for i in range(span // TILE))
    self_ends = (REACH * rows + TILE, TILE)

    text = caption_states.shape[0]
    caption_len = caption_segments.shape[1]
    member = own_ids[:, None] == jnp.arange(item_rows.shape[0], dtype=jnp.int32)[None, :]
    codes = item_rows * caption_len + item_segments
    query_code = jnp.sum(jnp.where(member, codes[None, :], 0), axis=1)
    key_code = (jnp.arange(text, dtype=jnp.int32) // caption_len) * caption_len + caption_segments.reshape(-1)
    text_code = jnp.broadcast_to(key_code[None], (tiles, text))
    no_numbers = jnp.zeros((tiles,), jnp.int32)
    text_ends = (text, 0)

    inputs = tokens.astype(F32)
    near_unit, near_scale = normalise(near_tokens.astype(F32))
    near_low = (near_unit * attn_gain + attn_bias).astype(BF16)
    low_one = near_low[REACH * rows :]
    queries = matmul(low_one, query_weight).astype(BF16)
    near_keys = matmul(near_low, key_weight).astype(BF16)
    near_values = matmul(near_low, value_weight).astype(BF16)
    self_att, self_lse = attend_forward(
        queries, near_keys, near_values, own_ids[:, None], windows[:, None, :], numbers, True, self_sizes, self_ends
    )
    after_one = inputs + matmul(self_att, output_weight)
    unit_two, scale_two = normalise(after_one)
    low_two = (unit_two * cross_gain + cross_bias).astype(BF16)
    cross_q = matmul(low_two, cross_query).astype(BF16)
    text_keys = matmul(caption_states, cross_key).astype(BF16)
    text_values = matmul(caption_states, cross_value).astype(BF16)
    cross_att, cross_lse = attend_forward(
        cross_q, text_keys, text_values, query_code[:, None], text_code[:, None, :], no_numbers, False, (text,), text_ends
    )
    after_two = after_one + matmul(cross_att, cross_output)
    unit_three, scale_three = normalise(after_two)
    low_three = (unit_three * mlp_gain + mlp_bias).astype(BF16)
    hidden_pre = matmul(low_three, up_weight)
    hidden, slope = gelu_and_slope(hidden_pre)
    hidden_low = hidden.astype(BF16)
    block_output = (after_two + matmul(hidden_low, down_weight)).astype(BF16)

    grad_pre = (slope * right_product(out_grad, down_weight)).astype(BF16)
    down_grad = left_product(hidden_low, out_grad).astype(BF16)
    up_grad = left_product(low_three, grad_pre).astype(BF16)
    z_, y_, x_, c_ = 0, 1, 2, 3
    one_way = (c_, x_, y_, z_) if len(factors(count)) == 4 else (0,)
    other_way = (c_, y_, x_, z_) if len(factors(count)) == 4 else (0,)
    fused = count == 32
    grad_three = right_product(grad_pre, up_weight)
    mlp_gain_grad = jnp.sum(grad_three * unit_three, axis=0)
    mlp_bias_grad = jnp.sum(grad_three, axis=0)
    grad_two = out_grad.astype(F32) + norm_back(grad_three, unit_three, scale_three, mlp_gain)
    grad_two_low = grad_two.astype(BF16)

    cross_output_grad = left_product(cross_att, grad_two_low).astype(BF16)
    grad_cross = right_product(grad_two_low, cross_output).astype(BF16)
    grad_cq, grad_tk, grad_tv = attend_backward(
        cross_q, text_keys, text_values, grad_cross, cross_att, cross_lse,
        query_code[None, :], text_code[:, :, None], no_numbers, False, (text,), text_ends,
    )
    width = grad_tk.shape[1]
    cross_key_grad = left_product(caption_states, grad_tk).astype(BF16)
    cross_value_grad = left_product(caption_states, grad_tv).astype(BF16)
    caption_grad = (right_product(grad_tk, cross_key) + right_product(grad_tv, cross_value)).astype(BF16)
    cross_query_grad = left_product(low_two, grad_cq).astype(BF16)
    grad_norm_two = right_product(grad_cq, cross_query)
    cross_gain_grad = jnp.sum(grad_norm_two * unit_two, axis=0)
    cross_bias_grad = jnp.sum(grad_norm_two, axis=0)
    grad_one = grad_two + norm_back(grad_norm_two, unit_two, scale_two, cross_gain)
    grad_one_low = grad_one.astype(BF16)

    output_weight_grad = left_product(self_att, grad_one_low).astype(BF16)
    grad_self = right_product(grad_one_low, output_weight).astype(BF16)
    grads = [
        down_grad, up_grad, cross_output_grad, cross_query_grad, cross_key_grad, cross_value_grad, output_weight_grad,
    ]
    none = jnp.zeros_like(attn_gain)
    vectors = jnp.stack([none, none, cross_gain_grad, cross_bias_grad, mlp_gain_grad, mlp_bias_grad, none, none])
    if fused:
        share = text // count
        caption_blocks = jnp.pad(caption_grad.reshape(count, share, width), ((0, 0), (0, BLOCK - share), (0, 0)))
        arrays = [(grad, grad.shape[0] // count) for grad in grads]
        arrays.append((caption_blocks.reshape(count * BLOCK, width), share))
        starts = jnp.sum((near_ids[None, :] < own_ids[:, None]).astype(jnp.int32), axis=1)
        sums, small, input_grad = layer_tail(
            arrays,
            dict(
                queries=queries, near_keys=near_keys, near_values=near_values, self_att=self_att, grad_self=grad_self,
                near_low=near_low, near_tokens=near_tokens, grad_one=grad_one,
                query_weight=query_weight, key_weight=key_weight, value_weight=value_weight,
            ),
            dict(vectors=vectors, starts=starts[None, :], self_lse=self_lse, attn_gain=attn_gain[None, :]),
            rows,
        )
        (down_out, up_out, cross_output_out, cross_query_out, cross_key_out, cross_value_out,
         output_out, caption_out, query_out, key_out, value_out) = sums
        small = lax.dynamic_slice_in_dim(small, device * (width // count), width // count, 1)
    else:
        grad_q, grad_k, grad_v = attend_backward(
            queries, near_keys, near_values, grad_self, self_att, self_lse,
            own_ids[None, :], windows[:, :, None], numbers, True, self_sizes, self_ends,
        )
        grad_near = right_product(grad_k, key_weight) + right_product(grad_v, value_weight)
        grad_own = grad_near[REACH * rows :] + right_product(grad_q, query_weight)
        to_two = grad_near[:rows]
        to_one = grad_near[rows : REACH * rows].astype(BF16)
        from_swap = lax.ppermute(to_one, AXIS, swap).astype(F32)
        to_two = (to_two + jnp.where(odd, from_swap, 0.0)).astype(BF16)
        from_two = lax.ppermute(to_two, AXIS, behind).astype(F32)
        near_sum = jnp.concatenate([grad_near[: REACH * rows], grad_own], 0)
        attn_gain_grad = jnp.sum(near_sum * near_unit, axis=0)
        attn_bias_grad = jnp.sum(near_sum, axis=0)
        grad_norm_one = grad_own + from_two + jnp.where(odd, 0.0, from_swap)
        unit_one = near_unit[REACH * rows :]
        input_grad = grad_one + norm_back(grad_norm_one, unit_one, near_scale[REACH * rows :], attn_gain)
        query_grad = left_product(low_one, grad_q).astype(BF16)
        key_grad = left_product(near_low, grad_k).astype(BF16)
        value_grad = left_product(near_low, grad_v).astype(BF16)
        vectors = vectors.at[0].set(attn_gain_grad).at[1].set(attn_bias_grad)
        sums = [
            reduce_scatter(grad, one_way if i % 2 else other_way, BF16, count)
            for i, grad in enumerate([*grads, query_grad, key_grad, value_grad, caption_grad])
        ]
        small = reduce_scatter(vectors.T, one_way, F32, count).T
        (down_out, up_out, cross_output_out, cross_query_out, cross_key_out, cross_value_out,
         output_out, query_out, key_out, value_out, caption_out) = sums
    return (
        block_output, input_grad, caption_out,
        query_out, key_out, value_out, output_out,
        cross_query_out, cross_key_out, cross_value_out, cross_output_out,
        up_out, down_out,
        small[0], small[1], small[2], small[3], small[4], small[5],
    )


def solution(mesh):
    split = P(AXIS, None)
    return jax.shard_map(
        body,
        mesh=mesh,
        in_specs=(split, split) + (P(),) * 21,
        out_specs=(split,) * 13 + (P(AXIS),) * 6,
        check_vma=False,
    )
```

```python
import functools
from typing import Any, NamedTuple

import jax
import jax.numpy as jnp
from jax import lax
from jax.experimental import pallas as pl
from jax.experimental.pallas import tpu as pltpu
from jax.sharding import PartitionSpec as P

HEADS = 16
REACH = 2
EPS = 1e-05
NEG = -1e30
TILE = 256
LANES = 128
AXIS = "seq"
F32 = jnp.float32
BF16 = jnp.bfloat16

NT = (((1,), (1,)), ((), ()))
TN = (((0,), (0,)), ((), ()))


def head_lanes(value, half):
    lane = lax.broadcasted_iota(jnp.int32, value.shape, 1)
    keep = (lane < LANES // 2) if half == 0 else (lane >= LANES // 2)
    return jnp.where(keep, value, jnp.zeros_like(value))


def forward_kernel(causal, sizes, ends, n_ref, qid_ref, kid_ref, q_ref, k_ref, v_ref, o_ref, lse_ref, bias_ref):
    tile = pl.program_id(1)
    span = bias_ref.shape[2]

    @pl.when(pl.program_id(0) == 0)
    def _():
        last = ends[0] + tile * ends[1]
        kid = kid_ref[tile]
        qid = qid_ref[...]
        allowed = kid == qid
        if causal:
            kpos = lax.broadcasted_iota(jnp.int32, (TILE, span), 1)
            qpos = lax.broadcasted_iota(jnp.int32, (TILE, span), 0) + (span - TILE)
            allowed = allowed & (kpos <= qpos)
        bias_ref[tile] = jnp.where(allowed, 0.0, NEG)

    def run(size):
        start = pl.multiple_of(ends[0] + tile * ends[1] - size, TILE)
        keys = k_ref[pl.ds(start, size), :]
        values = v_ref[pl.ds(start, size), :]
        query = q_ref[...] * jnp.asarray(0.125, BF16)
        outs = []
        lses = []
        for half in range(2):
            scores = lax.dot_general(head_lanes(query, half), keys, NT, preferred_element_type=F32)
            scores = scores + bias_ref[tile, :, span - size :]
            row_max = jnp.max(scores, axis=1, keepdims=True)
            weights = jnp.exp(scores - row_max)
            summed = jnp.sum(weights, axis=1, keepdims=True)
            out = jnp.dot(weights.astype(BF16), values, preferred_element_type=F32)
            outs.append(out / summed)
            lses.append(row_max + jnp.log(summed))
        lane = lax.broadcasted_iota(jnp.int32, (TILE, LANES), 1)
        o_ref[...] = jnp.where(lane < LANES // 2, outs[0], outs[1]).astype(BF16)
        for half in range(2):
            lse_ref[0, half : half + 1, :] = jnp.transpose(jnp.broadcast_to(lses[half], (TILE, LANES)))[:1]

    if len(sizes) == 1:
        run(sizes[0])
    else:
        number = n_ref[tile]
        for size in sizes:
            pl.when(number == size // TILE)(functools.partial(run, size))


def attend_forward(queries, keys, values, qid, kid, numbers, causal, sizes, ends):
    rows, width = queries.shape
    tiles = rows // TILE
    pairs = width // LANES
    key_rows = keys.shape[0]
    span = max(sizes)
    flops = 4 * rows * span * width
    return pl.pallas_call(
        functools.partial(forward_kernel, causal, sizes, ends),
        grid_spec=pltpu.PrefetchScalarGridSpec(
            num_scalar_prefetch=1,
            grid=(pairs, tiles),
            in_specs=[
                pl.BlockSpec((TILE, 1), lambda h, t, n: (t, 0)),
                pl.BlockSpec((tiles, 1, span), lambda h, t, n: (0, 0, 0)),
                pl.BlockSpec((TILE, LANES), lambda h, t, n: (t, h)),
                pl.BlockSpec((key_rows, LANES), lambda h, t, n: (0, h)),
                pl.BlockSpec((key_rows, LANES), lambda h, t, n: (0, h)),
            ],
            out_specs=[
                pl.BlockSpec((TILE, LANES), lambda h, t, n: (t, h)),
                pl.BlockSpec((1, 2, TILE), lambda h, t, n: (h, 0, t)),
            ],
            scratch_shapes=[pltpu.VMEM((tiles, TILE, span), F32)],
        ),
        out_shape=[
            jax.ShapeDtypeStruct((rows, width), BF16),
            jax.ShapeDtypeStruct((pairs, 2, rows), F32),
        ],
        compiler_params=pltpu.CompilerParams(vmem_limit_bytes=48 << 20),
        cost_estimate=pl.CostEstimate(flops=4 * flops, bytes_accessed=8 << 20, transcendentals=rows * span * HEADS),
    )(numbers, qid, kid, queries, keys, values)


def backward_kernel(
    causal, sizes, ends, n_ref, qid_ref, kid_ref, q_ref, k_ref, v_ref, g_ref, o_ref, lse_ref,
    dq_ref, dk_ref, dv_ref, bias_ref, dk_sum, dv_sum,
):
    tile = pl.program_id(1)
    tiles = pl.num_programs(1)
    span = bias_ref.shape[1]

    @pl.when(pl.program_id(0) == 0)
    def _():
        kid = kid_ref[tile]
        qid = qid_ref[...]
        allowed = kid == qid
        if causal:
            kpos = lax.broadcasted_iota(jnp.int32, (span, TILE), 0)
            qpos = lax.broadcasted_iota(jnp.int32, (span, TILE), 1) + (span - TILE)
            allowed = allowed & (kpos <= qpos)
        bias_ref[tile] = jnp.where(allowed, 0.0, NEG)

    @pl.when(tile == 0)
    def _():
        dk_sum[...] = jnp.zeros_like(dk_sum)
        dv_sum[...] = jnp.zeros_like(dv_sum)

    def run(size):
        start = pl.multiple_of(ends[0] + tile * ends[1] - size, TILE)
        window = pl.ds(start, size)
        keys = k_ref[window, :]
        values = v_ref[window, :]
        query = q_ref[...] * jnp.asarray(0.125, BF16)
        grad = g_ref[...]
        inner = grad.astype(F32) * o_ref[...].astype(F32)
        inner_rows = jnp.transpose(inner)
        half_lanes = LANES // 2
        parts_dq = []
        dk = None
        dv = None
        for half in range(2):
            head_q = head_lanes(query, half)
            head_g = head_lanes(grad, half)
            lse = lse_ref[0, half : half + 1, :]
            delta = jnp.sum(inner_rows[half * half_lanes : (half + 1) * half_lanes, :], axis=0, keepdims=True)
            scores = lax.dot_general(keys, head_q, NT, preferred_element_type=F32)
            probs = jnp.exp(scores + bias_ref[tile, span - size :, :] - lse)
            grad_probs = lax.dot_general(values, head_g, NT, preferred_element_type=F32)
            grad_scores = (probs * (grad_probs - delta)).astype(BF16)
            probs = probs.astype(BF16)
            part_k = jnp.dot(grad_scores, head_q, preferred_element_type=F32)
            part_v = jnp.dot(probs, head_g, preferred_element_type=F32)
            dk = part_k if dk is None else dk + part_k
            dv = part_v if dv is None else dv + part_v
            parts_dq.append(lax.dot_general(grad_scores, keys, TN, preferred_element_type=F32))
        lane = lax.broadcasted_iota(jnp.int32, (TILE, LANES), 1)
        dq_ref[...] = (jnp.where(lane < half_lanes, parts_dq[0], parts_dq[1]) * 0.125).astype(BF16)
        dk_sum[window, :] += dk
        dv_sum[window, :] += dv

    if len(sizes) == 1:
        run(sizes[0])
    else:
        number = n_ref[tile]
        for size in sizes:
            pl.when(number == size // TILE)(functools.partial(run, size))

    @pl.when(tile == tiles - 1)
    def _():
        dk_ref[...] = dk_sum[...].astype(BF16)
        dv_ref[...] = dv_sum[...].astype(BF16)


def attend_backward(queries, keys, values, grad, out, lse, qid, kid, numbers, causal, sizes, ends):
    rows, width = queries.shape
    tiles = rows // TILE
    pairs = width // LANES
    key_rows = keys.shape[0]
    span = max(sizes)
    flops = 10 * rows * span * width
    near = pl.BlockSpec((TILE, LANES), lambda h, t, n: (t, h))
    wide = pl.BlockSpec((key_rows, LANES), lambda h, t, n: (0, h))
    return pl.pallas_call(
        functools.partial(backward_kernel, causal, sizes, ends),
        grid_spec=pltpu.PrefetchScalarGridSpec(
            num_scalar_prefetch=1,
            grid=(pairs, tiles),
            in_specs=[
                pl.BlockSpec((1, TILE), lambda h, t, n: (0, t)),
                pl.BlockSpec((tiles, span, 1), lambda h, t, n: (0, 0, 0)),
                near,
                wide,
                wide,
                near,
                near,
                pl.BlockSpec((1, 2, TILE), lambda h, t, n: (h, 0, t)),
            ],
            out_specs=[near, wide, wide],
            scratch_shapes=[
                pltpu.VMEM((tiles, span, TILE), F32),
                pltpu.VMEM((key_rows, LANES), F32),
                pltpu.VMEM((key_rows, LANES), F32),
            ],
        ),
        out_shape=[
            jax.ShapeDtypeStruct((rows, width), BF16),
            jax.ShapeDtypeStruct((key_rows, width), BF16),
            jax.ShapeDtypeStruct((key_rows, width), BF16),
        ],
        compiler_params=pltpu.CompilerParams(vmem_limit_bytes=48 << 20),
        cost_estimate=pl.CostEstimate(flops=4 * flops, bytes_accessed=12 << 20, transcendentals=rows * span * HEADS),
    )(numbers, qid, kid, queries, keys, values, grad, out, lse)


def factors(count):
    return {32: (4, 2, 2, 2), 128: (4, 4, 4, 2)}.get(count, (count,))


def coordinates(count):
    sizes = factors(count)
    left = lax.axis_index(AXIS)
    places = []
    for size in reversed(sizes):
        places.insert(0, lax.rem(left, size))
        left = lax.div(left, size)
    return places


def peers_along(count, axis, step):
    sizes = factors(count)
    stride = 1
    for size in sizes[axis + 1 :]:
        stride *= size
    size = sizes[axis]
    pairs = []
    for device in range(count):
        place = (device // stride) % size
        pairs.append((device, device + ((place + step) % size - place) * stride))
    return pairs


def take(value, place, axis):
    return lax.dynamic_slice_in_dim(value, place, 1, axis)


def total(terms):
    summed = terms[0].astype(F32)
    for term in terms[1:]:
        summed = summed + term.astype(F32)
    return summed


def reduce_scatter(value, order, kind, count):
    sizes = factors(count)
    places = coordinates(count)
    rows, width = value.shape
    terms = [value.reshape(*sizes, rows // count, width)]
    for axis in order:
        size = sizes[axis]
        arrived = []
        for step in range(1, size):
            other = lax.rem(places[axis] + step, size)
            sent = total([take(term, other, axis) for term in terms]).astype(kind)
            arrived.append(lax.ppermute(sent, AXIS, peers_along(count, axis, step)))
        terms = [take(term, places[axis], axis) for term in terms] + arrived
    return total(terms).reshape(rows // count, width)


def all_gather(value, order, count):
    sizes = factors(count)
    places = coordinates(count)
    rows, width = value.shape
    held = value.reshape(*([1] * len(sizes)), rows, width)
    for axis in order:
        size = sizes[axis]
        shape = list(held.shape)
        shape[axis] = size
        gathered = lax.dynamic_update_slice_in_dim(jnp.zeros(shape, held.dtype), held, places[axis], axis)
        for step in range(1, size):
            arrived = lax.ppermute(held, AXIS, peers_along(count, axis, step))
            source = lax.rem(places[axis] + size - step, size)
            gathered = lax.dynamic_update_slice_in_dim(gathered, arrived, source, axis)
        held = gathered
    return held.reshape(rows * count, width)


MESH = pl.DeviceIdType.MESH
BLOCK = 32
WIDE = 1024


def places32():
    me = lax.axis_index(AXIS)
    core = lax.rem(me, 2)
    x = lax.rem(lax.div(me, 2), 2)
    y = lax.rem(lax.div(me, 4), 2)
    z = lax.div(me, 8)
    return me, core, x, y, z


GELU_A = 0.7978845608028654
GELU_B = 0.044715


def gelu_and_slope(value):
    square = value * value
    bend = jnp.tanh(GELU_A * (value + GELU_B * value * square))
    gate = 0.5 * (1.0 + bend)
    slope = gate + value * 0.5 * (1.0 - bend * bend) * (GELU_A * (1.0 + 3.0 * GELU_B * square))
    return value * gate, slope


def normalise_rows(value):
    mean = jnp.mean(value, axis=-1, keepdims=True)
    centred = value - mean
    scale = lax.rsqrt(jnp.mean(centred * centred, axis=-1, keepdims=True) + EPS)
    return centred * scale, scale


class Far(NamedTuple):
    low_three: Any
    out_grad: Any
    after_two: Any
    up_weight: Any
    down_weight: Any
    cross_att: Any
    cross_q: Any
    text_keys: Any
    text_values: Any
    low_two: Any
    after_one: Any
    captions: Any
    cross_output: Any
    cross_key: Any
    cross_value: Any
    cross_query: Any
    output_weight: Any
    queries: Any
    near_keys: Any
    near_values: Any
    self_att: Any
    near_low: Any
    near_tokens: Any
    query_weight: Any
    key_weight: Any
    value_weight: Any


class Near(NamedTuple):
    starts: Any
    self_lse: Any
    query_code: Any
    key_code: Any
    cross_lse: Any
    gains: Any


class Sums(NamedTuple):
    up: Any
    down: Any
    cross_output: Any
    cross_key: Any
    cross_value: Any
    caption: Any
    cross_query: Any
    output: Any
    query: Any
    key: Any
    value: Any


class Scratch(NamedTuple):
    arena: Any
    sums: Any
    accum_k: Any
    accum_v: Any
    back_one: Any
    back_two: Any
    vec: Any
    vec_in: Any
    tiles: Any
    r0: Any
    r1: Any
    r2: Any
    r3: Any
    load: Any
    s0: Any
    d0: Any
    s1: Any
    d1: Any
    s2: Any
    d2: Any
    s3: Any
    d3: Any
    vs: Any
    vd: Any
    bs: Any
    bd: Any
    credit: Any


UP, DOWN, CROSS_OUTPUT, CROSS_KEY, CROSS_VALUE, CAPTION, CROSS_QUERY, OUTPUT, QUERY, KEY, VALUE = range(11)
PIECES = (
    (UP, 0), (UP, 1), (UP, 2), (UP, 3), (DOWN, 0), (DOWN, 1), (DOWN, 2), (DOWN, 3),
    (CROSS_OUTPUT, 0), (CROSS_KEY, 0), (CROSS_VALUE, 0), (CAPTION, 0), (CROSS_QUERY, 0), (OUTPUT, 0),
    (QUERY, 0), (KEY, 0), (VALUE, 0),
)
PLAN = (
    (), (), (), (), ((2, 0),), (), ((2, 1),), ((2, 2),), (), ((2, 3),), (), (), (), ((3, 0), (2, 4)), (), (), (),
    (), ((3, 1),), (), (), (), ((2, 5),), (), (), (), (), ((3, 2), (2, 6)), (), (), (), ((3, 3),), (), ((2, 7),),
    (), (), ((3, 4), (2, 8)), ((3, 6), (3, 5)), ((1, 13),), ((3, 7),), (), ((2, 9),), (), (), ((2, 10),), (), (),
    ((2, 11),), (), ((3, 8), (2, 12)), (), (), ((3, 9),), (), ((2, 13), (3, 11)), ((3, 10),), ((3, 12),), (),
    ((2, 14),), ((3, 13),),
)
LANDINGS = 9
SLOTS = 2
HALF = LANES // 2
STEP = 64
LOADS = 48


def layer_kernel(rows, *refs):
    total = len(PIECES)
    n_far, n_near, n_sums = len(Far._fields), len(Near._fields), len(Sums._fields)
    far = Far(*refs[:n_far])
    near = Near(*refs[n_far : n_far + n_near])
    refs = refs[n_far + n_near :]
    outs = Sums(*refs[:n_sums])
    vec_out, block_output, input_grad = refs[n_sums : n_sums + 3]
    held = Scratch(*refs[n_sums + 3 :])
    (arena, sums, accum_k, accum_v, back_one, back_two, vec, vec_in, tiles, r0, r1, r2, r3,
     load, s0, d0, s1, d1, s2, d2, s3, d3, vs, vd, bs, bd, credit) = held

    me, core, x, y, z = places32()
    sibling = me + 1 - 2 * core
    x_peer = me + 2 - 4 * x
    y_peer = me + 4 - 8 * y
    z_other = [lax.rem(z + m, 4) for m in range(1, 4)]
    z_peers = [me + 8 * (o - z) for o in z_other]
    has_before = me >= 2
    has_after = me < 30

    barrier = pltpu.get_barrier_semaphore()
    for peer in (sibling, x_peer, y_peer, *z_peers):
        pl.semaphore_signal(barrier, inc=1, device_id=(peer,), device_id_type=MESH)

    @pl.when(has_before)
    def _():
        pl.semaphore_signal(barrier, inc=1, device_id=(me - 2,), device_id_type=MESH)

    @pl.when(has_after)
    def _():
        pl.semaphore_signal(barrier, inc=1, device_id=(me + 2,), device_id_type=MESH)

    numbers = iter(range(LOADS))

    def fetch(source, slot):
        return start_copy(source, arena.at[pl.ds(slot * rows, source.shape[0])])

    def start_copy(source, target):
        copy = pltpu.make_async_copy(source, target, load.at[next(numbers)])
        copy.start()
        return copy

    def at(slot, count=1):
        return pl.ds(slot * rows, count * rows)

    def up_part(part):
        return far.up_weight.at[:, pl.ds(part * WIDE, WIDE)]

    def down_part(part):
        return far.down_weight.at[pl.ds(part * WIDE, WIDE)]

    ONE, TWO, THREE = 12, 14, 10
    low_three_load = fetch(far.low_three, 8)
    up_loads = [fetch(up_part(0), THREE)]
    out_grad_load = fetch(far.out_grad, 9)
    down_loads = [fetch(down_part(0), ONE)]
    up_loads.append(fetch(up_part(1), TWO))
    after_load = start_copy(far.after_two, sums.at[2])

    pl.semaphore_wait(barrier, 6 + jnp.where(has_before, 1, 0) + jnp.where(has_after, 1, 0))

    def remote(src, dst, send, recv, peer):
        return pltpu.make_async_remote_copy(
            src_ref=src, dst_ref=dst, send_sem=send, recv_sem=recv, device_id=(peer,), device_id_type=MESH
        )

    def along(c):
        even = lax.rem(c, 2) == 0
        return (
            jnp.where(even, x, y),
            jnp.where(even, x_peer, y_peer),
            jnp.where(even, y, x),
            jnp.where(even, y_peer, x_peer),
        )

    def add_blocks(count, dst, src):
        @pl.loop(0, count, unroll=4)
        def _(i):
            dst(i)[...] = dst(i)[...] + src(i)[...]

    def take_credit(c):
        if c >= LANDINGS:
            pl.semaphore_wait(credit, 1)

    def give(c):
        take_credit(c)
        remote(tiles.at[c % SLOTS, 1 - core], r0.at[c % LANDINGS], s0.at[c], d0.at[c], sibling).start()

    def make(c, left_at, right_at, depth):
        @pl.loop(0, 4)
        def _(zz):
            left = arena[pl.ds(left_at * rows, depth), pl.ds(pl.multiple_of(zz * TILE, TILE), TILE)]
            for part in range(2):
                cols = slice(part * (WIDE // 2), (part + 1) * (WIDE // 2))
                result = lax.dot_general(
                    left, arena[pl.ds(right_at * rows, depth), cols], TN, preferred_element_type=F32
                ).astype(BF16)
                for block in range(8):
                    yy, xx, cc = block // 4, (block // 2) % 2, block % 2
                    f, s = (xx, yy) if c % 2 == 0 else (yy, xx)
                    tiles[c % SLOTS, cc, f, s, zz, :, cols] = result[block * BLOCK : (block + 1) * BLOCK]

        give(c)

    def make_down(c, part):
        @pl.loop(0, 4)
        def _(zz):
            for quarter in range(4):
                yy, xx = quarter // 2, quarter % 2
                f, s = (xx, yy) if c % 2 == 0 else (yy, xx)
                left = arena[
                    pl.ds(pl.multiple_of(zz * rows, rows), rows), quarter * TILE : (quarter + 1) * TILE
                ]
                result = lax.dot_general(
                    left, arena[at(9), part * TILE : (part + 1) * TILE], TN, preferred_element_type=F32
                ).astype(BF16)
                for cc in range(2):
                    for group in range(4):
                        top = cc * 128 + group * BLOCK
                        tiles[c % SLOTS, cc, f, s, zz, :, group * TILE : (group + 1) * TILE] = result[top : top + BLOCK]

        give(c)

    def first(c):
        f, fp, _, _ = along(c)
        slot, place = c % SLOTS, c % LANDINGS
        copy = remote(tiles.at[slot, 1 - core], r0.at[place], s0.at[c], d0.at[c], sibling)
        copy.wait_recv()
        add_blocks(
            16,
            lambda i: r0.at[place, i // 8, (i // 4) % 2, i % 4],
            lambda i: tiles.at[slot, core, i // 8, (i // 4) % 2, i % 4],
        )
        remote(r0.at[place, 1 - f], r1.at[c], s1.at[c], d1.at[c], fp).start()
        copy.wait_send()

    def second(c):
        f, fp, s, sp = along(c)
        place = c % LANDINGS
        copy = remote(r0.at[place, 1 - f], r1.at[c], s1.at[c], d1.at[c], fp)
        copy.wait_recv()
        add_blocks(8, lambda i: r1.at[c, i // 4, i % 4], lambda i: r0.at[place, f, i // 4, i % 4])
        remote(r1.at[c, 1 - s], r2.at[c], s2.at[c], d2.at[c], sp).start()
        copy.wait_send()
        if c < total - LANDINGS:
            pl.semaphore_signal(credit, inc=1, device_id=(sibling,), device_id_type=MESH)

    def third(c):
        _, _, s, sp = along(c)
        copy = remote(r1.at[c, 1 - s], r2.at[c], s2.at[c], d2.at[c], sp)
        copy.wait_recv()
        add_blocks(4, lambda i: r2.at[c, i], lambda i: r1.at[c, s, i])
        for m in range(3):
            remote(r2.at[c, z_other[m]], r3.at[c, m], s3.at[c, m], d3.at[c, m], z_peers[m]).start()
        copy.wait_send()

    def last(c):
        number, part = PIECES[c]
        for m in range(3):
            remote(r2.at[c, z_other[m]], r3.at[c, m], s3.at[c, m], d3.at[c, m], z_peers[m]).wait()
        summed = r2[c, z].astype(F32) + r3[c, 0].astype(F32) + r3[c, 1].astype(F32) + r3[c, 2].astype(F32)
        out = outs[number]
        if number == DOWN:
            for group in range(4):
                out[group * BLOCK : (group + 1) * BLOCK, part * TILE : (part + 1) * TILE] = summed[
                    :, group * TILE : (group + 1) * TILE
                ]
        else:
            out[:, part * WIDE : (part + 1) * WIDE] = summed[: out.shape[0]]

    def each_tile(run):
        @pl.loop(0, WIDE // TILE, unroll=2)
        def _(n):
            run(pl.multiple_of(n * TILE, TILE))

    def product(pairs, add=False):
        def run(n):
            result = None
            for slot, weight in pairs:
                term = lax.dot_general(
                    arena[at(slot), :], arena[pl.ds(weight * rows + n, TILE), :], NT, preferred_element_type=F32
                )
                result = term if result is None else result + term
            if add:
                result += sums[0, :, pl.ds(n, TILE)]
            sums[0, :, pl.ds(n, TILE)] = result

        each_tile(run)

    def plain_product(slot, weight, add):
        def run(n):
            result = jnp.dot(arena[at(slot), :], arena[at(weight, 2), pl.ds(n, TILE)], preferred_element_type=F32)
            if add:
                result += sums[0, :, pl.ds(n, TILE)]
            sums[0, :, pl.ds(n, TILE)] = result

        each_tile(run)

    def low_product(slot, weight, target):
        def run(n):
            result = lax.dot_general(
                arena[at(slot), :], arena[pl.ds(weight * rows + n, TILE), :], NT, preferred_element_type=F32
            )
            arena[at(target), pl.ds(n, TILE)] = result.astype(BF16)

        each_tile(run)

    def each_step(run):
        @pl.loop(0, rows // STEP)
        def _(i):
            run(pl.multiple_of(i * STEP, STEP))

    vec[...] = jnp.zeros_like(vec)

    def add_gains(row, grad, unit):
        vec[row : row + 1] += jnp.sum(grad * unit, axis=0, keepdims=True)
        vec[row + 1 : row + 2] += jnp.sum(grad, axis=0, keepdims=True)

    def norm_back_rows(grad, unit, scale, gain):
        scaled = grad * gain
        return scale * (
            scaled - jnp.mean(scaled, axis=-1, keepdims=True) - unit * jnp.mean(scaled * unit, axis=-1, keepdims=True)
        )

    def attend_step(keys, values, query, grad, out, lse, allowed):
        query = query * jnp.asarray(0.125, BF16)
        inner = jnp.transpose(grad.astype(F32) * out.astype(F32))
        turned_keys = jnp.transpose(keys)
        parts = []
        dk = None
        dv = None
        for half in range(2):
            head_q = head_lanes(query, half)
            head_g = head_lanes(grad, half)
            delta = jnp.sum(inner[half * HALF : (half + 1) * HALF], axis=0, keepdims=True)
            scores = lax.dot_general(keys, head_q, NT, preferred_element_type=F32)
            probs = jnp.exp(jnp.where(allowed, scores - lse[half], NEG))
            grad_probs = lax.dot_general(values, head_g, NT, preferred_element_type=F32)
            grad_scores = (probs * (grad_probs - delta)).astype(BF16)
            part_k = jnp.dot(grad_scores, head_q, preferred_element_type=F32)
            part_v = jnp.dot(probs.astype(BF16), head_g, preferred_element_type=F32)
            dk = part_k if dk is None else dk + part_k
            dv = part_v if dv is None else dv + part_v
            parts.append(jnp.dot(turned_keys, grad_scores, preferred_element_type=F32))
        dq = jnp.concatenate([parts[0][:HALF], parts[1][HALF:]], 0)
        return (jnp.transpose(dq) * 0.125).astype(BF16), dk, dv

    position = [0]

    def take_steps(steps):
        for kind, c in steps:
            (first, second, third)[kind - 1](c)

    def tick():
        take_steps(PLAN[position[0]])
        position[0] += 1

    def loop_tick(base, i):
        for number, steps in enumerate(PLAN[base : base + 16]):
            if steps:
                pl.when(i == number)(functools.partial(take_steps, steps))

    def activate(part, up_at, down_at):
        def run(n):
            cols = pl.ds(n, TILE)
            pre = jnp.dot(arena[at(8), :], arena[at(up_at, 2), cols], preferred_element_type=F32)
            grad = lax.dot_general(
                arena[at(9), :], arena[pl.ds(down_at * rows + n, TILE), :], NT, preferred_element_type=F32
            )
            hidden, slope = gelu_and_slope(pre)
            arena[at(part), cols] = hidden.astype(BF16)
            arena[at(4 + part), cols] = (slope * grad).astype(BF16)

        each_tile(run)

    low_three_load.wait()
    out_grad_load.wait()
    places = ((THREE, ONE), (TWO, THREE), (ONE, TWO), (THREE, ONE))
    for part in range(4):
        up_loads[part].wait()
        down_loads[part].wait()
        activate(part, *places[part])
        if part == 0:
            down_loads.append(fetch(down_part(1), THREE))
            up_loads.append(fetch(up_part(2), ONE))
        if part == 1:
            down_loads.append(fetch(down_part(2), TWO))
            up_loads.append(fetch(up_part(3), THREE))
        if part == 2:
            down_loads.append(fetch(down_part(3), ONE))
            weight_two = fetch(up_part(1), TWO)
        if part == 3:
            weight_one = fetch(up_part(0), ONE)
        make(part, 8, 4 + part, rows)
        if part > 0:
            first(part - 1)
        tick()
    places = (ONE, TWO, THREE, ONE)
    loads = [weight_one, weight_two, fetch(up_part(2), THREE)]
    for part in range(4):
        make_down(4 + part, part)
        loads[part].wait()
        product([(4 + part, places[part])], add=part > 0)
        if part == 0:
            loads.append(fetch(up_part(3), ONE))
        first(3 + part)
        tick()
    weight_two = fetch(far.cross_output, TWO)
    weight_three = fetch(down_part(0), THREE)
    weight_one = fetch(down_part(1), ONE)
    low_two_load = fetch(far.low_two, 4)
    captions_load = fetch(far.captions, 5)
    cross_att_load = fetch(far.cross_att, 6)
    cross_q_load = fetch(far.cross_q, 7)
    after_load.wait()
    gains = near.gains

    def norm_three(n):
        here = pl.ds(n, STEP)
        unit, scale = normalise_rows(sums[2, here, :])
        grad = sums[0, here, :]
        add_gains(4, grad, unit)
        value = arena[pl.ds(9 * rows + n, STEP), :].astype(F32) + norm_back_rows(grad, unit, scale, gains[2:3])
        sums[1, here, :] = value
        arena[pl.ds(9 * rows + n, STEP), :] = value.astype(BF16)

    each_step(norm_three)
    first(7)
    tick()

    weight_two.wait()
    low_product(9, TWO, 8)
    weight_two = fetch(down_part(2), TWO)
    cross_att_load.wait()
    make(8, 6, 9, rows)
    tick()
    weight_three.wait()
    plain_product(0, THREE, False)
    weight_three = fetch(down_part(3), THREE)
    tick()
    weight_one.wait()
    plain_product(1, ONE, True)
    weight_one = fetch(far.cross_key, ONE)
    first(8)
    tick()
    weight_two.wait()
    plain_product(2, TWO, True)
    weight_two = fetch(far.cross_value, TWO)
    keys_load = fetch(far.text_keys, 2)
    tick()
    weight_three.wait()
    plain_product(3, THREE, True)
    weight_three = fetch(far.cross_query, THREE)
    values_load = fetch(far.text_values, 3)
    tick()

    def finish_block(n):
        here = pl.ds(n, STEP)
        arena[pl.ds(n, STEP), :] = (sums[2, here, :] + sums[0, here, :]).astype(BF16)

    each_step(finish_block)
    tick()
    loop_base = position[0]
    position[0] += 16
    block_copy = start_copy(arena.at[at(0)], block_output)
    after_load = start_copy(far.after_one, sums.at[2])

    text = far.text_keys.shape[0]
    cross_q_load.wait()
    keys_load.wait()
    values_load.wait()

    @pl.loop(0, 16)
    def _(i):
        h, t = lax.div(i, 2), lax.rem(i, 2)
        lanes = pl.ds(pl.multiple_of(h * LANES, LANES), LANES)
        own = pl.multiple_of(t * TILE, TILE)
        mine = pl.ds(7 * rows + own, TILE)
        allowed = near.key_code[...] == near.query_code[:, pl.ds(own, TILE)]
        lse = [near.cross_lse[h, half : half + 1, pl.ds(own, TILE)] for half in range(2)]
        dq, dk, dv = attend_step(
            arena[at(2), lanes], arena[at(3), lanes], arena[mine, lanes],
            arena[pl.ds(8 * rows + own, TILE), lanes], arena[pl.ds(6 * rows + own, TILE), lanes], lse, allowed,
        )
        arena[mine, lanes] = dq

        @pl.when(t == 0)
        def _():
            accum_k[:text] = dk
            accum_v[:text] = dv

        @pl.when(t == 1)
        def _():
            arena[at(2), lanes] = (accum_k[:text] + dk).astype(BF16)
            arena[at(3), lanes] = (accum_v[:text] + dv).astype(BF16)

        loop_tick(loop_base, i)

    block_copy.wait()
    self_att_load = fetch(far.self_att, 8)
    captions_load.wait()
    make(9, 5, 2, rows)
    tick()
    weight_one.wait()
    weight_two.wait()
    product([(2, ONE), (3, TWO)])
    weight_one = fetch(far.output_weight, ONE)
    make(10, 5, 3, rows)
    first(9)
    tick()

    c = 11
    for zz in range(4):
        for block in range(8):
            yy, xx, cc = block // 4, (block // 2) % 2, block % 2
            f, s = (xx, yy) if c % 2 == 0 else (yy, xx)
            top = (zz * 8 + block) * 16
            tiles[c % SLOTS, cc, f, s, zz, :16, :] = sums[0, top : top + 16, :].astype(BF16)
            tiles[c % SLOTS, cc, f, s, zz, 16:, :] = jnp.zeros((16, WIDE), BF16)
    give(c)
    tick()
    keys_load = fetch(far.near_keys, 1)
    weight_three.wait()
    product([(7, THREE)])
    near_low_load = fetch(far.near_low, 9)
    first(10)
    tick()
    low_two_load.wait()
    make(12, 4, 7, rows)
    values_load = fetch(far.near_values, 4)
    queries_load = fetch(far.queries, 0)
    first(11)
    tick()
    after_load.wait()

    def norm_two(n):
        here = pl.ds(n, STEP)
        unit, scale = normalise_rows(sums[2, here, :])
        grad = sums[0, here, :]
        add_gains(2, grad, unit)
        value = sums[1, here, :] + norm_back_rows(grad, unit, scale, gains[1:2])
        sums[1, here, :] = value
        arena[pl.ds(14 * rows + n, STEP), :] = value.astype(BF16)

    each_step(norm_two)
    first(12)
    tick()

    weight_one.wait()
    low_product(14, ONE, 7)
    weight_one = fetch(far.value_weight, ONE)
    self_att_load.wait()
    make(13, 8, 14, rows)
    tick()
    loop_base = position[0]
    position[0] += 16
    weight_two = fetch(far.key_weight, TWO)
    queries_load.wait()
    keys_load.wait()
    values_load.wait()

    span = 2 * rows + TILE

    @pl.loop(0, 16)
    def _(i):
        h, t = lax.div(i, 2), lax.rem(i, 2)
        lanes = pl.ds(pl.multiple_of(h * LANES, LANES), LANES)
        own = pl.multiple_of(t * TILE, TILE)
        mine = pl.ds(own, TILE)
        kpos = lax.broadcasted_iota(jnp.int32, (span, TILE), 0)
        qpos = lax.broadcasted_iota(jnp.int32, (TILE, TILE), 1)
        dpos = lax.broadcasted_iota(jnp.int32, (TILE, TILE), 0)
        allowed = kpos >= near.starts[:, mine] - own
        allowed = jnp.concatenate([allowed[: span - TILE], allowed[span - TILE :] & (dpos <= qpos)], 0)
        lse = [near.self_lse[h, half : half + 1, mine] for half in range(2)]
        dq, dk, dv = attend_step(
            arena[pl.ds(rows + own, span), lanes], arena[pl.ds(4 * rows + own, span), lanes], arena[mine, lanes],
            arena[pl.ds(7 * rows + own, TILE), lanes], arena[pl.ds(8 * rows + own, TILE), lanes], lse, allowed,
        )
        arena[mine, lanes] = dq

        @pl.when(t == 0)
        def _():
            accum_k[:span] = dk
            accum_v[:span] = dv

        @pl.when(t == 1)
        def _():
            for target, accum, part in ((1, accum_k, dk), (4, accum_v, dv)):
                arena[pl.ds(target * rows, TILE), lanes] = accum[:TILE].astype(BF16)
                arena[pl.ds(target * rows + TILE, span - TILE), lanes] = (accum[TILE:span] + part[: span - TILE]).astype(BF16)
                arena[pl.ds(target * rows + span, TILE), lanes] = part[span - TILE :].astype(BF16)

        loop_tick(loop_base, i)

    near_low_load.wait()
    make(14, 11, 0, rows)
    weight_two.wait()
    weight_one.wait()
    product([(2, TWO), (5, ONE)])

    def as_low(slot, extra):
        def run(n):
            value = sums[0, pl.ds(n, STEP), :]
            if extra is not None:
                value = value + jnp.where(core == 1, extra[pl.ds(n, STEP), :].astype(F32), 0.0)
            arena[pl.ds(slot * rows + n, STEP), :] = value.astype(BF16)

        each_step(run)

    as_low(7, None)
    swap = remote(arena.at[at(7)], back_one, bs.at[0], bd.at[0], sibling)
    swap.start()
    first(14)
    tick()
    product([(1, TWO), (4, ONE)])
    swap.wait()
    as_low(8, back_one)
    send_back = remote(arena.at[at(8)], back_two, bs.at[1], bd.at[1], me - 2)

    @pl.when(has_before)
    def _():
        send_back.start()

    tick()
    make(15, 9, 1, 3 * rows)
    tick()
    query_weight_load = fetch(far.query_weight, 1)
    make(16, 9, 4, 3 * rows)
    token_load = fetch(far.near_tokens, 9)
    first(15)
    tick()

    def block_gains(slot, grad_slot, factor):
        def run(n):
            unit, _ = normalise_rows(arena[pl.ds(slot * rows + n, STEP), :].astype(F32))
            if grad_slot is None:
                grad = sums[0, pl.ds(n, STEP), :]
            else:
                grad = arena[pl.ds(grad_slot * rows + n, STEP), :].astype(F32)
            if factor is not None:
                grad = grad * factor
            add_gains(0, grad, unit)

        each_step(run)

    token_load.wait()
    block_gains(9, 8, None)
    block_gains(10, 7, jnp.where(core == 1, 1.0, 0.0))
    first(16)
    tick()
    query_weight_load.wait()
    product([(0, 1), (3, TWO), (6, ONE)])
    tick()
    block_gains(11, None, None)

    def vec_step(number, peer):
        step = remote(vec, vec_in.at[number], vs.at[number], vd.at[number], peer)
        step.start()
        return step

    def norm_one(n):
        here = pl.ds(n, STEP)
        unit, scale = normalise_rows(arena[pl.ds(11 * rows + n, STEP), :].astype(F32))
        grad = sums[0, here, :]
        grad = grad + jnp.where(core == 0, back_one[here, :].astype(F32), 0.0)
        grad = grad + jnp.where(has_after, back_two[here, :].astype(F32), 0.0)
        sums[1, here, :] += norm_back_rows(grad, unit, scale, gains[0:1])

    step = vec_step(0, sibling)
    step.wait()
    vec[...] += vec_in[0]
    step = vec_step(1, x_peer)
    second(15)

    @pl.when(has_before)
    def _():
        send_back.wait_send()

    @pl.when(has_after)
    def _():
        send_back.wait_recv()

    each_step(norm_one)
    out_copy = start_copy(sums.at[1], input_grad)
    step.wait()
    vec[...] += vec_in[1]
    step = vec_step(2, y_peer)
    third(14)
    second(16)
    step.wait()
    vec[...] += vec_in[2]
    steps = [vec_step(3 + m, z_peers[m]) for m in range(3)]
    for c in range(total - 3):
        last(c)
    third(15)
    third(16)
    for step in steps:
        step.wait()
    vec_out[...] = vec[...] + vec_in[3] + vec_in[4] + vec_in[5]
    for c in range(total - 3, total):
        last(c)
    out_copy.wait()


def layer_tail(far, near):
    rows, width = far.queries.shape
    count = 32
    sizes = {UP: (BLOCK, 4 * WIDE), DOWN: (4 * BLOCK, WIDE), CAPTION: (far.captions.shape[0] // count, WIDE)}
    total = len(PIECES)
    local = pl.BlockSpec(memory_space=pltpu.VMEM)
    anywhere = pl.BlockSpec(memory_space=pl.ANY)
    dma = pltpu.SemaphoreType.DMA
    scratch = Scratch(
        arena=pltpu.VMEM((16 * rows, width), BF16),
        sums=pltpu.VMEM((3, rows, width), F32),
        accum_k=pltpu.VMEM((3 * rows, LANES), F32),
        accum_v=pltpu.VMEM((3 * rows, LANES), F32),
        back_one=pltpu.VMEM((rows, width), BF16),
        back_two=pltpu.VMEM((rows, width), BF16),
        vec=pltpu.VMEM((8, width), F32),
        vec_in=pltpu.VMEM((6, 8, width), F32),
        tiles=pltpu.VMEM((SLOTS, 2, 2, 2, 4, BLOCK, WIDE), BF16),
        r0=pltpu.VMEM((LANDINGS, 2, 2, 4, BLOCK, WIDE), BF16),
        r1=pltpu.VMEM((total, 2, 4, BLOCK, WIDE), BF16),
        r2=pltpu.VMEM((total, 4, BLOCK, WIDE), BF16),
        r3=pltpu.VMEM((total, 3, BLOCK, WIDE), BF16),
        load=dma((LOADS,)), s0=dma((total,)), d0=dma((total,)), s1=dma((total,)), d1=dma((total,)),
        s2=dma((total,)), d2=dma((total,)), s3=dma((total, 3)), d3=dma((total, 3)), vs=dma((6,)), vd=dma((6,)),
        bs=dma((2,)), bd=dma((2,)), credit=pltpu.SemaphoreType.REGULAR,
    )
    results = pl.pallas_call(
        functools.partial(layer_kernel, rows),
        in_specs=[anywhere] * len(far) + [local] * len(near),
        out_specs=[local] * (len(Sums._fields) + 1) + [anywhere] * 2,
        out_shape=[jax.ShapeDtypeStruct(sizes.get(number, (BLOCK, WIDE)), F32) for number in range(len(Sums._fields))]
        + [
            jax.ShapeDtypeStruct((8, width), F32),
            jax.ShapeDtypeStruct((rows, width), BF16),
            jax.ShapeDtypeStruct((rows, width), F32),
        ],
        scratch_shapes=list(scratch),
        compiler_params=pltpu.CompilerParams(collective_id=0, has_side_effects=True, vmem_limit_bytes=63 << 20),
        cost_estimate=pl.CostEstimate(flops=1 << 34, bytes_accessed=64 << 20, transcendentals=0),
    )(*far, *near)
    return Sums(*results[: len(Sums._fields)]), *results[len(Sums._fields) :]


def matmul(left, right):
    return jnp.dot(left, right, preferred_element_type=F32)


def left_product(left, right):
    return lax.dot_general(left, right, TN, preferred_element_type=F32)


def right_product(left, right):
    return lax.dot_general(left, right, NT, preferred_element_type=F32)


def normalise(value):
    mean = jnp.mean(value, axis=-1, keepdims=True)
    centred = value - mean
    scale = lax.rsqrt(jnp.mean(centred * centred, axis=-1, keepdims=True) + EPS)
    return centred * scale, scale


def norm_back(grad, unit, scale, gain):
    scaled = grad * gain
    return scale * (
        scaled
        - jnp.mean(scaled, axis=-1, keepdims=True)
        - unit * jnp.mean(scaled * unit, axis=-1, keepdims=True)
    )


def body(
    tokens, out_grad, caption_states,
    query_weight, key_weight, value_weight, output_weight,
    cross_query, cross_key, cross_value, cross_output,
    up_weight, down_weight,
    attn_gain, attn_bias, cross_gain, cross_bias, mlp_gain, mlp_bias,
    item_ids, caption_segments, item_rows, item_segments,
):
    device = lax.axis_index(AXIS)
    count = lax.axis_size(AXIS)
    rows = tokens.shape[0]
    tiles = rows // TILE
    odd = lax.rem(device, 2) == 1
    swap = [(i, i ^ 1) for i in range(count)]
    ahead = [(i, i + 2) for i in range(count - 2)]
    behind = [(i + 2, i) for i in range(count - 2)]

    block_two = lax.ppermute(tokens, AXIS, ahead)
    block_one = lax.ppermute(jnp.where(odd, block_two, tokens), AXIS, swap)
    near_tokens = jnp.concatenate([block_two, block_one, tokens], 0)

    all_ids = jnp.concatenate([jnp.full((REACH * rows,), -1, jnp.int32), item_ids])
    near_ids = lax.dynamic_slice_in_dim(all_ids, device * rows, (REACH + 1) * rows)
    own_ids = near_ids[REACH * rows :]
    near_rows = (REACH + 1) * rows
    span = REACH * rows + TILE
    windows = jnp.stack([near_ids[t * TILE : t * TILE + span] for t in range(tiles)])
    firsts = own_ids[::TILE]
    before = jnp.sum((near_ids[None, :] < firsts[:, None]).astype(jnp.int32), axis=1)
    lasts = REACH * rows + TILE * (1 + jnp.arange(tiles, dtype=jnp.int32))
    numbers = lasts // TILE - before // TILE
    numbers = jnp.clip(numbers, 1, span // TILE)
    self_sizes = tuple(TILE * (i + 1) for i in range(span // TILE))
    self_ends = (REACH * rows + TILE, TILE)

    text = caption_states.shape[0]
    caption_len = caption_segments.shape[1]
    member = own_ids[:, None] == jnp.arange(item_rows.shape[0], dtype=jnp.int32)[None, :]
    codes = item_rows * caption_len + item_segments
    query_code = jnp.sum(jnp.where(member, codes[None, :], 0), axis=1)
    key_code = (jnp.arange(text, dtype=jnp.int32) // caption_len) * caption_len + caption_segments.reshape(-1)
    text_code = jnp.broadcast_to(key_code[None], (tiles, text))
    no_numbers = jnp.zeros((tiles,), jnp.int32)
    text_ends = (text, 0)

    inputs = tokens.astype(F32)
    near_unit, near_scale = normalise(near_tokens.astype(F32))
    near_low = (near_unit * attn_gain + attn_bias).astype(BF16)
    low_one = near_low[REACH * rows :]
    queries = matmul(low_one, query_weight).astype(BF16)
    near_keys = matmul(near_low, key_weight).astype(BF16)
    near_values = matmul(near_low, value_weight).astype(BF16)
    self_att, self_lse = attend_forward(
        queries, near_keys, near_values, own_ids[:, None], windows[:, None, :], numbers, True, self_sizes, self_ends
    )
    after_one = inputs + matmul(self_att, output_weight)
    unit_two, scale_two = normalise(after_one)
    low_two = (unit_two * cross_gain + cross_bias).astype(BF16)
    cross_q = matmul(low_two, cross_query).astype(BF16)
    text_keys = matmul(caption_states, cross_key).astype(BF16)
    text_values = matmul(caption_states, cross_value).astype(BF16)
    cross_att, cross_lse = attend_forward(
        cross_q, text_keys, text_values, query_code[:, None], text_code[:, None, :], no_numbers, False, (text,), text_ends
    )
    after_two = after_one + matmul(cross_att, cross_output)
    unit_three, scale_three = normalise(after_two)
    low_three = (unit_three * mlp_gain + mlp_bias).astype(BF16)
    width = tokens.shape[1]
    if count == 32:
        starts = jnp.sum((near_ids[None, :] < own_ids[:, None]).astype(jnp.int32), axis=1)
        sums, small, block_output, input_grad = layer_tail(
            Far(
                low_three=low_three, out_grad=out_grad, after_two=after_two,
                up_weight=up_weight, down_weight=down_weight,
                cross_att=cross_att, cross_q=cross_q, text_keys=text_keys, text_values=text_values,
                low_two=low_two, after_one=after_one, captions=caption_states,
                cross_output=cross_output, cross_key=cross_key, cross_value=cross_value, cross_query=cross_query,
                output_weight=output_weight,
                queries=queries, near_keys=near_keys, near_values=near_values, self_att=self_att,
                near_low=near_low, near_tokens=near_tokens,
                query_weight=query_weight, key_weight=key_weight, value_weight=value_weight,
            ),
            Near(
                starts=starts[None, :], self_lse=self_lse, query_code=query_code[None, :], key_code=key_code[:, None],
                cross_lse=cross_lse, gains=jnp.stack([attn_gain, cross_gain, mlp_gain]),
            ),
        )
        small = lax.dynamic_slice_in_dim(small, device * (width // count), width // count, 1)
    else:
        hidden_pre = matmul(low_three, up_weight)
        hidden, slope = gelu_and_slope(hidden_pre)
        hidden_low = hidden.astype(BF16)
        grad_pre = (slope * right_product(out_grad, down_weight)).astype(BF16)
        block_output = (after_two + matmul(hidden_low, down_weight)).astype(BF16)

        down_grad = left_product(hidden_low, out_grad).astype(BF16)
        up_grad = left_product(low_three, grad_pre).astype(BF16)
        z_, y_, x_, c_ = 0, 1, 2, 3
        one_way = (c_, x_, y_, z_) if len(factors(count)) == 4 else (0,)
        other_way = (c_, y_, x_, z_) if len(factors(count)) == 4 else (0,)
        grad_three = right_product(grad_pre, up_weight)
        mlp_gain_grad = jnp.sum(grad_three * unit_three, axis=0)
        mlp_bias_grad = jnp.sum(grad_three, axis=0)
        grad_two = out_grad.astype(F32) + norm_back(grad_three, unit_three, scale_three, mlp_gain)
        grad_two_low = grad_two.astype(BF16)

        cross_output_grad = left_product(cross_att, grad_two_low).astype(BF16)
        grad_cross = right_product(grad_two_low, cross_output).astype(BF16)
        grad_cq, grad_tk, grad_tv = attend_backward(
            cross_q, text_keys, text_values, grad_cross, cross_att, cross_lse,
            query_code[None, :], text_code[:, :, None], no_numbers, False, (text,), text_ends,
        )
        width = grad_tk.shape[1]
        cross_key_grad = left_product(caption_states, grad_tk).astype(BF16)
        cross_value_grad = left_product(caption_states, grad_tv).astype(BF16)
        caption_grad = (right_product(grad_tk, cross_key) + right_product(grad_tv, cross_value)).astype(BF16)
        cross_query_grad = left_product(low_two, grad_cq).astype(BF16)
        grad_norm_two = right_product(grad_cq, cross_query)
        cross_gain_grad = jnp.sum(grad_norm_two * unit_two, axis=0)
        cross_bias_grad = jnp.sum(grad_norm_two, axis=0)
        grad_one = grad_two + norm_back(grad_norm_two, unit_two, scale_two, cross_gain)
        grad_one_low = grad_one.astype(BF16)

        output_weight_grad = left_product(self_att, grad_one_low).astype(BF16)
        grad_self = right_product(grad_one_low, output_weight).astype(BF16)
        grad_q, grad_k, grad_v = attend_backward(
            queries, near_keys, near_values, grad_self, self_att, self_lse,
            own_ids[None, :], windows[:, :, None], numbers, True, self_sizes, self_ends,
        )
        grad_near = right_product(grad_k, key_weight) + right_product(grad_v, value_weight)
        grad_own = grad_near[REACH * rows :] + right_product(grad_q, query_weight)
        to_two = grad_near[:rows]
        to_one = grad_near[rows : REACH * rows].astype(BF16)
        from_swap = lax.ppermute(to_one, AXIS, swap).astype(F32)
        to_two = (to_two + jnp.where(odd, from_swap, 0.0)).astype(BF16)
        from_two = lax.ppermute(to_two, AXIS, behind).astype(F32)
        near_sum = jnp.concatenate([grad_near[: REACH * rows], grad_own], 0)
        attn_gain_grad = jnp.sum(near_sum * near_unit, axis=0)
        attn_bias_grad = jnp.sum(near_sum, axis=0)
        grad_norm_one = grad_own + from_two + jnp.where(odd, 0.0, from_swap)
        unit_one = near_unit[REACH * rows :]
        input_grad = grad_one + norm_back(grad_norm_one, unit_one, near_scale[REACH * rows :], attn_gain)
        query_grad = left_product(low_one, grad_q).astype(BF16)
        key_grad = left_product(near_low, grad_k).astype(BF16)
        value_grad = left_product(near_low, grad_v).astype(BF16)
        vectors = jnp.stack(
            [attn_gain_grad, attn_bias_grad, cross_gain_grad, cross_bias_grad, mlp_gain_grad, mlp_bias_grad]
        )
        grads = [
            down_grad, up_grad, cross_output_grad, cross_query_grad, cross_key_grad, cross_value_grad, output_weight_grad,
        ]
        sums = [
            reduce_scatter(grad, one_way if i % 2 else other_way, BF16, count)
            for i, grad in enumerate([*grads, query_grad, key_grad, value_grad, caption_grad])
        ]
        small = reduce_scatter(vectors.T, one_way, F32, count).T
        (down_out, up_out, cross_output_out, cross_query_out, cross_key_out, cross_value_out,
         output_out, query_out, key_out, value_out, caption_out) = sums
        sums = Sums(
            up=up_out, down=down_out, cross_output=cross_output_out, cross_key=cross_key_out,
            cross_value=cross_value_out, caption=caption_out, cross_query=cross_query_out, output=output_out,
            query=query_out, key=key_out, value=value_out,
        )
    return (
        block_output, input_grad, sums.caption,
        sums.query, sums.key, sums.value, sums.output,
        sums.cross_query, sums.cross_key, sums.cross_value, sums.cross_output,
        sums.up, sums.down,
        small[0], small[1], small[2], small[3], small[4], small[5],
    )


def solution(mesh):
    split = P(AXIS, None)
    return jax.shard_map(
        body,
        mesh=mesh,
        in_specs=(split, split) + (P(),) * 21,
        out_specs=(split,) * 13 + (P(AXIS),) * 6,
        check_vma=False,
    )
```

```python
import functools
from typing import Any, NamedTuple

import jax
import jax.numpy as jnp
from jax import lax
from jax.experimental import pallas as pl
from jax.experimental.pallas import tpu as pltpu
from jax.sharding import PartitionSpec as P

HEADS = 16
REACH = 2
EPS = 1e-05
NEG = -1e30
TILE = 256
LANES = 128
AXIS = "seq"
F32 = jnp.float32
BF16 = jnp.bfloat16

NT = (((1,), (1,)), ((), ()))
TN = (((0,), (0,)), ((), ()))


def head_lanes(value, half):
    lane = lax.broadcasted_iota(jnp.int32, value.shape, 1)
    keep = (lane < LANES // 2) if half == 0 else (lane >= LANES // 2)
    return jnp.where(keep, value, jnp.zeros_like(value))


def forward_kernel(causal, sizes, ends, n_ref, qid_ref, kid_ref, q_ref, k_ref, v_ref, o_ref, lse_ref, bias_ref):
    tile = pl.program_id(1)
    span = bias_ref.shape[2]

    @pl.when(pl.program_id(0) == 0)
    def _():
        last = ends[0] + tile * ends[1]
        kid = kid_ref[tile]
        qid = qid_ref[...]
        allowed = kid == qid
        if causal:
            kpos = lax.broadcasted_iota(jnp.int32, (TILE, span), 1)
            qpos = lax.broadcasted_iota(jnp.int32, (TILE, span), 0) + (span - TILE)
            allowed = allowed & (kpos <= qpos)
        bias_ref[tile] = jnp.where(allowed, 0.0, NEG)

    def run(size):
        start = pl.multiple_of(ends[0] + tile * ends[1] - size, TILE)
        keys = k_ref[pl.ds(start, size), :]
        values = v_ref[pl.ds(start, size), :]
        query = q_ref[...] * jnp.asarray(0.125, BF16)
        outs = []
        lses = []
        for half in range(2):
            scores = lax.dot_general(head_lanes(query, half), keys, NT, preferred_element_type=F32)
            scores = scores + bias_ref[tile, :, span - size :]
            row_max = jnp.max(scores, axis=1, keepdims=True)
            weights = jnp.exp(scores - row_max)
            summed = jnp.sum(weights, axis=1, keepdims=True)
            out = jnp.dot(weights.astype(BF16), values, preferred_element_type=F32)
            outs.append(out / summed)
            lses.append(row_max + jnp.log(summed))
        lane = lax.broadcasted_iota(jnp.int32, (TILE, LANES), 1)
        o_ref[...] = jnp.where(lane < LANES // 2, outs[0], outs[1]).astype(BF16)
        for half in range(2):
            lse_ref[0, half : half + 1, :] = jnp.transpose(jnp.broadcast_to(lses[half], (TILE, LANES)))[:1]

    if len(sizes) == 1:
        run(sizes[0])
    else:
        number = n_ref[tile]
        for size in sizes:
            pl.when(number == size // TILE)(functools.partial(run, size))


def attend_forward(queries, keys, values, qid, kid, numbers, causal, sizes, ends):
    rows, width = queries.shape
    tiles = rows // TILE
    pairs = width // LANES
    key_rows = keys.shape[0]
    span = max(sizes)
    flops = 4 * rows * span * width
    return pl.pallas_call(
        functools.partial(forward_kernel, causal, sizes, ends),
        grid_spec=pltpu.PrefetchScalarGridSpec(
            num_scalar_prefetch=1,
            grid=(pairs, tiles),
            in_specs=[
                pl.BlockSpec((TILE, 1), lambda h, t, n: (t, 0)),
                pl.BlockSpec((tiles, 1, span), lambda h, t, n: (0, 0, 0)),
                pl.BlockSpec((TILE, LANES), lambda h, t, n: (t, h)),
                pl.BlockSpec((key_rows, LANES), lambda h, t, n: (0, h)),
                pl.BlockSpec((key_rows, LANES), lambda h, t, n: (0, h)),
            ],
            out_specs=[
                pl.BlockSpec((TILE, LANES), lambda h, t, n: (t, h)),
                pl.BlockSpec((1, 2, TILE), lambda h, t, n: (h, 0, t)),
            ],
            scratch_shapes=[pltpu.VMEM((tiles, TILE, span), F32)],
        ),
        out_shape=[
            jax.ShapeDtypeStruct((rows, width), BF16),
            jax.ShapeDtypeStruct((pairs, 2, rows), F32),
        ],
        compiler_params=pltpu.CompilerParams(vmem_limit_bytes=48 << 20),
        cost_estimate=pl.CostEstimate(flops=4 * flops, bytes_accessed=8 << 20, transcendentals=rows * span * HEADS),
    )(numbers, qid, kid, queries, keys, values)


def caption_lanes(value, lines, length):
    return jnp.concatenate([value[r * length : (r + 1) * length] for r in range(lines)], 1)


def spread(value, in_row):
    return jnp.concatenate([jnp.where(mask, value, jnp.zeros_like(value)) for mask in in_row], 1)


def rows_of(code, lines, length):
    return [(code >= r * length) & (code < (r + 1) * length) for r in range(lines)]


def either(masks):
    result = masks[0]
    for mask in masks[1:]:
        result = result | mask
    return result


def cross_forward_kernel(code_ref, key_ref, q_ref, k_ref, v_ref, o_ref, lse_ref):
    lines, length = key_ref.shape
    keys = caption_lanes(k_ref[...], lines, length)
    values = caption_lanes(v_ref[...], lines, length)
    lane = lax.broadcasted_iota(jnp.int32, (TILE, LANES), 1)
    for tile in range(q_ref.shape[0] // TILE):
        mine = slice(tile * TILE, (tile + 1) * TILE)
        code = jnp.broadcast_to(code_ref[mine, :], (TILE, LANES))
        in_row = rows_of(code, lines, length)
        allowed = either([code[:, :length] == key_ref[r : r + 1, :] for r in range(lines)])
        query = q_ref[mine, :] * jnp.asarray(0.125, BF16)
        outs = []
        for half in range(2):
            scores = lax.dot_general(
                spread(head_lanes(query, half), in_row), keys, NT, preferred_element_type=F32
            )
            scores = jnp.where(allowed, scores, NEG)
            row_max = jnp.max(scores, axis=1, keepdims=True)
            weights = jnp.exp(scores - row_max)
            summed = jnp.sum(weights, axis=1, keepdims=True)
            wide = jnp.dot(weights.astype(BF16), values, preferred_element_type=F32)
            out = jnp.zeros((TILE, LANES), F32)
            for r in range(lines):
                out = jnp.where(in_row[r], wide[:, r * LANES : (r + 1) * LANES], out)
            outs.append(out / summed)
            lse = jnp.broadcast_to(row_max + jnp.log(summed), (TILE, LANES))
            lse_ref[0, half : half + 1, mine] = jnp.transpose(lse)[:1]
        o_ref[mine, :] = jnp.where(lane < LANES // 2, outs[0], outs[1]).astype(BF16)


def cross_forward(queries, keys, values, query_code, key_codes):
    rows, width = queries.shape
    pairs = width // LANES
    text = keys.shape[0]
    own = pl.BlockSpec((rows, LANES), lambda h: (0, h))
    wide = pl.BlockSpec((text, LANES), lambda h: (0, h))
    return pl.pallas_call(
        cross_forward_kernel,
        grid=(pairs,),
        in_specs=[
            pl.BlockSpec((rows, 1), lambda h: (0, 0)), pl.BlockSpec(key_codes.shape, lambda h: (0, 0)), own, wide, wide,
        ],
        out_specs=[own, pl.BlockSpec((1, 2, rows), lambda h: (h, 0, 0))],
        out_shape=[
            jax.ShapeDtypeStruct((rows, width), BF16),
            jax.ShapeDtypeStruct((pairs, 2, rows), F32),
        ],
        compiler_params=pltpu.CompilerParams(vmem_limit_bytes=32 << 20),
        cost_estimate=pl.CostEstimate(
            flops=4 * rows * text * width, bytes_accessed=4 << 20, transcendentals=rows * text * HEADS // 4
        ),
    )(query_code, key_codes, queries, keys, values)


def backward_kernel(
    causal, sizes, ends, n_ref, qid_ref, kid_ref, q_ref, k_ref, v_ref, g_ref, o_ref, lse_ref,
    dq_ref, dk_ref, dv_ref, bias_ref, dk_sum, dv_sum,
):
    tile = pl.program_id(1)
    tiles = pl.num_programs(1)
    span = bias_ref.shape[1]

    @pl.when(pl.program_id(0) == 0)
    def _():
        kid = kid_ref[tile]
        qid = qid_ref[...]
        allowed = kid == qid
        if causal:
            kpos = lax.broadcasted_iota(jnp.int32, (span, TILE), 0)
            qpos = lax.broadcasted_iota(jnp.int32, (span, TILE), 1) + (span - TILE)
            allowed = allowed & (kpos <= qpos)
        bias_ref[tile] = jnp.where(allowed, 0.0, NEG)

    @pl.when(tile == 0)
    def _():
        dk_sum[...] = jnp.zeros_like(dk_sum)
        dv_sum[...] = jnp.zeros_like(dv_sum)

    def run(size):
        start = pl.multiple_of(ends[0] + tile * ends[1] - size, TILE)
        window = pl.ds(start, size)
        keys = k_ref[window, :]
        values = v_ref[window, :]
        query = q_ref[...] * jnp.asarray(0.125, BF16)
        grad = g_ref[...]
        inner = grad.astype(F32) * o_ref[...].astype(F32)
        inner_rows = jnp.transpose(inner)
        half_lanes = LANES // 2
        parts_dq = []
        dk = None
        dv = None
        for half in range(2):
            head_q = head_lanes(query, half)
            head_g = head_lanes(grad, half)
            lse = lse_ref[0, half : half + 1, :]
            delta = jnp.sum(inner_rows[half * half_lanes : (half + 1) * half_lanes, :], axis=0, keepdims=True)
            scores = lax.dot_general(keys, head_q, NT, preferred_element_type=F32)
            probs = jnp.exp(scores + bias_ref[tile, span - size :, :] - lse)
            grad_probs = lax.dot_general(values, head_g, NT, preferred_element_type=F32)
            grad_scores = (probs * (grad_probs - delta)).astype(BF16)
            probs = probs.astype(BF16)
            part_k = jnp.dot(grad_scores, head_q, preferred_element_type=F32)
            part_v = jnp.dot(probs, head_g, preferred_element_type=F32)
            dk = part_k if dk is None else dk + part_k
            dv = part_v if dv is None else dv + part_v
            parts_dq.append(lax.dot_general(grad_scores, keys, TN, preferred_element_type=F32))
        lane = lax.broadcasted_iota(jnp.int32, (TILE, LANES), 1)
        dq_ref[...] = (jnp.where(lane < half_lanes, parts_dq[0], parts_dq[1]) * 0.125).astype(BF16)
        dk_sum[window, :] += dk
        dv_sum[window, :] += dv

    if len(sizes) == 1:
        run(sizes[0])
    else:
        number = n_ref[tile]
        for size in sizes:
            pl.when(number == size // TILE)(functools.partial(run, size))

    @pl.when(tile == tiles - 1)
    def _():
        dk_ref[...] = dk_sum[...].astype(BF16)
        dv_ref[...] = dv_sum[...].astype(BF16)


def attend_backward(queries, keys, values, grad, out, lse, qid, kid, numbers, causal, sizes, ends):
    rows, width = queries.shape
    tiles = rows // TILE
    pairs = width // LANES
    key_rows = keys.shape[0]
    span = max(sizes)
    flops = 10 * rows * span * width
    near = pl.BlockSpec((TILE, LANES), lambda h, t, n: (t, h))
    wide = pl.BlockSpec((key_rows, LANES), lambda h, t, n: (0, h))
    return pl.pallas_call(
        functools.partial(backward_kernel, causal, sizes, ends),
        grid_spec=pltpu.PrefetchScalarGridSpec(
            num_scalar_prefetch=1,
            grid=(pairs, tiles),
            in_specs=[
                pl.BlockSpec((1, TILE), lambda h, t, n: (0, t)),
                pl.BlockSpec((tiles, span, 1), lambda h, t, n: (0, 0, 0)),
                near,
                wide,
                wide,
                near,
                near,
                pl.BlockSpec((1, 2, TILE), lambda h, t, n: (h, 0, t)),
            ],
            out_specs=[near, wide, wide],
            scratch_shapes=[
                pltpu.VMEM((tiles, span, TILE), F32),
                pltpu.VMEM((key_rows, LANES), F32),
                pltpu.VMEM((key_rows, LANES), F32),
            ],
        ),
        out_shape=[
            jax.ShapeDtypeStruct((rows, width), BF16),
            jax.ShapeDtypeStruct((key_rows, width), BF16),
            jax.ShapeDtypeStruct((key_rows, width), BF16),
        ],
        compiler_params=pltpu.CompilerParams(vmem_limit_bytes=48 << 20),
        cost_estimate=pl.CostEstimate(flops=4 * flops, bytes_accessed=12 << 20, transcendentals=rows * span * HEADS),
    )(numbers, qid, kid, queries, keys, values, grad, out, lse)


def factors(count):
    return {32: (4, 2, 2, 2), 128: (4, 4, 4, 2)}.get(count, (count,))


def coordinates(count):
    sizes = factors(count)
    left = lax.axis_index(AXIS)
    places = []
    for size in reversed(sizes):
        places.insert(0, lax.rem(left, size))
        left = lax.div(left, size)
    return places


def peers_along(count, axis, step):
    sizes = factors(count)
    stride = 1
    for size in sizes[axis + 1 :]:
        stride *= size
    size = sizes[axis]
    pairs = []
    for device in range(count):
        place = (device // stride) % size
        pairs.append((device, device + ((place + step) % size - place) * stride))
    return pairs


def take(value, place, axis):
    return lax.dynamic_slice_in_dim(value, place, 1, axis)


def total(terms):
    summed = terms[0].astype(F32)
    for term in terms[1:]:
        summed = summed + term.astype(F32)
    return summed


def reduce_scatter(value, order, kind, count):
    sizes = factors(count)
    places = coordinates(count)
    rows, width = value.shape
    terms = [value.reshape(*sizes, rows // count, width)]
    for axis in order:
        size = sizes[axis]
        arrived = []
        for step in range(1, size):
            other = lax.rem(places[axis] + step, size)
            sent = total([take(term, other, axis) for term in terms]).astype(kind)
            arrived.append(lax.ppermute(sent, AXIS, peers_along(count, axis, step)))
        terms = [take(term, places[axis], axis) for term in terms] + arrived
    return total(terms).reshape(rows // count, width)


def all_gather(value, order, count):
    sizes = factors(count)
    places = coordinates(count)
    rows, width = value.shape
    held = value.reshape(*([1] * len(sizes)), rows, width)
    for axis in order:
        size = sizes[axis]
        shape = list(held.shape)
        shape[axis] = size
        gathered = lax.dynamic_update_slice_in_dim(jnp.zeros(shape, held.dtype), held, places[axis], axis)
        for step in range(1, size):
            arrived = lax.ppermute(held, AXIS, peers_along(count, axis, step))
            source = lax.rem(places[axis] + size - step, size)
            gathered = lax.dynamic_update_slice_in_dim(gathered, arrived, source, axis)
        held = gathered
    return held.reshape(rows * count, width)


MESH = pl.DeviceIdType.MESH
BLOCK = 32
WIDE = 1024


def places32():
    me = lax.axis_index(AXIS)
    core = lax.rem(me, 2)
    x = lax.rem(lax.div(me, 2), 2)
    y = lax.rem(lax.div(me, 4), 2)
    z = lax.div(me, 8)
    return me, core, x, y, z


GELU_A = 0.7978845608028654
GELU_B = 0.044715


def gelu_and_slope(value):
    square = value * value
    bend = jnp.tanh(GELU_A * (value + GELU_B * value * square))
    gate = 0.5 * (1.0 + bend)
    slope = gate + value * 0.5 * (1.0 - bend * bend) * (GELU_A * (1.0 + 3.0 * GELU_B * square))
    return value * gate, slope


def normalise_rows(value):
    mean = jnp.mean(value, axis=-1, keepdims=True)
    centred = value - mean
    scale = lax.rsqrt(jnp.mean(centred * centred, axis=-1, keepdims=True) + EPS)
    return centred * scale, scale


class Far(NamedTuple):
    low_three: Any
    out_grad: Any
    after_two: Any
    up_weight: Any
    down_weight: Any
    cross_att: Any
    cross_q: Any
    text_keys: Any
    text_values: Any
    low_two: Any
    after_one: Any
    captions: Any
    cross_output: Any
    cross_key: Any
    cross_value: Any
    cross_query: Any
    output_weight: Any
    queries: Any
    near_keys: Any
    near_values: Any
    self_att: Any
    near_low: Any
    near_tokens: Any
    query_weight: Any
    key_weight: Any
    value_weight: Any


class Near(NamedTuple):
    starts: Any
    self_lse: Any
    query_code: Any
    key_code: Any
    cross_lse: Any
    gains: Any


class Sums(NamedTuple):
    up: Any
    down: Any
    cross_output: Any
    cross_key: Any
    cross_value: Any
    caption: Any
    cross_query: Any
    output: Any
    query: Any
    key: Any
    value: Any


class Scratch(NamedTuple):
    arena: Any
    sums: Any
    accum_k: Any
    accum_v: Any
    back_one: Any
    back_two: Any
    vec: Any
    vec_in: Any
    tiles: Any
    r0: Any
    r1: Any
    r2: Any
    r3: Any
    load: Any
    s0: Any
    d0: Any
    s1: Any
    d1: Any
    s2: Any
    d2: Any
    s3: Any
    d3: Any
    vs: Any
    vd: Any
    bs: Any
    bd: Any
    credit: Any


UP, DOWN, CROSS_OUTPUT, CROSS_KEY, CROSS_VALUE, CAPTION, CROSS_QUERY, OUTPUT, QUERY, KEY, VALUE = range(11)
PIECES = (
    (UP, 0), (UP, 1), (UP, 2), (UP, 3), (DOWN, 0), (DOWN, 1), (DOWN, 2), (DOWN, 3),
    (CROSS_OUTPUT, 0), (CROSS_KEY, 0), (CROSS_VALUE, 0), (CAPTION, 0), (CROSS_QUERY, 0), (OUTPUT, 0),
    (QUERY, 0), (KEY, 0), (VALUE, 0),
)
PLAN = (
    (), (), (), (), ((2, 0),), (), ((2, 1),), ((2, 2),), (), ((2, 3),), (), (), (), ((3, 0), (2, 4)), (), (), (),
    (), ((3, 1),), (), (), (), ((2, 5),), (), (), (), (), ((3, 2), (2, 6)), (), (), (), ((3, 3),), (), ((2, 7),),
    (), (), ((3, 4), (2, 8)), ((3, 6), (3, 5)), ((1, 13),), ((3, 7),), (), ((2, 9),), (), (), ((2, 10),), (), (),
    ((2, 11),), (), ((3, 8), (2, 12)), (), (), ((3, 9),), (), ((2, 13), (3, 11)), ((3, 10),), ((3, 12),), (),
    ((2, 14),), ((3, 13),),
)
LANDINGS = 9
SLOTS = 2
HALF = LANES // 2
STEP = 64
LOADS = 48


def layer_kernel(rows, *refs):
    total = len(PIECES)
    n_far, n_near, n_sums = len(Far._fields), len(Near._fields), len(Sums._fields)
    far = Far(*refs[:n_far])
    near = Near(*refs[n_far : n_far + n_near])
    refs = refs[n_far + n_near :]
    outs = Sums(*refs[:n_sums])
    vec_out, block_output, input_grad = refs[n_sums : n_sums + 3]
    held = Scratch(*refs[n_sums + 3 :])
    (arena, sums, accum_k, accum_v, back_one, back_two, vec, vec_in, tiles, r0, r1, r2, r3,
     load, s0, d0, s1, d1, s2, d2, s3, d3, vs, vd, bs, bd, credit) = held

    me, core, x, y, z = places32()
    sibling = me + 1 - 2 * core
    x_peer = me + 2 - 4 * x
    y_peer = me + 4 - 8 * y
    z_other = [lax.rem(z + m, 4) for m in range(1, 4)]
    z_peers = [me + 8 * (o - z) for o in z_other]
    has_before = me >= 2
    has_after = me < 30

    barrier = pltpu.get_barrier_semaphore()
    for peer in (sibling, x_peer, y_peer, *z_peers):
        pl.semaphore_signal(barrier, inc=1, device_id=(peer,), device_id_type=MESH)

    @pl.when(has_before)
    def _():
        pl.semaphore_signal(barrier, inc=1, device_id=(me - 2,), device_id_type=MESH)

    @pl.when(has_after)
    def _():
        pl.semaphore_signal(barrier, inc=1, device_id=(me + 2,), device_id_type=MESH)

    numbers = iter(range(LOADS))

    def fetch(source, slot):
        return start_copy(source, arena.at[pl.ds(slot * rows, source.shape[0])])

    def start_copy(source, target):
        copy = pltpu.make_async_copy(source, target, load.at[next(numbers)])
        copy.start()
        return copy

    def at(slot, count=1):
        return pl.ds(slot * rows, count * rows)

    def up_part(part):
        return far.up_weight.at[:, pl.ds(part * WIDE, WIDE)]

    def down_part(part):
        return far.down_weight.at[pl.ds(part * WIDE, WIDE)]

    ONE, TWO, THREE = 12, 14, 10
    low_three_load = fetch(far.low_three, 8)
    up_loads = [fetch(up_part(0), THREE)]
    out_grad_load = fetch(far.out_grad, 9)
    down_loads = [fetch(down_part(0), ONE)]
    up_loads.append(fetch(up_part(1), TWO))
    after_load = start_copy(far.after_two, sums.at[2])

    pl.semaphore_wait(barrier, 6 + jnp.where(has_before, 1, 0) + jnp.where(has_after, 1, 0))

    def remote(src, dst, send, recv, peer):
        return pltpu.make_async_remote_copy(
            src_ref=src, dst_ref=dst, send_sem=send, recv_sem=recv, device_id=(peer,), device_id_type=MESH
        )

    def along(c):
        even = lax.rem(c, 2) == 0
        return (
            jnp.where(even, x, y),
            jnp.where(even, x_peer, y_peer),
            jnp.where(even, y, x),
            jnp.where(even, y_peer, x_peer),
        )

    def add_blocks(count, dst, src):
        @pl.loop(0, count, unroll=4)
        def _(i):
            dst(i)[...] = dst(i)[...] + src(i)[...]

    def take_credit(c):
        if c >= LANDINGS:
            pl.semaphore_wait(credit, 1)

    def give(c):
        take_credit(c)
        remote(tiles.at[c % SLOTS, 1 - core], r0.at[c % LANDINGS], s0.at[c], d0.at[c], sibling).start()

    def make(c, left_at, right_at, depth):
        @pl.loop(0, 4)
        def _(zz):
            left = arena[pl.ds(left_at * rows, depth), pl.ds(pl.multiple_of(zz * TILE, TILE), TILE)]
            for part in range(2):
                cols = slice(part * (WIDE // 2), (part + 1) * (WIDE // 2))
                result = lax.dot_general(
                    left, arena[pl.ds(right_at * rows, depth), cols], TN, preferred_element_type=F32
                ).astype(BF16)
                for block in range(8):
                    yy, xx, cc = block // 4, (block // 2) % 2, block % 2
                    f, s = (xx, yy) if c % 2 == 0 else (yy, xx)
                    tiles[c % SLOTS, cc, f, s, zz, :, cols] = result[block * BLOCK : (block + 1) * BLOCK]

        give(c)

    def make_down(c, part):
        @pl.loop(0, 4)
        def _(zz):
            for quarter in range(4):
                yy, xx = quarter // 2, quarter % 2
                f, s = (xx, yy) if c % 2 == 0 else (yy, xx)
                left = arena[
                    pl.ds(pl.multiple_of(zz * rows, rows), rows), quarter * TILE : (quarter + 1) * TILE
                ]
                result = lax.dot_general(
                    left, arena[at(9), part * TILE : (part + 1) * TILE], TN, preferred_element_type=F32
                ).astype(BF16)
                for cc in range(2):
                    for group in range(4):
                        top = cc * 128 + group * BLOCK
                        tiles[c % SLOTS, cc, f, s, zz, :, group * TILE : (group + 1) * TILE] = result[top : top + BLOCK]

        give(c)

    def first(c):
        f, fp, _, _ = along(c)
        slot, place = c % SLOTS, c % LANDINGS
        copy = remote(tiles.at[slot, 1 - core], r0.at[place], s0.at[c], d0.at[c], sibling)
        copy.wait_recv()
        add_blocks(
            16,
            lambda i: r0.at[place, i // 8, (i // 4) % 2, i % 4],
            lambda i: tiles.at[slot, core, i // 8, (i // 4) % 2, i % 4],
        )
        remote(r0.at[place, 1 - f], r1.at[c], s1.at[c], d1.at[c], fp).start()
        copy.wait_send()

    def second(c):
        f, fp, s, sp = along(c)
        place = c % LANDINGS
        copy = remote(r0.at[place, 1 - f], r1.at[c], s1.at[c], d1.at[c], fp)
        copy.wait_recv()
        add_blocks(8, lambda i: r1.at[c, i // 4, i % 4], lambda i: r0.at[place, f, i // 4, i % 4])
        remote(r1.at[c, 1 - s], r2.at[c], s2.at[c], d2.at[c], sp).start()
        copy.wait_send()
        if c < total - LANDINGS:
            pl.semaphore_signal(credit, inc=1, device_id=(sibling,), device_id_type=MESH)

    def third(c):
        _, _, s, sp = along(c)
        copy = remote(r1.at[c, 1 - s], r2.at[c], s2.at[c], d2.at[c], sp)
        copy.wait_recv()
        add_blocks(4, lambda i: r2.at[c, i], lambda i: r1.at[c, s, i])
        for m in range(3):
            remote(r2.at[c, z_other[m]], r3.at[c, m], s3.at[c, m], d3.at[c, m], z_peers[m]).start()
        copy.wait_send()

    def last(c):
        number, part = PIECES[c]
        for m in range(3):
            remote(r2.at[c, z_other[m]], r3.at[c, m], s3.at[c, m], d3.at[c, m], z_peers[m]).wait()
        summed = r2[c, z].astype(F32) + r3[c, 0].astype(F32) + r3[c, 1].astype(F32) + r3[c, 2].astype(F32)
        out = outs[number]
        if number == DOWN:
            for group in range(4):
                out[group * BLOCK : (group + 1) * BLOCK, part * TILE : (part + 1) * TILE] = summed[
                    :, group * TILE : (group + 1) * TILE
                ]
        else:
            out[:, part * WIDE : (part + 1) * WIDE] = summed[: out.shape[0]]

    def each_tile(run):
        @pl.loop(0, WIDE // TILE, unroll=2)
        def _(n):
            run(pl.multiple_of(n * TILE, TILE))

    def product(pairs, add=False):
        def run(n):
            result = None
            for slot, weight in pairs:
                term = lax.dot_general(
                    arena[at(slot), :], arena[pl.ds(weight * rows + n, TILE), :], NT, preferred_element_type=F32
                )
                result = term if result is None else result + term
            if add:
                result += sums[0, :, pl.ds(n, TILE)]
            sums[0, :, pl.ds(n, TILE)] = result

        each_tile(run)

    def plain_product(slot, weight, add):
        def run(n):
            result = jnp.dot(arena[at(slot), :], arena[at(weight, 2), pl.ds(n, TILE)], preferred_element_type=F32)
            if add:
                result += sums[0, :, pl.ds(n, TILE)]
            sums[0, :, pl.ds(n, TILE)] = result

        each_tile(run)

    def low_product(slot, weight, target):
        def run(n):
            result = lax.dot_general(
                arena[at(slot), :], arena[pl.ds(weight * rows + n, TILE), :], NT, preferred_element_type=F32
            )
            arena[at(target), pl.ds(n, TILE)] = result.astype(BF16)

        each_tile(run)

    def each_step(run):
        @pl.loop(0, rows // STEP)
        def _(i):
            run(pl.multiple_of(i * STEP, STEP))

    vec[...] = jnp.zeros_like(vec)

    def add_gains(row, grad, unit):
        vec[row : row + 1] += jnp.sum(grad * unit, axis=0, keepdims=True)
        vec[row + 1 : row + 2] += jnp.sum(grad, axis=0, keepdims=True)

    def norm_back_rows(grad, unit, scale, gain):
        scaled = grad * gain
        return scale * (
            scaled - jnp.mean(scaled, axis=-1, keepdims=True) - unit * jnp.mean(scaled * unit, axis=-1, keepdims=True)
        )

    def attend_step(keys, values, query, grad, out, lse, allowed):
        query = query * jnp.asarray(0.125, BF16)
        inner = jnp.transpose(grad.astype(F32) * out.astype(F32))
        turned_keys = jnp.transpose(keys)
        parts = []
        dk = None
        dv = None
        for half in range(2):
            head_q = head_lanes(query, half)
            head_g = head_lanes(grad, half)
            delta = jnp.sum(inner[half * HALF : (half + 1) * HALF], axis=0, keepdims=True)
            scores = lax.dot_general(keys, head_q, NT, preferred_element_type=F32)
            probs = jnp.exp(jnp.where(allowed, scores - lse[half], NEG))
            grad_probs = lax.dot_general(values, head_g, NT, preferred_element_type=F32)
            grad_scores = (probs * (grad_probs - delta)).astype(BF16)
            part_k = jnp.dot(grad_scores, head_q, preferred_element_type=F32)
            part_v = jnp.dot(probs.astype(BF16), head_g, preferred_element_type=F32)
            dk = part_k if dk is None else dk + part_k
            dv = part_v if dv is None else dv + part_v
            parts.append(jnp.dot(turned_keys, grad_scores, preferred_element_type=F32))
        dq = jnp.concatenate([parts[0][:HALF], parts[1][HALF:]], 0)
        return (jnp.transpose(dq) * 0.125).astype(BF16), dk, dv

    position = [0]

    def take_steps(steps):
        for kind, c in steps:
            (first, second, third)[kind - 1](c)

    def tick():
        take_steps(PLAN[position[0]])
        position[0] += 1

    def loop_tick(base, i):
        for number, steps in enumerate(PLAN[base : base + 16]):
            if steps:
                pl.when(i == number)(functools.partial(take_steps, steps))

    def activate(part, up_at, down_at):
        def run(n):
            cols = pl.ds(n, TILE)
            pre = jnp.dot(arena[at(8), :], arena[at(up_at, 2), cols], preferred_element_type=F32)
            grad = lax.dot_general(
                arena[at(9), :], arena[pl.ds(down_at * rows + n, TILE), :], NT, preferred_element_type=F32
            )
            hidden, slope = gelu_and_slope(pre)
            arena[at(part), cols] = hidden.astype(BF16)
            arena[at(4 + part), cols] = (slope * grad).astype(BF16)

        each_tile(run)

    low_three_load.wait()
    out_grad_load.wait()
    places = ((THREE, ONE), (TWO, THREE), (ONE, TWO), (THREE, ONE))
    for part in range(4):
        up_loads[part].wait()
        down_loads[part].wait()
        activate(part, *places[part])
        if part == 0:
            down_loads.append(fetch(down_part(1), THREE))
            up_loads.append(fetch(up_part(2), ONE))
        if part == 1:
            down_loads.append(fetch(down_part(2), TWO))
            up_loads.append(fetch(up_part(3), THREE))
        if part == 2:
            down_loads.append(fetch(down_part(3), ONE))
            weight_two = fetch(up_part(1), TWO)
        if part == 3:
            weight_one = fetch(up_part(0), ONE)
        make(part, 8, 4 + part, rows)
        if part > 0:
            first(part - 1)
        tick()
    places = (ONE, TWO, THREE, ONE)
    loads = [weight_one, weight_two, fetch(up_part(2), THREE)]
    for part in range(4):
        make_down(4 + part, part)
        loads[part].wait()
        product([(4 + part, places[part])], add=part > 0)
        if part == 0:
            loads.append(fetch(up_part(3), ONE))
        first(3 + part)
        tick()
    weight_two = fetch(far.cross_output, TWO)
    weight_three = fetch(down_part(0), THREE)
    weight_one = fetch(down_part(1), ONE)
    low_two_load = fetch(far.low_two, 4)
    captions_load = fetch(far.captions, 5)
    cross_att_load = fetch(far.cross_att, 6)
    cross_q_load = fetch(far.cross_q, 7)
    after_load.wait()
    gains = near.gains

    def norm_three(n):
        here = pl.ds(n, STEP)
        unit, scale = normalise_rows(sums[2, here, :])
        grad = sums[0, here, :]
        add_gains(4, grad, unit)
        value = arena[pl.ds(9 * rows + n, STEP), :].astype(F32) + norm_back_rows(grad, unit, scale, gains[2:3])
        sums[1, here, :] = value
        arena[pl.ds(9 * rows + n, STEP), :] = value.astype(BF16)

    each_step(norm_three)
    first(7)
    tick()

    weight_two.wait()
    low_product(9, TWO, 8)
    weight_two = fetch(down_part(2), TWO)
    cross_att_load.wait()
    make(8, 6, 9, rows)
    tick()
    weight_three.wait()
    plain_product(0, THREE, False)
    weight_three = fetch(down_part(3), THREE)
    tick()
    weight_one.wait()
    plain_product(1, ONE, True)
    weight_one = fetch(far.cross_key, ONE)
    first(8)
    tick()
    weight_two.wait()
    plain_product(2, TWO, True)
    weight_two = fetch(far.cross_value, TWO)
    keys_load = fetch(far.text_keys, 2)
    tick()
    weight_three.wait()
    plain_product(3, THREE, True)
    weight_three = fetch(far.cross_query, THREE)
    values_load = fetch(far.text_values, 3)
    tick()

    def finish_block(n):
        here = pl.ds(n, STEP)
        arena[pl.ds(n, STEP), :] = (sums[2, here, :] + sums[0, here, :]).astype(BF16)

    each_step(finish_block)
    tick()
    loop_base = position[0]
    position[0] += 16
    block_copy = start_copy(arena.at[at(0)], block_output)
    after_load = start_copy(far.after_one, sums.at[2])

    text = far.text_keys.shape[0]
    cross_q_load.wait()
    keys_load.wait()
    values_load.wait()

    @pl.loop(0, 16)
    def _(i):
        h, t = lax.div(i, 2), lax.rem(i, 2)
        lanes = pl.ds(pl.multiple_of(h * LANES, LANES), LANES)
        own = pl.multiple_of(t * TILE, TILE)
        mine = pl.ds(7 * rows + own, TILE)
        allowed = near.key_code[...] == near.query_code[:, pl.ds(own, TILE)]
        lse = [near.cross_lse[h, half : half + 1, pl.ds(own, TILE)] for half in range(2)]
        dq, dk, dv = attend_step(
            arena[at(2), lanes], arena[at(3), lanes], arena[mine, lanes],
            arena[pl.ds(8 * rows + own, TILE), lanes], arena[pl.ds(6 * rows + own, TILE), lanes], lse, allowed,
        )
        arena[mine, lanes] = dq

        @pl.when(t == 0)
        def _():
            accum_k[:text] = dk
            accum_v[:text] = dv

        @pl.when(t == 1)
        def _():
            arena[at(2), lanes] = (accum_k[:text] + dk).astype(BF16)
            arena[at(3), lanes] = (accum_v[:text] + dv).astype(BF16)

        loop_tick(loop_base, i)

    block_copy.wait()
    self_att_load = fetch(far.self_att, 8)
    captions_load.wait()
    make(9, 5, 2, rows)
    tick()
    weight_one.wait()
    weight_two.wait()
    product([(2, ONE), (3, TWO)])
    weight_one = fetch(far.output_weight, ONE)
    make(10, 5, 3, rows)
    first(9)
    tick()

    c = 11
    for zz in range(4):
        for block in range(8):
            yy, xx, cc = block // 4, (block // 2) % 2, block % 2
            f, s = (xx, yy) if c % 2 == 0 else (yy, xx)
            top = (zz * 8 + block) * 16
            tiles[c % SLOTS, cc, f, s, zz, :16, :] = sums[0, top : top + 16, :].astype(BF16)
            tiles[c % SLOTS, cc, f, s, zz, 16:, :] = jnp.zeros((16, WIDE), BF16)
    give(c)
    tick()
    keys_load = fetch(far.near_keys, 1)
    weight_three.wait()
    product([(7, THREE)])
    near_low_load = fetch(far.near_low, 9)
    first(10)
    tick()
    low_two_load.wait()
    make(12, 4, 7, rows)
    values_load = fetch(far.near_values, 4)
    queries_load = fetch(far.queries, 0)
    first(11)
    tick()
    after_load.wait()

    def norm_two(n):
        here = pl.ds(n, STEP)
        unit, scale = normalise_rows(sums[2, here, :])
        grad = sums[0, here, :]
        add_gains(2, grad, unit)
        value = sums[1, here, :] + norm_back_rows(grad, unit, scale, gains[1:2])
        sums[1, here, :] = value
        arena[pl.ds(14 * rows + n, STEP), :] = value.astype(BF16)

    each_step(norm_two)
    first(12)
    tick()

    weight_one.wait()
    low_product(14, ONE, 7)
    weight_one = fetch(far.value_weight, ONE)
    self_att_load.wait()
    make(13, 8, 14, rows)
    tick()
    loop_base = position[0]
    position[0] += 16
    weight_two = fetch(far.key_weight, TWO)
    queries_load.wait()
    keys_load.wait()
    values_load.wait()

    span = 2 * rows + TILE

    @pl.loop(0, 16)
    def _(i):
        h, t = lax.div(i, 2), lax.rem(i, 2)
        lanes = pl.ds(pl.multiple_of(h * LANES, LANES), LANES)
        own = pl.multiple_of(t * TILE, TILE)
        mine = pl.ds(own, TILE)
        kpos = lax.broadcasted_iota(jnp.int32, (span, TILE), 0)
        qpos = lax.broadcasted_iota(jnp.int32, (TILE, TILE), 1)
        dpos = lax.broadcasted_iota(jnp.int32, (TILE, TILE), 0)
        allowed = kpos >= near.starts[:, mine] - own
        allowed = jnp.concatenate([allowed[: span - TILE], allowed[span - TILE :] & (dpos <= qpos)], 0)
        lse = [near.self_lse[h, half : half + 1, mine] for half in range(2)]
        dq, dk, dv = attend_step(
            arena[pl.ds(rows + own, span), lanes], arena[pl.ds(4 * rows + own, span), lanes], arena[mine, lanes],
            arena[pl.ds(7 * rows + own, TILE), lanes], arena[pl.ds(8 * rows + own, TILE), lanes], lse, allowed,
        )
        arena[mine, lanes] = dq

        @pl.when(t == 0)
        def _():
            accum_k[:span] = dk
            accum_v[:span] = dv

        @pl.when(t == 1)
        def _():
            for target, accum, part in ((1, accum_k, dk), (4, accum_v, dv)):
                arena[pl.ds(target * rows, TILE), lanes] = accum[:TILE].astype(BF16)
                arena[pl.ds(target * rows + TILE, span - TILE), lanes] = (accum[TILE:span] + part[: span - TILE]).astype(BF16)
                arena[pl.ds(target * rows + span, TILE), lanes] = part[span - TILE :].astype(BF16)

        loop_tick(loop_base, i)

    near_low_load.wait()
    make(14, 11, 0, rows)
    weight_two.wait()
    weight_one.wait()
    product([(2, TWO), (5, ONE)])

    def as_low(slot, extra):
        def run(n):
            value = sums[0, pl.ds(n, STEP), :]
            if extra is not None:
                value = value + jnp.where(core == 1, extra[pl.ds(n, STEP), :].astype(F32), 0.0)
            arena[pl.ds(slot * rows + n, STEP), :] = value.astype(BF16)

        each_step(run)

    as_low(7, None)
    swap = remote(arena.at[at(7)], back_one, bs.at[0], bd.at[0], sibling)
    swap.start()
    first(14)
    tick()
    product([(1, TWO), (4, ONE)])
    swap.wait()
    as_low(8, back_one)
    send_back = remote(arena.at[at(8)], back_two, bs.at[1], bd.at[1], me - 2)

    @pl.when(has_before)
    def _():
        send_back.start()

    tick()
    make(15, 9, 1, 3 * rows)
    tick()
    query_weight_load = fetch(far.query_weight, 1)
    make(16, 9, 4, 3 * rows)
    token_load = fetch(far.near_tokens, 9)
    first(15)
    tick()

    def block_gains(slot, grad_slot, factor):
        def run(n):
            unit, _ = normalise_rows(arena[pl.ds(slot * rows + n, STEP), :].astype(F32))
            if grad_slot is None:
                grad = sums[0, pl.ds(n, STEP), :]
            else:
                grad = arena[pl.ds(grad_slot * rows + n, STEP), :].astype(F32)
            if factor is not None:
                grad = grad * factor
            add_gains(0, grad, unit)

        each_step(run)

    token_load.wait()
    block_gains(9, 8, None)
    block_gains(10, 7, jnp.where(core == 1, 1.0, 0.0))
    first(16)
    tick()
    query_weight_load.wait()
    product([(0, 1), (3, TWO), (6, ONE)])
    tick()
    block_gains(11, None, None)

    def vec_step(number, peer):
        step = remote(vec, vec_in.at[number], vs.at[number], vd.at[number], peer)
        step.start()
        return step

    def norm_one(n):
        here = pl.ds(n, STEP)
        unit, scale = normalise_rows(arena[pl.ds(11 * rows + n, STEP), :].astype(F32))
        grad = sums[0, here, :]
        grad = grad + jnp.where(core == 0, back_one[here, :].astype(F32), 0.0)
        grad = grad + jnp.where(has_after, back_two[here, :].astype(F32), 0.0)
        sums[1, here, :] += norm_back_rows(grad, unit, scale, gains[0:1])

    step = vec_step(0, sibling)
    step.wait()
    vec[...] += vec_in[0]
    step = vec_step(1, x_peer)
    second(15)

    @pl.when(has_before)
    def _():
        send_back.wait_send()

    @pl.when(has_after)
    def _():
        send_back.wait_recv()

    each_step(norm_one)
    out_copy = start_copy(sums.at[1], input_grad)
    step.wait()
    vec[...] += vec_in[1]
    step = vec_step(2, y_peer)
    third(14)
    second(16)
    step.wait()
    vec[...] += vec_in[2]
    steps = [vec_step(3 + m, z_peers[m]) for m in range(3)]
    for c in range(total - 3):
        last(c)
    third(15)
    third(16)
    for step in steps:
        step.wait()
    vec_out[...] = vec[...] + vec_in[3] + vec_in[4] + vec_in[5]
    for c in range(total - 3, total):
        last(c)
    out_copy.wait()


def copy_kernel(number, *refs):
    sources, targets, staged = refs[:number], refs[number : 2 * number], refs[2 * number : 3 * number]
    sem_in, sem_out = refs[3 * number :]
    inward = [pltpu.make_async_copy(sources[i], staged[i], sem_in.at[i]) for i in range(number)]
    outward = [pltpu.make_async_copy(staged[i], targets[i], sem_out.at[i]) for i in range(number)]
    for copy in inward:
        copy.start()
    for i in range(number):
        inward[i].wait()
        outward[i].start()
    for copy in outward:
        copy.wait()


def copy_all(arrays):
    anywhere = pl.BlockSpec(memory_space=pl.ANY)
    return pl.pallas_call(
        functools.partial(copy_kernel, len(arrays)),
        in_specs=[anywhere] * len(arrays),
        out_specs=[anywhere] * len(arrays),
        out_shape=[jax.ShapeDtypeStruct(array.shape, array.dtype) for array in arrays],
        scratch_shapes=[pltpu.VMEM(array.shape, array.dtype) for array in arrays]
        + [pltpu.SemaphoreType.DMA((len(arrays),))] * 2,
        cost_estimate=pl.CostEstimate(flops=0, bytes_accessed=12 << 20, transcendentals=0),
    )(*arrays)


def layer_tail(far, near):
    rows, width = far.queries.shape
    count = 32
    sizes = {UP: (BLOCK, 4 * WIDE), DOWN: (4 * BLOCK, WIDE), CAPTION: (far.captions.shape[0] // count, WIDE)}
    total = len(PIECES)
    local = pl.BlockSpec(memory_space=pltpu.VMEM)
    anywhere = pl.BlockSpec(memory_space=pl.ANY)
    dma = pltpu.SemaphoreType.DMA
    scratch = Scratch(
        arena=pltpu.VMEM((16 * rows, width), BF16),
        sums=pltpu.VMEM((3, rows, width), F32),
        accum_k=pltpu.VMEM((3 * rows, LANES), F32),
        accum_v=pltpu.VMEM((3 * rows, LANES), F32),
        back_one=pltpu.VMEM((rows, width), BF16),
        back_two=pltpu.VMEM((rows, width), BF16),
        vec=pltpu.VMEM((8, width), F32),
        vec_in=pltpu.VMEM((6, 8, width), F32),
        tiles=pltpu.VMEM((SLOTS, 2, 2, 2, 4, BLOCK, WIDE), BF16),
        r0=pltpu.VMEM((LANDINGS, 2, 2, 4, BLOCK, WIDE), BF16),
        r1=pltpu.VMEM((total, 2, 4, BLOCK, WIDE), BF16),
        r2=pltpu.VMEM((total, 4, BLOCK, WIDE), BF16),
        r3=pltpu.VMEM((total, 3, BLOCK, WIDE), BF16),
        load=dma((LOADS,)), s0=dma((total,)), d0=dma((total,)), s1=dma((total,)), d1=dma((total,)),
        s2=dma((total,)), d2=dma((total,)), s3=dma((total, 3)), d3=dma((total, 3)), vs=dma((6,)), vd=dma((6,)),
        bs=dma((2,)), bd=dma((2,)), credit=pltpu.SemaphoreType.REGULAR,
    )
    results = pl.pallas_call(
        functools.partial(layer_kernel, rows),
        in_specs=[anywhere] * len(far) + [local] * len(near),
        out_specs=[local] * (len(Sums._fields) + 1) + [anywhere] * 2,
        out_shape=[jax.ShapeDtypeStruct(sizes.get(number, (BLOCK, WIDE)), F32) for number in range(len(Sums._fields))]
        + [
            jax.ShapeDtypeStruct((8, width), F32),
            jax.ShapeDtypeStruct((rows, width), BF16),
            jax.ShapeDtypeStruct((rows, width), F32),
        ],
        scratch_shapes=list(scratch),
        compiler_params=pltpu.CompilerParams(collective_id=0, has_side_effects=True, vmem_limit_bytes=63 << 20),
        cost_estimate=pl.CostEstimate(flops=1 << 34, bytes_accessed=64 << 20, transcendentals=0),
    )(*far, *near)
    small = results[len(Sums._fields)]
    copied = copy_all([*results[: len(Sums._fields)], *results[len(Sums._fields) + 1 :]])
    return Sums(*copied[:-2]), small, *copied[-2:]


def matmul(left, right):
    return jnp.dot(left, right, preferred_element_type=F32)


def left_product(left, right):
    return lax.dot_general(left, right, TN, preferred_element_type=F32)


def right_product(left, right):
    return lax.dot_general(left, right, NT, preferred_element_type=F32)


def normalise(value):
    mean = jnp.mean(value, axis=-1, keepdims=True)
    centred = value - mean
    scale = lax.rsqrt(jnp.mean(centred * centred, axis=-1, keepdims=True) + EPS)
    return centred * scale, scale


def norm_back(grad, unit, scale, gain):
    scaled = grad * gain
    return scale * (
        scaled
        - jnp.mean(scaled, axis=-1, keepdims=True)
        - unit * jnp.mean(scaled * unit, axis=-1, keepdims=True)
    )


def body(
    tokens, out_grad, caption_states,
    query_weight, key_weight, value_weight, output_weight,
    cross_query, cross_key, cross_value, cross_output,
    up_weight, down_weight,
    attn_gain, attn_bias, cross_gain, cross_bias, mlp_gain, mlp_bias,
    item_ids, caption_segments, item_rows, item_segments,
):
    device = lax.axis_index(AXIS)
    count = lax.axis_size(AXIS)
    rows = tokens.shape[0]
    tiles = rows // TILE
    odd = lax.rem(device, 2) == 1
    swap = [(i, i ^ 1) for i in range(count)]
    ahead = [(i, i + 2) for i in range(count - 2)]
    behind = [(i + 2, i) for i in range(count - 2)]

    inputs = tokens.astype(F32)
    low_one = (normalise(inputs)[0] * attn_gain + attn_bias).astype(BF16)
    queries = matmul(low_one, query_weight).astype(BF16)
    text_keys = matmul(caption_states, cross_key).astype(BF16)
    text_values = matmul(caption_states, cross_value).astype(BF16)
    block_two = lax.ppermute(tokens, AXIS, ahead)
    block_two, queries, text_keys, text_values = lax.optimization_barrier((block_two, queries, text_keys, text_values))
    block_one = lax.ppermute(jnp.where(odd, block_two, tokens), AXIS, swap)
    near_tokens = jnp.concatenate([block_two, block_one, tokens], 0)

    all_ids = jnp.concatenate([jnp.full((REACH * rows,), -1, jnp.int32), item_ids])
    near_ids = lax.dynamic_slice_in_dim(all_ids, device * rows, (REACH + 1) * rows)
    own_ids = near_ids[REACH * rows :]
    near_rows = (REACH + 1) * rows
    span = REACH * rows + TILE
    windows = jnp.stack([near_ids[t * TILE : t * TILE + span] for t in range(tiles)])
    firsts = own_ids[::TILE]
    before = jnp.sum((near_ids[None, :] < firsts[:, None]).astype(jnp.int32), axis=1)
    lasts = REACH * rows + TILE * (1 + jnp.arange(tiles, dtype=jnp.int32))
    numbers = lasts // TILE - before // TILE
    numbers = jnp.clip(numbers, 1, span // TILE)
    self_sizes = tuple(TILE * (i + 1) for i in range(span // TILE))
    self_ends = (REACH * rows + TILE, TILE)

    text = caption_states.shape[0]
    caption_len = caption_segments.shape[1]
    member = own_ids[:, None] == jnp.arange(item_rows.shape[0], dtype=jnp.int32)[None, :]
    codes = item_rows * caption_len + item_segments
    query_code = jnp.sum(jnp.where(member, codes[None, :], 0), axis=1)
    key_code = (jnp.arange(text, dtype=jnp.int32) // caption_len) * caption_len + caption_segments.reshape(-1)
    text_code = jnp.broadcast_to(key_code[None], (tiles, text))
    no_numbers = jnp.zeros((tiles,), jnp.int32)
    text_ends = (text, 0)

    near_unit, near_scale = normalise(near_tokens.astype(F32))
    near_low = (near_unit * attn_gain + attn_bias).astype(BF16)
    near_keys = matmul(near_low, key_weight).astype(BF16)
    near_values = matmul(near_low, value_weight).astype(BF16)
    self_att, self_lse = attend_forward(
        queries, near_keys, near_values, own_ids[:, None], windows[:, None, :], numbers, True, self_sizes, self_ends
    )
    after_one = inputs + matmul(self_att, output_weight)
    unit_two, scale_two = normalise(after_one)
    low_two = (unit_two * cross_gain + cross_bias).astype(BF16)
    cross_q = matmul(low_two, cross_query).astype(BF16)
    cross_att, cross_lse = cross_forward(
        cross_q, text_keys, text_values, query_code[:, None], key_code.reshape(-1, caption_len)
    )
    after_two = after_one + matmul(cross_att, cross_output)
    unit_three, scale_three = normalise(after_two)
    low_three = (unit_three * mlp_gain + mlp_bias).astype(BF16)
    width = tokens.shape[1]
    if count == 32:
        starts = jnp.sum((near_ids[None, :] < own_ids[:, None]).astype(jnp.int32), axis=1)
        sums, small, block_output, input_grad = layer_tail(
            Far(
                low_three=low_three, out_grad=out_grad, after_two=after_two,
                up_weight=up_weight, down_weight=down_weight,
                cross_att=cross_att, cross_q=cross_q, text_keys=text_keys, text_values=text_values,
                low_two=low_two, after_one=after_one, captions=caption_states,
                cross_output=cross_output, cross_key=cross_key, cross_value=cross_value, cross_query=cross_query,
                output_weight=output_weight,
                queries=queries, near_keys=near_keys, near_values=near_values, self_att=self_att,
                near_low=near_low, near_tokens=near_tokens,
                query_weight=query_weight, key_weight=key_weight, value_weight=value_weight,
            ),
            Near(
                starts=starts[None, :], self_lse=self_lse, query_code=query_code[None, :], key_code=key_code[:, None],
                cross_lse=cross_lse, gains=jnp.stack([attn_gain, cross_gain, mlp_gain]),
            ),
        )
        small = lax.dynamic_slice_in_dim(small, device * (width // count), width // count, 1)
    else:
        hidden_pre = matmul(low_three, up_weight)
        hidden, slope = gelu_and_slope(hidden_pre)
        hidden_low = hidden.astype(BF16)
        grad_pre = (slope * right_product(out_grad, down_weight)).astype(BF16)
        block_output = (after_two + matmul(hidden_low, down_weight)).astype(BF16)

        down_grad = left_product(hidden_low, out_grad).astype(BF16)
        up_grad = left_product(low_three, grad_pre).astype(BF16)
        z_, y_, x_, c_ = 0, 1, 2, 3
        one_way = (c_, x_, y_, z_) if len(factors(count)) == 4 else (0,)
        other_way = (c_, y_, x_, z_) if len(factors(count)) == 4 else (0,)
        grad_three = right_product(grad_pre, up_weight)
        mlp_gain_grad = jnp.sum(grad_three * unit_three, axis=0)
        mlp_bias_grad = jnp.sum(grad_three, axis=0)
        grad_two = out_grad.astype(F32) + norm_back(grad_three, unit_three, scale_three, mlp_gain)
        grad_two_low = grad_two.astype(BF16)

        cross_output_grad = left_product(cross_att, grad_two_low).astype(BF16)
        grad_cross = right_product(grad_two_low, cross_output).astype(BF16)
        grad_cq, grad_tk, grad_tv = attend_backward(
            cross_q, text_keys, text_values, grad_cross, cross_att, cross_lse,
            query_code[None, :], text_code[:, :, None], no_numbers, False, (text,), text_ends,
        )
        width = grad_tk.shape[1]
        cross_key_grad = left_product(caption_states, grad_tk).astype(BF16)
        cross_value_grad = left_product(caption_states, grad_tv).astype(BF16)
        caption_grad = (right_product(grad_tk, cross_key) + right_product(grad_tv, cross_value)).astype(BF16)
        cross_query_grad = left_product(low_two, grad_cq).astype(BF16)
        grad_norm_two = right_product(grad_cq, cross_query)
        cross_gain_grad = jnp.sum(grad_norm_two * unit_two, axis=0)
        cross_bias_grad = jnp.sum(grad_norm_two, axis=0)
        grad_one = grad_two + norm_back(grad_norm_two, unit_two, scale_two, cross_gain)
        grad_one_low = grad_one.astype(BF16)

        output_weight_grad = left_product(self_att, grad_one_low).astype(BF16)
        grad_self = right_product(grad_one_low, output_weight).astype(BF16)
        grad_q, grad_k, grad_v = attend_backward(
            queries, near_keys, near_values, grad_self, self_att, self_lse,
            own_ids[None, :], windows[:, :, None], numbers, True, self_sizes, self_ends,
        )
        grad_near = right_product(grad_k, key_weight) + right_product(grad_v, value_weight)
        grad_own = grad_near[REACH * rows :] + right_product(grad_q, query_weight)
        to_two = grad_near[:rows]
        to_one = grad_near[rows : REACH * rows].astype(BF16)
        from_swap = lax.ppermute(to_one, AXIS, swap).astype(F32)
        to_two = (to_two + jnp.where(odd, from_swap, 0.0)).astype(BF16)
        from_two = lax.ppermute(to_two, AXIS, behind).astype(F32)
        near_sum = jnp.concatenate([grad_near[: REACH * rows], grad_own], 0)
        attn_gain_grad = jnp.sum(near_sum * near_unit, axis=0)
        attn_bias_grad = jnp.sum(near_sum, axis=0)
        grad_norm_one = grad_own + from_two + jnp.where(odd, 0.0, from_swap)
        unit_one = near_unit[REACH * rows :]
        input_grad = grad_one + norm_back(grad_norm_one, unit_one, near_scale[REACH * rows :], attn_gain)
        query_grad = left_product(low_one, grad_q).astype(BF16)
        key_grad = left_product(near_low, grad_k).astype(BF16)
        value_grad = left_product(near_low, grad_v).astype(BF16)
        vectors = jnp.stack(
            [attn_gain_grad, attn_bias_grad, cross_gain_grad, cross_bias_grad, mlp_gain_grad, mlp_bias_grad]
        )
        grads = [
            down_grad, up_grad, cross_output_grad, cross_query_grad, cross_key_grad, cross_value_grad, output_weight_grad,
        ]
        sums = [
            reduce_scatter(grad, one_way if i % 2 else other_way, BF16, count)
            for i, grad in enumerate([*grads, query_grad, key_grad, value_grad, caption_grad])
        ]
        small = reduce_scatter(vectors.T, one_way, F32, count).T
        (down_out, up_out, cross_output_out, cross_query_out, cross_key_out, cross_value_out,
         output_out, query_out, key_out, value_out, caption_out) = sums
        sums = Sums(
            up=up_out, down=down_out, cross_output=cross_output_out, cross_key=cross_key_out,
            cross_value=cross_value_out, caption=caption_out, cross_query=cross_query_out, output=output_out,
            query=query_out, key=key_out, value=value_out,
        )
    return (
        block_output, input_grad, sums.caption,
        sums.query, sums.key, sums.value, sums.output,
        sums.cross_query, sums.cross_key, sums.cross_value, sums.cross_output,
        sums.up, sums.down,
        small[0], small[1], small[2], small[3], small[4], small[5],
    )


def solution(mesh):
    split = P(AXIS, None)
    return jax.shard_map(
        body,
        mesh=mesh,
        in_specs=(split, split) + (P(),) * 21,
        out_specs=(split,) * 13 + (P(AXIS),) * 6,
        check_vma=False,
    )
```

```python
import functools
from typing import Any, NamedTuple

import jax
import jax.numpy as jnp
from jax import lax
from jax.experimental import pallas as pl
from jax.experimental.pallas import tpu as pltpu
from jax.sharding import PartitionSpec as P

HEADS = 16
REACH = 2
EPS = 1e-05
NEG = -1e30
TILE = 256
LANES = 128
AXIS = "seq"
F32 = jnp.float32
BF16 = jnp.bfloat16

NT = (((1,), (1,)), ((), ()))
TN = (((0,), (0,)), ((), ()))


def head_lanes(value, half):
    lane = lax.broadcasted_iota(jnp.int32, value.shape, 1)
    keep = (lane < LANES // 2) if half == 0 else (lane >= LANES // 2)
    return jnp.where(keep, value, jnp.zeros_like(value))


def forward_kernel(causal, sizes, ends, n_ref, qid_ref, kid_ref, q_ref, k_ref, v_ref, o_ref, lse_ref, bias_ref):
    tile = pl.program_id(1)
    span = bias_ref.shape[2]

    @pl.when(pl.program_id(0) == 0)
    def _():
        last = ends[0] + tile * ends[1]
        kid = kid_ref[tile]
        qid = qid_ref[...]
        allowed = kid == qid
        if causal:
            kpos = lax.broadcasted_iota(jnp.int32, (TILE, span), 1)
            qpos = lax.broadcasted_iota(jnp.int32, (TILE, span), 0) + (span - TILE)
            allowed = allowed & (kpos <= qpos)
        bias_ref[tile] = jnp.where(allowed, 0.0, NEG)

    def run(size):
        start = pl.multiple_of(ends[0] + tile * ends[1] - size, TILE)
        keys = k_ref[pl.ds(start, size), :]
        values = v_ref[pl.ds(start, size), :]
        query = q_ref[...] * jnp.asarray(0.125, BF16)
        outs = []
        lses = []
        for half in range(2):
            scores = lax.dot_general(head_lanes(query, half), keys, NT, preferred_element_type=F32)
            scores = scores + bias_ref[tile, :, span - size :]
            row_max = jnp.max(scores, axis=1, keepdims=True)
            weights = jnp.exp(scores - row_max)
            summed = jnp.sum(weights, axis=1, keepdims=True)
            out = jnp.dot(weights.astype(BF16), values, preferred_element_type=F32)
            outs.append(out / summed)
            lses.append(row_max + jnp.log(summed))
        lane = lax.broadcasted_iota(jnp.int32, (TILE, LANES), 1)
        o_ref[...] = jnp.where(lane < LANES // 2, outs[0], outs[1]).astype(BF16)
        for half in range(2):
            lse_ref[0, half : half + 1, :] = jnp.transpose(jnp.broadcast_to(lses[half], (TILE, LANES)))[:1]

    if len(sizes) == 1:
        run(sizes[0])
    else:
        number = n_ref[tile]
        for size in sizes:
            pl.when(number == size // TILE)(functools.partial(run, size))


def attend_forward(queries, keys, values, qid, kid, numbers, causal, sizes, ends):
    rows, width = queries.shape
    tiles = rows // TILE
    pairs = width // LANES
    key_rows = keys.shape[0]
    span = max(sizes)
    flops = 4 * rows * span * width
    return pl.pallas_call(
        functools.partial(forward_kernel, causal, sizes, ends),
        grid_spec=pltpu.PrefetchScalarGridSpec(
            num_scalar_prefetch=1,
            grid=(pairs, tiles),
            in_specs=[
                pl.BlockSpec((TILE, 1), lambda h, t, n: (t, 0)),
                pl.BlockSpec((tiles, 1, span), lambda h, t, n: (0, 0, 0)),
                pl.BlockSpec((TILE, LANES), lambda h, t, n: (t, h)),
                pl.BlockSpec((key_rows, LANES), lambda h, t, n: (0, h)),
                pl.BlockSpec((key_rows, LANES), lambda h, t, n: (0, h)),
            ],
            out_specs=[
                pl.BlockSpec((TILE, LANES), lambda h, t, n: (t, h)),
                pl.BlockSpec((1, 2, TILE), lambda h, t, n: (h, 0, t)),
            ],
            scratch_shapes=[pltpu.VMEM((tiles, TILE, span), F32)],
        ),
        out_shape=[
            jax.ShapeDtypeStruct((rows, width), BF16),
            jax.ShapeDtypeStruct((pairs, 2, rows), F32),
        ],
        compiler_params=pltpu.CompilerParams(vmem_limit_bytes=24 << 20),
        cost_estimate=pl.CostEstimate(flops=4 * flops, bytes_accessed=8 << 20, transcendentals=rows * span * HEADS),
    )(numbers, qid, kid, queries, keys, values)


def caption_lanes(value, lines, length):
    return jnp.concatenate([value[r * length : (r + 1) * length] for r in range(lines)], 1)


def spread(value, in_row):
    return jnp.concatenate([jnp.where(mask, value, jnp.zeros_like(value)) for mask in in_row], 1)


def rows_of(code, lines, length):
    return [(code >= r * length) & (code < (r + 1) * length) for r in range(lines)]


def either(masks):
    result = masks[0]
    for mask in masks[1:]:
        result = result | mask
    return result


def cross_forward_kernel(code_ref, key_ref, q_ref, k_ref, v_ref, o_ref, lse_ref):
    lines, length = key_ref.shape
    keys = caption_lanes(k_ref[...], lines, length)
    values = caption_lanes(v_ref[...], lines, length)
    lane = lax.broadcasted_iota(jnp.int32, (TILE, LANES), 1)
    for tile in range(q_ref.shape[0] // TILE):
        mine = slice(tile * TILE, (tile + 1) * TILE)
        code = jnp.broadcast_to(code_ref[mine, :], (TILE, LANES))
        in_row = rows_of(code, lines, length)
        allowed = either([code[:, :length] == key_ref[r : r + 1, :] for r in range(lines)])
        query = q_ref[mine, :] * jnp.asarray(0.125, BF16)
        outs = []
        for half in range(2):
            scores = lax.dot_general(
                spread(head_lanes(query, half), in_row), keys, NT, preferred_element_type=F32
            )
            scores = jnp.where(allowed, scores, NEG)
            row_max = jnp.max(scores, axis=1, keepdims=True)
            weights = jnp.exp(scores - row_max)
            summed = jnp.sum(weights, axis=1, keepdims=True)
            wide = jnp.dot(weights.astype(BF16), values, preferred_element_type=F32)
            out = jnp.zeros((TILE, LANES), F32)
            for r in range(lines):
                out = jnp.where(in_row[r], wide[:, r * LANES : (r + 1) * LANES], out)
            outs.append(out / summed)
            lse = jnp.broadcast_to(row_max + jnp.log(summed), (TILE, LANES))
            lse_ref[0, half : half + 1, mine] = jnp.transpose(lse)[:1]
        o_ref[mine, :] = jnp.where(lane < LANES // 2, outs[0], outs[1]).astype(BF16)


def cross_forward(queries, keys, values, query_code, key_codes):
    rows, width = queries.shape
    pairs = width // LANES
    text = keys.shape[0]
    own = pl.BlockSpec((rows, LANES), lambda h: (0, h))
    wide = pl.BlockSpec((text, LANES), lambda h: (0, h))
    return pl.pallas_call(
        cross_forward_kernel,
        grid=(pairs,),
        in_specs=[
            pl.BlockSpec((rows, 1), lambda h: (0, 0)), pl.BlockSpec(key_codes.shape, lambda h: (0, 0)), own, wide, wide,
        ],
        out_specs=[own, pl.BlockSpec((1, 2, rows), lambda h: (h, 0, 0))],
        out_shape=[
            jax.ShapeDtypeStruct((rows, width), BF16),
            jax.ShapeDtypeStruct((pairs, 2, rows), F32),
        ],
        compiler_params=pltpu.CompilerParams(vmem_limit_bytes=16 << 20),
        cost_estimate=pl.CostEstimate(
            flops=4 * rows * text * width, bytes_accessed=4 << 20, transcendentals=rows * text * HEADS // 4
        ),
    )(query_code, key_codes, queries, keys, values)


def backward_kernel(
    causal, sizes, ends, n_ref, qid_ref, kid_ref, q_ref, k_ref, v_ref, g_ref, o_ref, lse_ref,
    dq_ref, dk_ref, dv_ref, bias_ref, dk_sum, dv_sum,
):
    tile = pl.program_id(1)
    tiles = pl.num_programs(1)
    span = bias_ref.shape[1]

    @pl.when(pl.program_id(0) == 0)
    def _():
        kid = kid_ref[tile]
        qid = qid_ref[...]
        allowed = kid == qid
        if causal:
            kpos = lax.broadcasted_iota(jnp.int32, (span, TILE), 0)
            qpos = lax.broadcasted_iota(jnp.int32, (span, TILE), 1) + (span - TILE)
            allowed = allowed & (kpos <= qpos)
        bias_ref[tile] = jnp.where(allowed, 0.0, NEG)

    @pl.when(tile == 0)
    def _():
        dk_sum[...] = jnp.zeros_like(dk_sum)
        dv_sum[...] = jnp.zeros_like(dv_sum)

    def run(size):
        start = pl.multiple_of(ends[0] + tile * ends[1] - size, TILE)
        window = pl.ds(start, size)
        keys = k_ref[window, :]
        values = v_ref[window, :]
        query = q_ref[...] * jnp.asarray(0.125, BF16)
        grad = g_ref[...]
        inner = grad.astype(F32) * o_ref[...].astype(F32)
        inner_rows = jnp.transpose(inner)
        half_lanes = LANES // 2
        parts_dq = []
        dk = None
        dv = None
        for half in range(2):
            head_q = head_lanes(query, half)
            head_g = head_lanes(grad, half)
            lse = lse_ref[0, half : half + 1, :]
            delta = jnp.sum(inner_rows[half * half_lanes : (half + 1) * half_lanes, :], axis=0, keepdims=True)
            scores = lax.dot_general(keys, head_q, NT, preferred_element_type=F32)
            probs = jnp.exp(scores + bias_ref[tile, span - size :, :] - lse)
            grad_probs = lax.dot_general(values, head_g, NT, preferred_element_type=F32)
            grad_scores = (probs * (grad_probs - delta)).astype(BF16)
            probs = probs.astype(BF16)
            part_k = jnp.dot(grad_scores, head_q, preferred_element_type=F32)
            part_v = jnp.dot(probs, head_g, preferred_element_type=F32)
            dk = part_k if dk is None else dk + part_k
            dv = part_v if dv is None else dv + part_v
            parts_dq.append(lax.dot_general(grad_scores, keys, TN, preferred_element_type=F32))
        lane = lax.broadcasted_iota(jnp.int32, (TILE, LANES), 1)
        dq_ref[...] = (jnp.where(lane < half_lanes, parts_dq[0], parts_dq[1]) * 0.125).astype(BF16)
        dk_sum[window, :] += dk
        dv_sum[window, :] += dv

    if len(sizes) == 1:
        run(sizes[0])
    else:
        number = n_ref[tile]
        for size in sizes:
            pl.when(number == size // TILE)(functools.partial(run, size))

    @pl.when(tile == tiles - 1)
    def _():
        dk_ref[...] = dk_sum[...].astype(BF16)
        dv_ref[...] = dv_sum[...].astype(BF16)


def attend_backward(queries, keys, values, grad, out, lse, qid, kid, numbers, causal, sizes, ends):
    rows, width = queries.shape
    tiles = rows // TILE
    pairs = width // LANES
    key_rows = keys.shape[0]
    span = max(sizes)
    flops = 10 * rows * span * width
    near = pl.BlockSpec((TILE, LANES), lambda h, t, n: (t, h))
    wide = pl.BlockSpec((key_rows, LANES), lambda h, t, n: (0, h))
    return pl.pallas_call(
        functools.partial(backward_kernel, causal, sizes, ends),
        grid_spec=pltpu.PrefetchScalarGridSpec(
            num_scalar_prefetch=1,
            grid=(pairs, tiles),
            in_specs=[
                pl.BlockSpec((1, TILE), lambda h, t, n: (0, t)),
                pl.BlockSpec((tiles, span, 1), lambda h, t, n: (0, 0, 0)),
                near,
                wide,
                wide,
                near,
                near,
                pl.BlockSpec((1, 2, TILE), lambda h, t, n: (h, 0, t)),
            ],
            out_specs=[near, wide, wide],
            scratch_shapes=[
                pltpu.VMEM((tiles, span, TILE), F32),
                pltpu.VMEM((key_rows, LANES), F32),
                pltpu.VMEM((key_rows, LANES), F32),
            ],
        ),
        out_shape=[
            jax.ShapeDtypeStruct((rows, width), BF16),
            jax.ShapeDtypeStruct((key_rows, width), BF16),
            jax.ShapeDtypeStruct((key_rows, width), BF16),
        ],
        compiler_params=pltpu.CompilerParams(vmem_limit_bytes=48 << 20),
        cost_estimate=pl.CostEstimate(flops=4 * flops, bytes_accessed=12 << 20, transcendentals=rows * span * HEADS),
    )(numbers, qid, kid, queries, keys, values, grad, out, lse)


def factors(count):
    return {32: (4, 2, 2, 2), 128: (4, 4, 4, 2)}.get(count, (count,))


def coordinates(count):
    sizes = factors(count)
    left = lax.axis_index(AXIS)
    places = []
    for size in reversed(sizes):
        places.insert(0, lax.rem(left, size))
        left = lax.div(left, size)
    return places


def peers_along(count, axis, step):
    sizes = factors(count)
    stride = 1
    for size in sizes[axis + 1 :]:
        stride *= size
    size = sizes[axis]
    pairs = []
    for device in range(count):
        place = (device // stride) % size
        pairs.append((device, device + ((place + step) % size - place) * stride))
    return pairs


def take(value, place, axis):
    return lax.dynamic_slice_in_dim(value, place, 1, axis)


def total(terms):
    summed = terms[0].astype(F32)
    for term in terms[1:]:
        summed = summed + term.astype(F32)
    return summed


def reduce_scatter(value, order, kind, count):
    sizes = factors(count)
    places = coordinates(count)
    rows, width = value.shape
    terms = [value.reshape(*sizes, rows // count, width)]
    for axis in order:
        size = sizes[axis]
        arrived = []
        for step in range(1, size):
            other = lax.rem(places[axis] + step, size)
            sent = total([take(term, other, axis) for term in terms]).astype(kind)
            arrived.append(lax.ppermute(sent, AXIS, peers_along(count, axis, step)))
        terms = [take(term, places[axis], axis) for term in terms] + arrived
    return total(terms).reshape(rows // count, width)


def all_gather(value, order, count):
    sizes = factors(count)
    places = coordinates(count)
    rows, width = value.shape
    held = value.reshape(*([1] * len(sizes)), rows, width)
    for axis in order:
        size = sizes[axis]
        shape = list(held.shape)
        shape[axis] = size
        gathered = lax.dynamic_update_slice_in_dim(jnp.zeros(shape, held.dtype), held, places[axis], axis)
        for step in range(1, size):
            arrived = lax.ppermute(held, AXIS, peers_along(count, axis, step))
            source = lax.rem(places[axis] + size - step, size)
            gathered = lax.dynamic_update_slice_in_dim(gathered, arrived, source, axis)
        held = gathered
    return held.reshape(rows * count, width)


MESH = pl.DeviceIdType.MESH
BLOCK = 32
WIDE = 1024


def places32():
    me = lax.axis_index(AXIS)
    core = lax.rem(me, 2)
    x = lax.rem(lax.div(me, 2), 2)
    y = lax.rem(lax.div(me, 4), 2)
    z = lax.div(me, 8)
    return me, core, x, y, z


GELU_A = 0.7978845608028654
GELU_B = 0.044715


def gelu_and_slope(value):
    square = value * value
    bend = jnp.tanh(GELU_A * (value + GELU_B * value * square))
    gate = 0.5 * (1.0 + bend)
    slope = gate + value * 0.5 * (1.0 - bend * bend) * (GELU_A * (1.0 + 3.0 * GELU_B * square))
    return value * gate, slope


def normalise_rows(value):
    mean = jnp.mean(value, axis=-1, keepdims=True)
    centred = value - mean
    scale = lax.rsqrt(jnp.mean(centred * centred, axis=-1, keepdims=True) + EPS)
    return centred * scale, scale


class Far(NamedTuple):
    low_three: Any
    out_grad: Any
    after_two: Any
    up_weight: Any
    down_weight: Any
    cross_att: Any
    cross_q: Any
    text_keys: Any
    text_values: Any
    low_two: Any
    after_one: Any
    captions: Any
    cross_output: Any
    cross_key: Any
    cross_value: Any
    cross_query: Any
    output_weight: Any
    queries: Any
    near_keys: Any
    near_values: Any
    self_att: Any
    near_low: Any
    near_tokens: Any
    query_weight: Any
    key_weight: Any
    value_weight: Any


class Near(NamedTuple):
    starts: Any
    self_lse: Any
    query_code: Any
    key_code: Any
    cross_lse: Any
    gains: Any


class Sums(NamedTuple):
    up: Any
    down: Any
    cross_output: Any
    cross_key: Any
    cross_value: Any
    caption: Any
    cross_query: Any
    output: Any
    query: Any
    key: Any
    value: Any


class Scratch(NamedTuple):
    arena: Any
    sums: Any
    accum_k: Any
    accum_v: Any
    back_one: Any
    back_two: Any
    vec: Any
    vec_in: Any
    tiles: Any
    r0: Any
    r1: Any
    r2: Any
    r3: Any
    load: Any
    s0: Any
    d0: Any
    s1: Any
    d1: Any
    s2: Any
    d2: Any
    s3: Any
    d3: Any
    vs: Any
    vd: Any
    bs: Any
    bd: Any
    credit: Any


UP, DOWN, CROSS_OUTPUT, CROSS_KEY, CROSS_VALUE, CAPTION, CROSS_QUERY, OUTPUT, QUERY, KEY, VALUE = range(11)
PIECES = (
    (UP, 0), (UP, 1), (UP, 2), (UP, 3), (DOWN, 0), (DOWN, 1), (DOWN, 2), (DOWN, 3),
    (CROSS_OUTPUT, 0), (CROSS_KEY, 0), (CROSS_VALUE, 0), (CAPTION, 0), (CROSS_QUERY, 0), (OUTPUT, 0),
    (QUERY, 0), (KEY, 0), (VALUE, 0),
)
PLAN = (
    (), (), (), (), ((2, 0),), (), ((2, 1),), ((2, 2),), (), ((2, 3),), (), (), (), ((3, 0), (2, 4)), (), (), (),
    (), ((3, 1),), (), (), (), ((2, 5),), (), (), (), (), ((3, 2), (2, 6)), (), (), (), ((3, 3),), (), ((2, 7),),
    (), (), ((3, 4), (2, 8)), ((3, 6), (3, 5)), ((1, 13),), ((3, 7),), (), ((2, 9),), (), (), ((2, 10),), (), (),
    ((2, 11),), (), ((3, 8), (2, 12)), (), (), ((3, 9),), (), ((2, 13), (3, 11)), ((3, 10),), ((3, 12),), (),
    ((2, 14),), ((3, 13),),
)
LANDINGS = 9
SLOTS = 2
HALF = LANES // 2
STEP = 64
LOADS = 48


def layer_kernel(rows, *refs):
    total = len(PIECES)
    n_far, n_near, n_sums = len(Far._fields), len(Near._fields), len(Sums._fields)
    far = Far(*refs[:n_far])
    near = Near(*refs[n_far : n_far + n_near])
    refs = refs[n_far + n_near :]
    outs = Sums(*refs[:n_sums])
    vec_out, block_output, input_grad = refs[n_sums : n_sums + 3]
    held = Scratch(*refs[n_sums + 3 :])
    (arena, sums, accum_k, accum_v, back_one, back_two, vec, vec_in, tiles, r0, r1, r2, r3,
     load, s0, d0, s1, d1, s2, d2, s3, d3, vs, vd, bs, bd, credit) = held

    me, core, x, y, z = places32()
    sibling = me + 1 - 2 * core
    x_peer = me + 2 - 4 * x
    y_peer = me + 4 - 8 * y
    z_other = [lax.rem(z + m, 4) for m in range(1, 4)]
    z_peers = [me + 8 * (o - z) for o in z_other]
    has_before = me >= 2
    has_after = me < 30

    barrier = pltpu.get_barrier_semaphore()
    for peer in (sibling, x_peer, y_peer, *z_peers):
        pl.semaphore_signal(barrier, inc=1, device_id=(peer,), device_id_type=MESH)

    @pl.when(has_before)
    def _():
        pl.semaphore_signal(barrier, inc=1, device_id=(me - 2,), device_id_type=MESH)

    @pl.when(has_after)
    def _():
        pl.semaphore_signal(barrier, inc=1, device_id=(me + 2,), device_id_type=MESH)

    numbers = iter(range(LOADS))

    def fetch(source, slot):
        return start_copy(source, arena.at[pl.ds(slot * rows, source.shape[0])])

    def start_copy(source, target):
        copy = pltpu.make_async_copy(source, target, load.at[next(numbers)])
        copy.start()
        return copy

    def at(slot, count=1):
        return pl.ds(slot * rows, count * rows)

    def up_part(part):
        return far.up_weight.at[:, pl.ds(part * WIDE, WIDE)]

    def down_part(part):
        return far.down_weight.at[pl.ds(part * WIDE, WIDE)]

    ONE, TWO, THREE = 12, 14, 10
    low_three_load = fetch(far.low_three, 8)
    up_loads = [fetch(up_part(0), THREE)]
    out_grad_load = fetch(far.out_grad, 9)
    down_loads = [fetch(down_part(0), ONE)]
    up_loads.append(fetch(up_part(1), TWO))
    after_load = start_copy(far.after_two, sums.at[2])

    pl.semaphore_wait(barrier, 6 + jnp.where(has_before, 1, 0) + jnp.where(has_after, 1, 0))

    def remote(src, dst, send, recv, peer):
        return pltpu.make_async_remote_copy(
            src_ref=src, dst_ref=dst, send_sem=send, recv_sem=recv, device_id=(peer,), device_id_type=MESH
        )

    def along(c):
        even = lax.rem(c, 2) == 0
        return (
            jnp.where(even, x, y),
            jnp.where(even, x_peer, y_peer),
            jnp.where(even, y, x),
            jnp.where(even, y_peer, x_peer),
        )

    def add_blocks(count, dst, src):
        @pl.loop(0, count, unroll=4)
        def _(i):
            dst(i)[...] = dst(i)[...] + src(i)[...]

    def take_credit(c):
        if c >= LANDINGS:
            pl.semaphore_wait(credit, 1)

    def give(c):
        take_credit(c)
        remote(tiles.at[c % SLOTS, 1 - core], r0.at[c % LANDINGS], s0.at[c], d0.at[c], sibling).start()

    def make(c, left_at, right_at, depth):
        @pl.loop(0, 4)
        def _(zz):
            left = arena[pl.ds(left_at * rows, depth), pl.ds(pl.multiple_of(zz * TILE, TILE), TILE)]
            for part in range(2):
                cols = slice(part * (WIDE // 2), (part + 1) * (WIDE // 2))
                result = lax.dot_general(
                    left, arena[pl.ds(right_at * rows, depth), cols], TN, preferred_element_type=F32
                ).astype(BF16)
                for block in range(8):
                    yy, xx, cc = block // 4, (block // 2) % 2, block % 2
                    f, s = (xx, yy) if c % 2 == 0 else (yy, xx)
                    tiles[c % SLOTS, cc, f, s, zz, :, cols] = result[block * BLOCK : (block + 1) * BLOCK]

        give(c)

    def make_down(c, part):
        @pl.loop(0, 4)
        def _(zz):
            for quarter in range(4):
                yy, xx = quarter // 2, quarter % 2
                f, s = (xx, yy) if c % 2 == 0 else (yy, xx)
                left = arena[
                    pl.ds(pl.multiple_of(zz * rows, rows), rows), quarter * TILE : (quarter + 1) * TILE
                ]
                result = lax.dot_general(
                    left, arena[at(9), part * TILE : (part + 1) * TILE], TN, preferred_element_type=F32
                ).astype(BF16)
                for cc in range(2):
                    for group in range(4):
                        top = cc * 128 + group * BLOCK
                        tiles[c % SLOTS, cc, f, s, zz, :, group * TILE : (group + 1) * TILE] = result[top : top + BLOCK]

        give(c)

    def first(c):
        f, fp, _, _ = along(c)
        slot, place = c % SLOTS, c % LANDINGS
        copy = remote(tiles.at[slot, 1 - core], r0.at[place], s0.at[c], d0.at[c], sibling)
        copy.wait_recv()
        add_blocks(
            16,
            lambda i: r0.at[place, i // 8, (i // 4) % 2, i % 4],
            lambda i: tiles.at[slot, core, i // 8, (i // 4) % 2, i % 4],
        )
        remote(r0.at[place, 1 - f], r1.at[c], s1.at[c], d1.at[c], fp).start()
        copy.wait_send()

    def second(c):
        f, fp, s, sp = along(c)
        place = c % LANDINGS
        copy = remote(r0.at[place, 1 - f], r1.at[c], s1.at[c], d1.at[c], fp)
        copy.wait_recv()
        add_blocks(8, lambda i: r1.at[c, i // 4, i % 4], lambda i: r0.at[place, f, i // 4, i % 4])
        remote(r1.at[c, 1 - s], r2.at[c], s2.at[c], d2.at[c], sp).start()
        copy.wait_send()
        if c < total - LANDINGS:
            pl.semaphore_signal(credit, inc=1, device_id=(sibling,), device_id_type=MESH)

    def third(c):
        _, _, s, sp = along(c)
        copy = remote(r1.at[c, 1 - s], r2.at[c], s2.at[c], d2.at[c], sp)
        copy.wait_recv()
        add_blocks(4, lambda i: r2.at[c, i], lambda i: r1.at[c, s, i])
        for m in range(3):
            remote(r2.at[c, z_other[m]], r3.at[c, m], s3.at[c, m], d3.at[c, m], z_peers[m]).start()
        copy.wait_send()

    def last(c):
        number, part = PIECES[c]
        for m in range(3):
            remote(r2.at[c, z_other[m]], r3.at[c, m], s3.at[c, m], d3.at[c, m], z_peers[m]).wait()
        summed = r2[c, z].astype(F32) + r3[c, 0].astype(F32) + r3[c, 1].astype(F32) + r3[c, 2].astype(F32)
        out = outs[number]
        if number == DOWN:
            for group in range(4):
                out[group * BLOCK : (group + 1) * BLOCK, part * TILE : (part + 1) * TILE] = summed[
                    :, group * TILE : (group + 1) * TILE
                ]
        else:
            out[:, part * WIDE : (part + 1) * WIDE] = summed[: out.shape[0]]

    def each_tile(run):
        @pl.loop(0, WIDE // TILE, unroll=2)
        def _(n):
            run(pl.multiple_of(n * TILE, TILE))

    def product(pairs, add=False):
        def run(n):
            result = None
            for slot, weight in pairs:
                term = lax.dot_general(
                    arena[at(slot), :], arena[pl.ds(weight * rows + n, TILE), :], NT, preferred_element_type=F32
                )
                result = term if result is None else result + term
            if add:
                result += sums[0, :, pl.ds(n, TILE)]
            sums[0, :, pl.ds(n, TILE)] = result

        each_tile(run)

    def plain_product(slot, weight, add):
        def run(n):
            result = jnp.dot(arena[at(slot), :], arena[at(weight, 2), pl.ds(n, TILE)], preferred_element_type=F32)
            if add:
                result += sums[0, :, pl.ds(n, TILE)]
            sums[0, :, pl.ds(n, TILE)] = result

        each_tile(run)

    def low_product(slot, weight, target):
        def run(n):
            result = lax.dot_general(
                arena[at(slot), :], arena[pl.ds(weight * rows + n, TILE), :], NT, preferred_element_type=F32
            )
            arena[at(target), pl.ds(n, TILE)] = result.astype(BF16)

        each_tile(run)

    def each_step(run):
        @pl.loop(0, rows // STEP)
        def _(i):
            run(pl.multiple_of(i * STEP, STEP))

    vec[...] = jnp.zeros_like(vec)

    def add_gains(row, grad, unit):
        vec[row : row + 1] += jnp.sum(grad * unit, axis=0, keepdims=True)
        vec[row + 1 : row + 2] += jnp.sum(grad, axis=0, keepdims=True)

    def norm_back_rows(grad, unit, scale, gain):
        scaled = grad * gain
        return scale * (
            scaled - jnp.mean(scaled, axis=-1, keepdims=True) - unit * jnp.mean(scaled * unit, axis=-1, keepdims=True)
        )

    def attend_step(keys, values, query, grad, out, lse, allowed):
        query = query * jnp.asarray(0.125, BF16)
        inner = jnp.transpose(grad.astype(F32) * out.astype(F32))
        turned_keys = jnp.transpose(keys)
        parts = []
        dk = None
        dv = None
        for half in range(2):
            head_q = head_lanes(query, half)
            head_g = head_lanes(grad, half)
            delta = jnp.sum(inner[half * HALF : (half + 1) * HALF], axis=0, keepdims=True)
            scores = lax.dot_general(keys, head_q, NT, preferred_element_type=F32)
            probs = jnp.exp(jnp.where(allowed, scores - lse[half], NEG))
            grad_probs = lax.dot_general(values, head_g, NT, preferred_element_type=F32)
            grad_scores = (probs * (grad_probs - delta)).astype(BF16)
            part_k = jnp.dot(grad_scores, head_q, preferred_element_type=F32)
            part_v = jnp.dot(probs.astype(BF16), head_g, preferred_element_type=F32)
            dk = part_k if dk is None else dk + part_k
            dv = part_v if dv is None else dv + part_v
            parts.append(jnp.dot(turned_keys, grad_scores, preferred_element_type=F32))
        dq = jnp.concatenate([parts[0][:HALF], parts[1][HALF:]], 0)
        return (jnp.transpose(dq) * 0.125).astype(BF16), dk, dv

    position = [0]

    def take_steps(steps):
        for kind, c in steps:
            (first, second, third)[kind - 1](c)

    def tick():
        take_steps(PLAN[position[0]])
        position[0] += 1

    def loop_tick(base, i):
        for number, steps in enumerate(PLAN[base : base + 16]):
            if steps:
                pl.when(i == number)(functools.partial(take_steps, steps))

    def activate(part, up_at, down_at):
        def run(n):
            cols = pl.ds(n, TILE)
            pre = jnp.dot(arena[at(8), :], arena[at(up_at, 2), cols], preferred_element_type=F32)
            grad = lax.dot_general(
                arena[at(9), :], arena[pl.ds(down_at * rows + n, TILE), :], NT, preferred_element_type=F32
            )
            hidden, slope = gelu_and_slope(pre)
            arena[at(part), cols] = hidden.astype(BF16)
            arena[at(4 + part), cols] = (slope * grad).astype(BF16)

        each_tile(run)

    low_three_load.wait()
    out_grad_load.wait()
    places = ((THREE, ONE), (TWO, THREE), (ONE, TWO), (THREE, ONE))
    for part in range(4):
        up_loads[part].wait()
        down_loads[part].wait()
        activate(part, *places[part])
        if part == 0:
            down_loads.append(fetch(down_part(1), THREE))
            up_loads.append(fetch(up_part(2), ONE))
        if part == 1:
            down_loads.append(fetch(down_part(2), TWO))
            up_loads.append(fetch(up_part(3), THREE))
        if part == 2:
            down_loads.append(fetch(down_part(3), ONE))
            weight_two = fetch(up_part(1), TWO)
        if part == 3:
            weight_one = fetch(up_part(0), ONE)
        make(part, 8, 4 + part, rows)
        if part > 0:
            first(part - 1)
        tick()
    places = (ONE, TWO, THREE, ONE)
    loads = [weight_one, weight_two, fetch(up_part(2), THREE)]
    for part in range(4):
        make_down(4 + part, part)
        loads[part].wait()
        product([(4 + part, places[part])], add=part > 0)
        if part == 0:
            loads.append(fetch(up_part(3), ONE))
        first(3 + part)
        tick()
    weight_two = fetch(far.cross_output, TWO)
    weight_three = fetch(down_part(0), THREE)
    weight_one = fetch(down_part(1), ONE)
    low_two_load = fetch(far.low_two, 4)
    captions_load = fetch(far.captions, 5)
    cross_att_load = fetch(far.cross_att, 6)
    cross_q_load = fetch(far.cross_q, 7)
    after_load.wait()
    gains = near.gains

    def norm_three(n):
        here = pl.ds(n, STEP)
        unit, scale = normalise_rows(sums[2, here, :])
        grad = sums[0, here, :]
        add_gains(4, grad, unit)
        value = arena[pl.ds(9 * rows + n, STEP), :].astype(F32) + norm_back_rows(grad, unit, scale, gains[2:3])
        sums[1, here, :] = value
        arena[pl.ds(9 * rows + n, STEP), :] = value.astype(BF16)

    each_step(norm_three)
    first(7)
    tick()

    weight_two.wait()
    low_product(9, TWO, 8)
    weight_two = fetch(down_part(2), TWO)
    cross_att_load.wait()
    make(8, 6, 9, rows)
    tick()
    weight_three.wait()
    plain_product(0, THREE, False)
    weight_three = fetch(down_part(3), THREE)
    tick()
    weight_one.wait()
    plain_product(1, ONE, True)
    weight_one = fetch(far.cross_key, ONE)
    first(8)
    tick()
    weight_two.wait()
    plain_product(2, TWO, True)
    weight_two = fetch(far.cross_value, TWO)
    keys_load = fetch(far.text_keys, 2)
    tick()
    weight_three.wait()
    plain_product(3, THREE, True)
    weight_three = fetch(far.cross_query, THREE)
    values_load = fetch(far.text_values, 3)
    tick()

    def finish_block(n):
        here = pl.ds(n, STEP)
        arena[pl.ds(n, STEP), :] = (sums[2, here, :] + sums[0, here, :]).astype(BF16)

    each_step(finish_block)
    tick()
    loop_base = position[0]
    position[0] += 16
    block_copy = start_copy(arena.at[at(0)], block_output)
    after_load = start_copy(far.after_one, sums.at[2])

    text = far.text_keys.shape[0]
    cross_q_load.wait()
    keys_load.wait()
    values_load.wait()

    @pl.loop(0, 16)
    def _(i):
        h, t = lax.div(i, 2), lax.rem(i, 2)
        lanes = pl.ds(pl.multiple_of(h * LANES, LANES), LANES)
        own = pl.multiple_of(t * TILE, TILE)
        mine = pl.ds(7 * rows + own, TILE)
        allowed = near.key_code[...] == near.query_code[:, pl.ds(own, TILE)]
        lse = [near.cross_lse[h, half : half + 1, pl.ds(own, TILE)] for half in range(2)]
        dq, dk, dv = attend_step(
            arena[at(2), lanes], arena[at(3), lanes], arena[mine, lanes],
            arena[pl.ds(8 * rows + own, TILE), lanes], arena[pl.ds(6 * rows + own, TILE), lanes], lse, allowed,
        )
        arena[mine, lanes] = dq

        @pl.when(t == 0)
        def _():
            accum_k[:text] = dk
            accum_v[:text] = dv

        @pl.when(t == 1)
        def _():
            arena[at(2), lanes] = (accum_k[:text] + dk).astype(BF16)
            arena[at(3), lanes] = (accum_v[:text] + dv).astype(BF16)

        loop_tick(loop_base, i)

    block_copy.wait()
    self_att_load = fetch(far.self_att, 8)
    captions_load.wait()
    make(9, 5, 2, rows)
    tick()
    weight_one.wait()
    weight_two.wait()
    product([(2, ONE), (3, TWO)])
    weight_one = fetch(far.output_weight, ONE)
    make(10, 5, 3, rows)
    first(9)
    tick()

    c = 11
    for zz in range(4):
        for block in range(8):
            yy, xx, cc = block // 4, (block // 2) % 2, block % 2
            f, s = (xx, yy) if c % 2 == 0 else (yy, xx)
            top = (zz * 8 + block) * 16
            tiles[c % SLOTS, cc, f, s, zz, :16, :] = sums[0, top : top + 16, :].astype(BF16)
            tiles[c % SLOTS, cc, f, s, zz, 16:, :] = jnp.zeros((16, WIDE), BF16)
    give(c)
    tick()
    keys_load = fetch(far.near_keys, 1)
    weight_three.wait()
    product([(7, THREE)])
    near_low_load = fetch(far.near_low, 9)
    first(10)
    tick()
    low_two_load.wait()
    make(12, 4, 7, rows)
    values_load = fetch(far.near_values, 4)
    queries_load = fetch(far.queries, 0)
    first(11)
    tick()
    after_load.wait()

    def norm_two(n):
        here = pl.ds(n, STEP)
        unit, scale = normalise_rows(sums[2, here, :])
        grad = sums[0, here, :]
        add_gains(2, grad, unit)
        value = sums[1, here, :] + norm_back_rows(grad, unit, scale, gains[1:2])
        sums[1, here, :] = value
        arena[pl.ds(14 * rows + n, STEP), :] = value.astype(BF16)

    each_step(norm_two)
    first(12)
    tick()

    weight_one.wait()
    low_product(14, ONE, 7)
    weight_one = fetch(far.value_weight, ONE)
    self_att_load.wait()
    make(13, 8, 14, rows)
    tick()
    loop_base = position[0]
    position[0] += 16
    weight_two = fetch(far.key_weight, TWO)
    queries_load.wait()
    keys_load.wait()
    values_load.wait()

    span = 2 * rows + TILE

    @pl.loop(0, 16)
    def _(i):
        h, t = lax.div(i, 2), lax.rem(i, 2)
        lanes = pl.ds(pl.multiple_of(h * LANES, LANES), LANES)
        own = pl.multiple_of(t * TILE, TILE)
        mine = pl.ds(own, TILE)
        kpos = lax.broadcasted_iota(jnp.int32, (span, TILE), 0)
        qpos = lax.broadcasted_iota(jnp.int32, (TILE, TILE), 1)
        dpos = lax.broadcasted_iota(jnp.int32, (TILE, TILE), 0)
        allowed = kpos >= near.starts[:, mine] - own
        allowed = jnp.concatenate([allowed[: span - TILE], allowed[span - TILE :] & (dpos <= qpos)], 0)
        lse = [near.self_lse[h, half : half + 1, mine] for half in range(2)]
        dq, dk, dv = attend_step(
            arena[pl.ds(rows + own, span), lanes], arena[pl.ds(4 * rows + own, span), lanes], arena[mine, lanes],
            arena[pl.ds(7 * rows + own, TILE), lanes], arena[pl.ds(8 * rows + own, TILE), lanes], lse, allowed,
        )
        arena[mine, lanes] = dq

        @pl.when(t == 0)
        def _():
            accum_k[:span] = dk
            accum_v[:span] = dv

        @pl.when(t == 1)
        def _():
            for target, accum, part in ((1, accum_k, dk), (4, accum_v, dv)):
                arena[pl.ds(target * rows, TILE), lanes] = accum[:TILE].astype(BF16)
                arena[pl.ds(target * rows + TILE, span - TILE), lanes] = (accum[TILE:span] + part[: span - TILE]).astype(BF16)
                arena[pl.ds(target * rows + span, TILE), lanes] = part[span - TILE :].astype(BF16)

        loop_tick(loop_base, i)

    near_low_load.wait()
    make(14, 11, 0, rows)
    weight_two.wait()
    weight_one.wait()
    product([(2, TWO), (5, ONE)])

    def as_low(slot, extra):
        def run(n):
            value = sums[0, pl.ds(n, STEP), :]
            if extra is not None:
                value = value + jnp.where(core == 1, extra[pl.ds(n, STEP), :].astype(F32), 0.0)
            arena[pl.ds(slot * rows + n, STEP), :] = value.astype(BF16)

        each_step(run)

    as_low(7, None)
    swap = remote(arena.at[at(7)], back_one, bs.at[0], bd.at[0], sibling)
    swap.start()
    first(14)
    tick()
    product([(1, TWO), (4, ONE)])
    swap.wait()
    as_low(8, back_one)
    send_back = remote(arena.at[at(8)], back_two, bs.at[1], bd.at[1], me - 2)

    @pl.when(has_before)
    def _():
        send_back.start()

    tick()
    make(15, 9, 1, 3 * rows)
    tick()
    query_weight_load = fetch(far.query_weight, 1)
    make(16, 9, 4, 3 * rows)
    token_load = fetch(far.near_tokens, 9)
    first(15)
    tick()

    def block_gains(slot, grad_slot, factor):
        def run(n):
            unit, _ = normalise_rows(arena[pl.ds(slot * rows + n, STEP), :].astype(F32))
            if grad_slot is None:
                grad = sums[0, pl.ds(n, STEP), :]
            else:
                grad = arena[pl.ds(grad_slot * rows + n, STEP), :].astype(F32)
            if factor is not None:
                grad = grad * factor
            add_gains(0, grad, unit)

        each_step(run)

    token_load.wait()
    block_gains(9, 8, None)
    block_gains(10, 7, jnp.where(core == 1, 1.0, 0.0))
    first(16)
    tick()
    query_weight_load.wait()
    product([(0, 1), (3, TWO), (6, ONE)])
    tick()
    block_gains(11, None, None)

    def vec_step(number, peer):
        step = remote(vec, vec_in.at[number], vs.at[number], vd.at[number], peer)
        step.start()
        return step

    def norm_one(n):
        here = pl.ds(n, STEP)
        unit, scale = normalise_rows(arena[pl.ds(11 * rows + n, STEP), :].astype(F32))
        grad = sums[0, here, :]
        grad = grad + jnp.where(core == 0, back_one[here, :].astype(F32), 0.0)
        grad = grad + jnp.where(has_after, back_two[here, :].astype(F32), 0.0)
        sums[1, here, :] += norm_back_rows(grad, unit, scale, gains[0:1])

    step = vec_step(0, sibling)
    step.wait()
    vec[...] += vec_in[0]
    step = vec_step(1, x_peer)
    second(15)

    @pl.when(has_before)
    def _():
        send_back.wait_send()

    @pl.when(has_after)
    def _():
        send_back.wait_recv()

    each_step(norm_one)
    out_copy = start_copy(sums.at[1], input_grad)
    step.wait()
    vec[...] += vec_in[1]
    step = vec_step(2, y_peer)
    third(14)
    second(16)
    step.wait()
    vec[...] += vec_in[2]
    steps = [vec_step(3 + m, z_peers[m]) for m in range(3)]
    for c in range(total - 3):
        last(c)
    third(15)
    third(16)
    for step in steps:
        step.wait()
    vec_out[...] = vec[...] + vec_in[3] + vec_in[4] + vec_in[5]
    for c in range(total - 3, total):
        last(c)
    out_copy.wait()


def copy_kernel(number, *refs):
    sources, targets, staged = refs[:number], refs[number : 2 * number], refs[2 * number : 3 * number]
    sem_in, sem_out = refs[3 * number :]
    inward = [pltpu.make_async_copy(sources[i], staged[i], sem_in.at[i]) for i in range(number)]
    outward = [pltpu.make_async_copy(staged[i], targets[i], sem_out.at[i]) for i in range(number)]
    for copy in inward:
        copy.start()
    for i in range(number):
        inward[i].wait()
        outward[i].start()
    for copy in outward:
        copy.wait()


def copy_all(arrays):
    anywhere = pl.BlockSpec(memory_space=pl.ANY)
    return pl.pallas_call(
        functools.partial(copy_kernel, len(arrays)),
        in_specs=[anywhere] * len(arrays),
        out_specs=[anywhere] * len(arrays),
        out_shape=[jax.ShapeDtypeStruct(array.shape, array.dtype) for array in arrays],
        scratch_shapes=[pltpu.VMEM(array.shape, array.dtype) for array in arrays]
        + [pltpu.SemaphoreType.DMA((len(arrays),))] * 2,
        cost_estimate=pl.CostEstimate(flops=0, bytes_accessed=12 << 20, transcendentals=0),
    )(*arrays)


def layer_tail(far, near):
    rows, width = far.queries.shape
    count = 32
    sizes = {UP: (BLOCK, 4 * WIDE), DOWN: (4 * BLOCK, WIDE), CAPTION: (far.captions.shape[0] // count, WIDE)}
    total = len(PIECES)
    local = pl.BlockSpec(memory_space=pltpu.VMEM)
    anywhere = pl.BlockSpec(memory_space=pl.ANY)
    dma = pltpu.SemaphoreType.DMA
    scratch = Scratch(
        arena=pltpu.VMEM((16 * rows, width), BF16),
        sums=pltpu.VMEM((3, rows, width), F32),
        accum_k=pltpu.VMEM((3 * rows, LANES), F32),
        accum_v=pltpu.VMEM((3 * rows, LANES), F32),
        back_one=pltpu.VMEM((rows, width), BF16),
        back_two=pltpu.VMEM((rows, width), BF16),
        vec=pltpu.VMEM((8, width), F32),
        vec_in=pltpu.VMEM((6, 8, width), F32),
        tiles=pltpu.VMEM((SLOTS, 2, 2, 2, 4, BLOCK, WIDE), BF16),
        r0=pltpu.VMEM((LANDINGS, 2, 2, 4, BLOCK, WIDE), BF16),
        r1=pltpu.VMEM((total, 2, 4, BLOCK, WIDE), BF16),
        r2=pltpu.VMEM((total, 4, BLOCK, WIDE), BF16),
        r3=pltpu.VMEM((total, 3, BLOCK, WIDE), BF16),
        load=dma((LOADS,)), s0=dma((total,)), d0=dma((total,)), s1=dma((total,)), d1=dma((total,)),
        s2=dma((total,)), d2=dma((total,)), s3=dma((total, 3)), d3=dma((total, 3)), vs=dma((6,)), vd=dma((6,)),
        bs=dma((2,)), bd=dma((2,)), credit=pltpu.SemaphoreType.REGULAR,
    )
    results = pl.pallas_call(
        functools.partial(layer_kernel, rows),
        in_specs=[anywhere] * len(far) + [local] * len(near),
        out_specs=[local] * (len(Sums._fields) + 1) + [anywhere] * 2,
        out_shape=[jax.ShapeDtypeStruct(sizes.get(number, (BLOCK, WIDE)), F32) for number in range(len(Sums._fields))]
        + [
            jax.ShapeDtypeStruct((8, width), F32),
            jax.ShapeDtypeStruct((rows, width), BF16),
            jax.ShapeDtypeStruct((rows, width), F32),
        ],
        scratch_shapes=list(scratch),
        compiler_params=pltpu.CompilerParams(collective_id=0, has_side_effects=True, vmem_limit_bytes=63 << 20),
        cost_estimate=pl.CostEstimate(flops=1 << 34, bytes_accessed=64 << 20, transcendentals=0),
    )(*far, *near)
    small = results[len(Sums._fields)]
    copied = copy_all([*results[: len(Sums._fields)], *results[len(Sums._fields) + 1 :]])
    return Sums(*copied[:-2]), small, *copied[-2:]


def matmul(left, right):
    return jnp.dot(left, right, preferred_element_type=F32)


def left_product(left, right):
    return lax.dot_general(left, right, TN, preferred_element_type=F32)


def right_product(left, right):
    return lax.dot_general(left, right, NT, preferred_element_type=F32)


def normalise(value):
    mean = jnp.mean(value, axis=-1, keepdims=True)
    centred = value - mean
    scale = lax.rsqrt(jnp.mean(centred * centred, axis=-1, keepdims=True) + EPS)
    return centred * scale, scale


def norm_back(grad, unit, scale, gain):
    scaled = grad * gain
    return scale * (
        scaled
        - jnp.mean(scaled, axis=-1, keepdims=True)
        - unit * jnp.mean(scaled * unit, axis=-1, keepdims=True)
    )


def body(
    tokens, out_grad, caption_states,
    query_weight, key_weight, value_weight, output_weight,
    cross_query, cross_key, cross_value, cross_output,
    up_weight, down_weight,
    attn_gain, attn_bias, cross_gain, cross_bias, mlp_gain, mlp_bias,
    item_ids, caption_segments, item_rows, item_segments,
):
    device = lax.axis_index(AXIS)
    count = lax.axis_size(AXIS)
    rows = tokens.shape[0]
    tiles = rows // TILE
    odd = lax.rem(device, 2) == 1
    swap = [(i, i ^ 1) for i in range(count)]
    ahead = [(i, i + 2) for i in range(count - 2)]
    behind = [(i + 2, i) for i in range(count - 2)]

    inputs = tokens.astype(F32)
    low_one = (normalise(inputs)[0] * attn_gain + attn_bias).astype(BF16)
    queries = matmul(low_one, query_weight).astype(BF16)
    text_keys = matmul(caption_states, cross_key).astype(BF16)
    text_values = matmul(caption_states, cross_value).astype(BF16)
    block_two = lax.ppermute(tokens, AXIS, ahead)
    block_two, queries, text_keys, text_values = lax.optimization_barrier((block_two, queries, text_keys, text_values))
    block_one = lax.ppermute(jnp.where(odd, block_two, tokens), AXIS, swap)
    near_tokens = jnp.concatenate([block_two, block_one, tokens], 0)

    all_ids = jnp.concatenate([jnp.full((REACH * rows,), -1, jnp.int32), item_ids])
    near_ids = lax.dynamic_slice_in_dim(all_ids, device * rows, (REACH + 1) * rows)
    own_ids = near_ids[REACH * rows :]
    near_rows = (REACH + 1) * rows
    span = REACH * rows + TILE
    windows = jnp.stack([near_ids[t * TILE : t * TILE + span] for t in range(tiles)])
    firsts = own_ids[::TILE]
    before = jnp.sum((near_ids[None, :] < firsts[:, None]).astype(jnp.int32), axis=1)
    lasts = REACH * rows + TILE * (1 + jnp.arange(tiles, dtype=jnp.int32))
    numbers = lasts // TILE - before // TILE
    numbers = jnp.clip(numbers, 1, span // TILE)
    self_sizes = tuple(TILE * (i + 1) for i in range(span // TILE))
    self_ends = (REACH * rows + TILE, TILE)

    text = caption_states.shape[0]
    caption_len = caption_segments.shape[1]
    member = own_ids[:, None] == jnp.arange(item_rows.shape[0], dtype=jnp.int32)[None, :]
    codes = item_rows * caption_len + item_segments
    query_code = jnp.sum(jnp.where(member, codes[None, :], 0), axis=1)
    key_code = (jnp.arange(text, dtype=jnp.int32) // caption_len) * caption_len + caption_segments.reshape(-1)
    text_code = jnp.broadcast_to(key_code[None], (tiles, text))
    no_numbers = jnp.zeros((tiles,), jnp.int32)
    text_ends = (text, 0)

    near_unit, near_scale = normalise(near_tokens.astype(F32))
    near_low = (near_unit * attn_gain + attn_bias).astype(BF16)
    near_keys = matmul(near_low, key_weight).astype(BF16)
    near_values = matmul(near_low, value_weight).astype(BF16)
    self_att, self_lse = attend_forward(
        queries, near_keys, near_values, own_ids[:, None], windows[:, None, :], numbers, True, self_sizes, self_ends
    )
    after_one = inputs + matmul(self_att, output_weight)
    unit_two, scale_two = normalise(after_one)
    low_two = (unit_two * cross_gain + cross_bias).astype(BF16)
    cross_q = matmul(low_two, cross_query).astype(BF16)
    cross_att, cross_lse = cross_forward(
        cross_q, text_keys, text_values, query_code[:, None], key_code.reshape(-1, caption_len)
    )
    after_two = after_one + matmul(cross_att, cross_output)
    unit_three, scale_three = normalise(after_two)
    low_three = (unit_three * mlp_gain + mlp_bias).astype(BF16)
    width = tokens.shape[1]
    if count == 32:
        starts = jnp.sum((near_ids[None, :] < own_ids[:, None]).astype(jnp.int32), axis=1)
        sums, small, block_output, input_grad = layer_tail(
            Far(
                low_three=low_three, out_grad=out_grad, after_two=after_two,
                up_weight=up_weight, down_weight=down_weight,
                cross_att=cross_att, cross_q=cross_q, text_keys=text_keys, text_values=text_values,
                low_two=low_two, after_one=after_one, captions=caption_states,
                cross_output=cross_output, cross_key=cross_key, cross_value=cross_value, cross_query=cross_query,
                output_weight=output_weight,
                queries=queries, near_keys=near_keys, near_values=near_values, self_att=self_att,
                near_low=near_low, near_tokens=near_tokens,
                query_weight=query_weight, key_weight=key_weight, value_weight=value_weight,
            ),
            Near(
                starts=starts[None, :], self_lse=self_lse, query_code=query_code[None, :], key_code=key_code[:, None],
                cross_lse=cross_lse, gains=jnp.stack([attn_gain, cross_gain, mlp_gain]),
            ),
        )
        small = lax.dynamic_slice_in_dim(small, device * (width // count), width // count, 1)
    else:
        hidden_pre = matmul(low_three, up_weight)
        hidden, slope = gelu_and_slope(hidden_pre)
        hidden_low = hidden.astype(BF16)
        grad_pre = (slope * right_product(out_grad, down_weight)).astype(BF16)
        block_output = (after_two + matmul(hidden_low, down_weight)).astype(BF16)

        down_grad = left_product(hidden_low, out_grad).astype(BF16)
        up_grad = left_product(low_three, grad_pre).astype(BF16)
        z_, y_, x_, c_ = 0, 1, 2, 3
        one_way = (c_, x_, y_, z_) if len(factors(count)) == 4 else (0,)
        other_way = (c_, y_, x_, z_) if len(factors(count)) == 4 else (0,)
        grad_three = right_product(grad_pre, up_weight)
        mlp_gain_grad = jnp.sum(grad_three * unit_three, axis=0)
        mlp_bias_grad = jnp.sum(grad_three, axis=0)
        grad_two = out_grad.astype(F32) + norm_back(grad_three, unit_three, scale_three, mlp_gain)
        grad_two_low = grad_two.astype(BF16)

        cross_output_grad = left_product(cross_att, grad_two_low).astype(BF16)
        grad_cross = right_product(grad_two_low, cross_output).astype(BF16)
        grad_cq, grad_tk, grad_tv = attend_backward(
            cross_q, text_keys, text_values, grad_cross, cross_att, cross_lse,
            query_code[None, :], text_code[:, :, None], no_numbers, False, (text,), text_ends,
        )
        width = grad_tk.shape[1]
        cross_key_grad = left_product(caption_states, grad_tk).astype(BF16)
        cross_value_grad = left_product(caption_states, grad_tv).astype(BF16)
        caption_grad = (right_product(grad_tk, cross_key) + right_product(grad_tv, cross_value)).astype(BF16)
        cross_query_grad = left_product(low_two, grad_cq).astype(BF16)
        grad_norm_two = right_product(grad_cq, cross_query)
        cross_gain_grad = jnp.sum(grad_norm_two * unit_two, axis=0)
        cross_bias_grad = jnp.sum(grad_norm_two, axis=0)
        grad_one = grad_two + norm_back(grad_norm_two, unit_two, scale_two, cross_gain)
        grad_one_low = grad_one.astype(BF16)

        output_weight_grad = left_product(self_att, grad_one_low).astype(BF16)
        grad_self = right_product(grad_one_low, output_weight).astype(BF16)
        grad_q, grad_k, grad_v = attend_backward(
            queries, near_keys, near_values, grad_self, self_att, self_lse,
            own_ids[None, :], windows[:, :, None], numbers, True, self_sizes, self_ends,
        )
        grad_near = right_product(grad_k, key_weight) + right_product(grad_v, value_weight)
        grad_own = grad_near[REACH * rows :] + right_product(grad_q, query_weight)
        to_two = grad_near[:rows]
        to_one = grad_near[rows : REACH * rows].astype(BF16)
        from_swap = lax.ppermute(to_one, AXIS, swap).astype(F32)
        to_two = (to_two + jnp.where(odd, from_swap, 0.0)).astype(BF16)
        from_two = lax.ppermute(to_two, AXIS, behind).astype(F32)
        near_sum = jnp.concatenate([grad_near[: REACH * rows], grad_own], 0)
        attn_gain_grad = jnp.sum(near_sum * near_unit, axis=0)
        attn_bias_grad = jnp.sum(near_sum, axis=0)
        grad_norm_one = grad_own + from_two + jnp.where(odd, 0.0, from_swap)
        unit_one = near_unit[REACH * rows :]
        input_grad = grad_one + norm_back(grad_norm_one, unit_one, near_scale[REACH * rows :], attn_gain)
        query_grad = left_product(low_one, grad_q).astype(BF16)
        key_grad = left_product(near_low, grad_k).astype(BF16)
        value_grad = left_product(near_low, grad_v).astype(BF16)
        vectors = jnp.stack(
            [attn_gain_grad, attn_bias_grad, cross_gain_grad, cross_bias_grad, mlp_gain_grad, mlp_bias_grad]
        )
        grads = [
            down_grad, up_grad, cross_output_grad, cross_query_grad, cross_key_grad, cross_value_grad, output_weight_grad,
        ]
        sums = [
            reduce_scatter(grad, one_way if i % 2 else other_way, BF16, count)
            for i, grad in enumerate([*grads, query_grad, key_grad, value_grad, caption_grad])
        ]
        small = reduce_scatter(vectors.T, one_way, F32, count).T
        (down_out, up_out, cross_output_out, cross_query_out, cross_key_out, cross_value_out,
         output_out, query_out, key_out, value_out, caption_out) = sums
        sums = Sums(
            up=up_out, down=down_out, cross_output=cross_output_out, cross_key=cross_key_out,
            cross_value=cross_value_out, caption=caption_out, cross_query=cross_query_out, output=output_out,
            query=query_out, key=key_out, value=value_out,
        )
    return (
        block_output, input_grad, sums.caption,
        sums.query, sums.key, sums.value, sums.output,
        sums.cross_query, sums.cross_key, sums.cross_value, sums.cross_output,
        sums.up, sums.down,
        small[0], small[1], small[2], small[3], small[4], small[5],
    )


def solution(mesh):
    split = P(AXIS, None)
    return jax.shard_map(
        body,
        mesh=mesh,
        in_specs=(split, split) + (P(),) * 21,
        out_specs=(split,) * 13 + (P(AXIS),) * 6,
        check_vma=False,
    )
```

```python
import functools
from typing import Any, NamedTuple

import jax
import jax.numpy as jnp
from jax import lax
from jax.experimental import pallas as pl
from jax.experimental.pallas import tpu as pltpu
from jax.sharding import PartitionSpec as P

HEADS = 16
REACH = 2
EPS = 1e-05
NEG = -1e30
TILE = 256
LANES = 128
AXIS = "seq"
F32 = jnp.float32
BF16 = jnp.bfloat16

NT = (((1,), (1,)), ((), ()))
TN = (((0,), (0,)), ((), ()))


def head_lanes(value, half):
    lane = lax.broadcasted_iota(jnp.int32, value.shape, 1)
    keep = (lane < LANES // 2) if half == 0 else (lane >= LANES // 2)
    return jnp.where(keep, value, jnp.zeros_like(value))


def forward_kernel(causal, sizes, ends, n_ref, qid_ref, kid_ref, q_ref, k_ref, v_ref, o_ref, lse_ref, bias_ref):
    tile = pl.program_id(1)
    span = bias_ref.shape[2]

    @pl.when(pl.program_id(0) == 0)
    def _():
        last = ends[0] + tile * ends[1]
        kid = kid_ref[tile]
        qid = qid_ref[...]
        allowed = kid == qid
        if causal:
            kpos = lax.broadcasted_iota(jnp.int32, (TILE, span), 1)
            qpos = lax.broadcasted_iota(jnp.int32, (TILE, span), 0) + (span - TILE)
            allowed = allowed & (kpos <= qpos)
        bias_ref[tile] = jnp.where(allowed, 0.0, NEG)

    def run(size):
        start = pl.multiple_of(ends[0] + tile * ends[1] - size, TILE)
        keys = k_ref[pl.ds(start, size), :]
        values = v_ref[pl.ds(start, size), :]
        query = q_ref[...] * jnp.asarray(0.125, BF16)
        outs = []
        lses = []
        for half in range(2):
            scores = lax.dot_general(head_lanes(query, half), keys, NT, preferred_element_type=F32)
            scores = scores + bias_ref[tile, :, span - size :]
            row_max = jnp.max(scores, axis=1, keepdims=True)
            weights = jnp.exp(scores - row_max)
            summed = jnp.sum(weights, axis=1, keepdims=True)
            out = jnp.dot(weights.astype(BF16), values, preferred_element_type=F32)
            outs.append(out / summed)
            lses.append(row_max + jnp.log(summed))
        lane = lax.broadcasted_iota(jnp.int32, (TILE, LANES), 1)
        o_ref[...] = jnp.where(lane < LANES // 2, outs[0], outs[1]).astype(BF16)
        for half in range(2):
            lse_ref[0, half : half + 1, :] = jnp.transpose(jnp.broadcast_to(lses[half], (TILE, LANES)))[:1]

    if len(sizes) == 1:
        run(sizes[0])
    else:
        number = n_ref[tile]
        for size in sizes:
            pl.when(number == size // TILE)(functools.partial(run, size))


def attend_forward(queries, keys, values, qid, kid, numbers, causal, sizes, ends):
    rows, width = queries.shape
    tiles = rows // TILE
    pairs = width // LANES
    key_rows = keys.shape[0]
    span = max(sizes)
    flops = 4 * rows * span * width
    return pl.pallas_call(
        functools.partial(forward_kernel, causal, sizes, ends),
        grid_spec=pltpu.PrefetchScalarGridSpec(
            num_scalar_prefetch=1,
            grid=(pairs, tiles),
            in_specs=[
                pl.BlockSpec((TILE, 1), lambda h, t, n: (t, 0)),
                pl.BlockSpec((tiles, 1, span), lambda h, t, n: (0, 0, 0)),
                pl.BlockSpec((TILE, LANES), lambda h, t, n: (t, h)),
                pl.BlockSpec((key_rows, LANES), lambda h, t, n: (0, h)),
                pl.BlockSpec((key_rows, LANES), lambda h, t, n: (0, h)),
            ],
            out_specs=[
                pl.BlockSpec((TILE, LANES), lambda h, t, n: (t, h)),
                pl.BlockSpec((1, 2, TILE), lambda h, t, n: (h, 0, t)),
            ],
            scratch_shapes=[pltpu.VMEM((tiles, TILE, span), F32)],
        ),
        out_shape=[
            jax.ShapeDtypeStruct((rows, width), BF16),
            jax.ShapeDtypeStruct((pairs, 2, rows), F32),
        ],
        compiler_params=pltpu.CompilerParams(vmem_limit_bytes=24 << 20),
        cost_estimate=pl.CostEstimate(flops=4 * flops, bytes_accessed=8 << 20, transcendentals=rows * span * HEADS),
    )(numbers, qid, kid, queries, keys, values)


def caption_lanes(value, lines, length):
    return jnp.concatenate([value[r * length : (r + 1) * length] for r in range(lines)], 1)


def spread(value, in_row):
    return jnp.concatenate([jnp.where(mask, value, jnp.zeros_like(value)) for mask in in_row], 1)


def rows_of(code, lines, length):
    return [(code >= r * length) & (code < (r + 1) * length) for r in range(lines)]


def either(masks):
    result = masks[0]
    for mask in masks[1:]:
        result = result | mask
    return result


def cross_forward_kernel(code_ref, key_ref, q_ref, k_ref, v_ref, o_ref, lse_ref):
    lines, length = key_ref.shape
    keys = caption_lanes(k_ref[...], lines, length)
    values = caption_lanes(v_ref[...], lines, length)
    lane = lax.broadcasted_iota(jnp.int32, (TILE, LANES), 1)
    for tile in range(q_ref.shape[0] // TILE):
        mine = slice(tile * TILE, (tile + 1) * TILE)
        code = jnp.broadcast_to(code_ref[mine, :], (TILE, LANES))
        in_row = rows_of(code, lines, length)
        allowed = either([code[:, :length] == key_ref[r : r + 1, :] for r in range(lines)])
        query = q_ref[mine, :] * jnp.asarray(0.125, BF16)
        outs = []
        for half in range(2):
            scores = lax.dot_general(
                spread(head_lanes(query, half), in_row), keys, NT, preferred_element_type=F32
            )
            scores = jnp.where(allowed, scores, NEG)
            row_max = jnp.max(scores, axis=1, keepdims=True)
            weights = jnp.exp(scores - row_max)
            summed = jnp.sum(weights, axis=1, keepdims=True)
            wide = jnp.dot(weights.astype(BF16), values, preferred_element_type=F32)
            out = jnp.zeros((TILE, LANES), F32)
            for r in range(lines):
                out = jnp.where(in_row[r], wide[:, r * LANES : (r + 1) * LANES], out)
            outs.append(out / summed)
            lse = jnp.broadcast_to(row_max + jnp.log(summed), (TILE, LANES))
            lse_ref[0, half : half + 1, mine] = jnp.transpose(lse)[:1]
        o_ref[mine, :] = jnp.where(lane < LANES // 2, outs[0], outs[1]).astype(BF16)


def cross_forward(queries, keys, values, query_code, key_codes):
    rows, width = queries.shape
    pairs = width // LANES
    text = keys.shape[0]
    own = pl.BlockSpec((rows, LANES), lambda h: (0, h))
    wide = pl.BlockSpec((text, LANES), lambda h: (0, h))
    return pl.pallas_call(
        cross_forward_kernel,
        grid=(pairs,),
        in_specs=[
            pl.BlockSpec((rows, 1), lambda h: (0, 0)), pl.BlockSpec(key_codes.shape, lambda h: (0, 0)), own, wide, wide,
        ],
        out_specs=[own, pl.BlockSpec((1, 2, rows), lambda h: (h, 0, 0))],
        out_shape=[
            jax.ShapeDtypeStruct((rows, width), BF16),
            jax.ShapeDtypeStruct((pairs, 2, rows), F32),
        ],
        compiler_params=pltpu.CompilerParams(vmem_limit_bytes=16 << 20),
        cost_estimate=pl.CostEstimate(
            flops=4 * rows * text * width, bytes_accessed=4 << 20, transcendentals=rows * text * HEADS // 4
        ),
    )(query_code, key_codes, queries, keys, values)


def backward_kernel(
    causal, sizes, ends, n_ref, qid_ref, kid_ref, q_ref, k_ref, v_ref, g_ref, o_ref, lse_ref,
    dq_ref, dk_ref, dv_ref, bias_ref, dk_sum, dv_sum,
):
    tile = pl.program_id(1)
    tiles = pl.num_programs(1)
    span = bias_ref.shape[1]

    @pl.when(pl.program_id(0) == 0)
    def _():
        kid = kid_ref[tile]
        qid = qid_ref[...]
        allowed = kid == qid
        if causal:
            kpos = lax.broadcasted_iota(jnp.int32, (span, TILE), 0)
            qpos = lax.broadcasted_iota(jnp.int32, (span, TILE), 1) + (span - TILE)
            allowed = allowed & (kpos <= qpos)
        bias_ref[tile] = jnp.where(allowed, 0.0, NEG)

    @pl.when(tile == 0)
    def _():
        dk_sum[...] = jnp.zeros_like(dk_sum)
        dv_sum[...] = jnp.zeros_like(dv_sum)

    def run(size):
        start = pl.multiple_of(ends[0] + tile * ends[1] - size, TILE)
        window = pl.ds(start, size)
        keys = k_ref[window, :]
        values = v_ref[window, :]
        query = q_ref[...] * jnp.asarray(0.125, BF16)
        grad = g_ref[...]
        inner = grad.astype(F32) * o_ref[...].astype(F32)
        inner_rows = jnp.transpose(inner)
        half_lanes = LANES // 2
        parts_dq = []
        dk = None
        dv = None
        for half in range(2):
            head_q = head_lanes(query, half)
            head_g = head_lanes(grad, half)
            lse = lse_ref[0, half : half + 1, :]
            delta = jnp.sum(inner_rows[half * half_lanes : (half + 1) * half_lanes, :], axis=0, keepdims=True)
            scores = lax.dot_general(keys, head_q, NT, preferred_element_type=F32)
            probs = jnp.exp(scores + bias_ref[tile, span - size :, :] - lse)
            grad_probs = lax.dot_general(values, head_g, NT, preferred_element_type=F32)
            grad_scores = (probs * (grad_probs - delta)).astype(BF16)
            probs = probs.astype(BF16)
            part_k = jnp.dot(grad_scores, head_q, preferred_element_type=F32)
            part_v = jnp.dot(probs, head_g, preferred_element_type=F32)
            dk = part_k if dk is None else dk + part_k
            dv = part_v if dv is None else dv + part_v
            parts_dq.append(lax.dot_general(grad_scores, keys, TN, preferred_element_type=F32))
        lane = lax.broadcasted_iota(jnp.int32, (TILE, LANES), 1)
        dq_ref[...] = (jnp.where(lane < half_lanes, parts_dq[0], parts_dq[1]) * 0.125).astype(BF16)
        dk_sum[window, :] += dk
        dv_sum[window, :] += dv

    if len(sizes) == 1:
        run(sizes[0])
    else:
        number = n_ref[tile]
        for size in sizes:
            pl.when(number == size // TILE)(functools.partial(run, size))

    @pl.when(tile == tiles - 1)
    def _():
        dk_ref[...] = dk_sum[...].astype(BF16)
        dv_ref[...] = dv_sum[...].astype(BF16)


def attend_backward(queries, keys, values, grad, out, lse, qid, kid, numbers, causal, sizes, ends):
    rows, width = queries.shape
    tiles = rows // TILE
    pairs = width // LANES
    key_rows = keys.shape[0]
    span = max(sizes)
    flops = 10 * rows * span * width
    near = pl.BlockSpec((TILE, LANES), lambda h, t, n: (t, h))
    wide = pl.BlockSpec((key_rows, LANES), lambda h, t, n: (0, h))
    return pl.pallas_call(
        functools.partial(backward_kernel, causal, sizes, ends),
        grid_spec=pltpu.PrefetchScalarGridSpec(
            num_scalar_prefetch=1,
            grid=(pairs, tiles),
            in_specs=[
                pl.BlockSpec((1, TILE), lambda h, t, n: (0, t)),
                pl.BlockSpec((tiles, span, 1), lambda h, t, n: (0, 0, 0)),
                near,
                wide,
                wide,
                near,
                near,
                pl.BlockSpec((1, 2, TILE), lambda h, t, n: (h, 0, t)),
            ],
            out_specs=[near, wide, wide],
            scratch_shapes=[
                pltpu.VMEM((tiles, span, TILE), F32),
                pltpu.VMEM((key_rows, LANES), F32),
                pltpu.VMEM((key_rows, LANES), F32),
            ],
        ),
        out_shape=[
            jax.ShapeDtypeStruct((rows, width), BF16),
            jax.ShapeDtypeStruct((key_rows, width), BF16),
            jax.ShapeDtypeStruct((key_rows, width), BF16),
        ],
        compiler_params=pltpu.CompilerParams(vmem_limit_bytes=48 << 20),
        cost_estimate=pl.CostEstimate(flops=4 * flops, bytes_accessed=12 << 20, transcendentals=rows * span * HEADS),
    )(numbers, qid, kid, queries, keys, values, grad, out, lse)


def factors(count):
    return {32: (4, 2, 2, 2), 128: (4, 4, 4, 2)}.get(count, (count,))


def coordinates(count):
    sizes = factors(count)
    left = lax.axis_index(AXIS)
    places = []
    for size in reversed(sizes):
        places.insert(0, lax.rem(left, size))
        left = lax.div(left, size)
    return places


def peers_along(count, axis, step):
    sizes = factors(count)
    stride = 1
    for size in sizes[axis + 1 :]:
        stride *= size
    size = sizes[axis]
    pairs = []
    for device in range(count):
        place = (device // stride) % size
        pairs.append((device, device + ((place + step) % size - place) * stride))
    return pairs


def take(value, place, axis):
    return lax.dynamic_slice_in_dim(value, place, 1, axis)


def total(terms):
    summed = terms[0].astype(F32)
    for term in terms[1:]:
        summed = summed + term.astype(F32)
    return summed


def reduce_scatter(value, order, kind, count):
    sizes = factors(count)
    places = coordinates(count)
    rows, width = value.shape
    terms = [value.reshape(*sizes, rows // count, width)]
    for axis in order:
        size = sizes[axis]
        arrived = []
        for step in range(1, size):
            other = lax.rem(places[axis] + step, size)
            sent = total([take(term, other, axis) for term in terms]).astype(kind)
            arrived.append(lax.ppermute(sent, AXIS, peers_along(count, axis, step)))
        terms = [take(term, places[axis], axis) for term in terms] + arrived
    return total(terms).reshape(rows // count, width)


def all_gather(value, order, count):
    sizes = factors(count)
    places = coordinates(count)
    rows, width = value.shape
    held = value.reshape(*([1] * len(sizes)), rows, width)
    for axis in order:
        size = sizes[axis]
        shape = list(held.shape)
        shape[axis] = size
        gathered = lax.dynamic_update_slice_in_dim(jnp.zeros(shape, held.dtype), held, places[axis], axis)
        for step in range(1, size):
            arrived = lax.ppermute(held, AXIS, peers_along(count, axis, step))
            source = lax.rem(places[axis] + size - step, size)
            gathered = lax.dynamic_update_slice_in_dim(gathered, arrived, source, axis)
        held = gathered
    return held.reshape(rows * count, width)


MESH = pl.DeviceIdType.MESH
BLOCK = 32
WIDE = 1024


def places32():
    me = lax.axis_index(AXIS)
    core = lax.rem(me, 2)
    x = lax.rem(lax.div(me, 2), 2)
    y = lax.rem(lax.div(me, 4), 2)
    z = lax.div(me, 8)
    return me, core, x, y, z


GELU_A = 0.7978845608028654
GELU_B = 0.044715


def gelu_and_slope(value):
    square = value * value
    bend = jnp.tanh(GELU_A * (value + GELU_B * value * square))
    gate = 0.5 * (1.0 + bend)
    slope = gate + value * 0.5 * (1.0 - bend * bend) * (GELU_A * (1.0 + 3.0 * GELU_B * square))
    return value * gate, slope


def normalise_rows(value):
    mean = jnp.mean(value, axis=-1, keepdims=True)
    centred = value - mean
    scale = lax.rsqrt(jnp.mean(centred * centred, axis=-1, keepdims=True) + EPS)
    return centred * scale, scale


class Far(NamedTuple):
    low_three: Any
    out_grad: Any
    after_two: Any
    up_weight: Any
    down_weight: Any
    cross_att: Any
    cross_q: Any
    text_keys: Any
    text_values: Any
    low_two: Any
    after_one: Any
    captions: Any
    cross_output: Any
    cross_key: Any
    cross_value: Any
    cross_query: Any
    output_weight: Any
    queries: Any
    near_keys: Any
    near_values: Any
    self_att: Any
    near_low: Any
    near_tokens: Any
    query_weight: Any
    key_weight: Any
    value_weight: Any


class Near(NamedTuple):
    starts: Any
    self_lse: Any
    query_code: Any
    key_code: Any
    cross_lse: Any
    gains: Any


class Sums(NamedTuple):
    up: Any
    down: Any
    cross_output: Any
    cross_key: Any
    cross_value: Any
    caption: Any
    cross_query: Any
    output: Any
    query: Any
    key: Any
    value: Any


class Scratch(NamedTuple):
    arena: Any
    sums: Any
    accum_k: Any
    accum_v: Any
    back_one: Any
    back_two: Any
    vec: Any
    vec_in: Any
    tiles: Any
    r0: Any
    r1: Any
    r2: Any
    r3: Any
    load: Any
    s0: Any
    d0: Any
    s1: Any
    d1: Any
    s2: Any
    d2: Any
    s3: Any
    d3: Any
    vs: Any
    vd: Any
    bs: Any
    bd: Any
    credit: Any


UP, DOWN, CROSS_OUTPUT, CROSS_KEY, CROSS_VALUE, CAPTION, CROSS_QUERY, OUTPUT, QUERY, KEY, VALUE = range(11)
PIECES = (
    (UP, 0), (UP, 1), (UP, 2), (UP, 3), (DOWN, 0), (DOWN, 1), (DOWN, 2), (DOWN, 3),
    (CROSS_OUTPUT, 0), (CROSS_KEY, 0), (CROSS_VALUE, 0), (CAPTION, 0), (CROSS_QUERY, 0), (OUTPUT, 0),
    (QUERY, 0), (KEY, 0), (VALUE, 0),
)
PLAN = (
    (), (), (), (), ((2, 0),), (), ((2, 1),), ((2, 2),), (), ((2, 3),), (), (), (), ((3, 0), (2, 4)), (), (), (),
    (), ((3, 1),), (), (), (), ((2, 5),), (), (), (), (), ((3, 2), (2, 6)), (), (), (), ((3, 3),), (), ((2, 7),),
    (), (), ((3, 4), (2, 8)), ((3, 6), (3, 5)), ((1, 13),), ((3, 7),), (), ((2, 9),), (), (), ((2, 10),), (), (),
    ((2, 11),), (), ((3, 8), (2, 12)), (), (), ((3, 9),), (), ((2, 13), (3, 11)), ((3, 10),), ((3, 12),), (),
    ((2, 14),), ((3, 13),),
)
LANDINGS = 9
SLOTS = 2
HALF = LANES // 2
STEP = 64
LOADS = 48


def layer_kernel(rows, *refs):
    total = len(PIECES)
    n_far, n_near, n_sums = len(Far._fields), len(Near._fields), len(Sums._fields)
    far = Far(*refs[:n_far])
    near = Near(*refs[n_far : n_far + n_near])
    refs = refs[n_far + n_near :]
    outs = Sums(*refs[:n_sums])
    vec_out, block_output, input_grad = refs[n_sums : n_sums + 3]
    held = Scratch(*refs[n_sums + 3 :])
    (arena, sums, accum_k, accum_v, back_one, back_two, vec, vec_in, tiles, r0, r1, r2, r3,
     load, s0, d0, s1, d1, s2, d2, s3, d3, vs, vd, bs, bd, credit) = held

    me, core, x, y, z = places32()
    sibling = me + 1 - 2 * core
    x_peer = me + 2 - 4 * x
    y_peer = me + 4 - 8 * y
    z_other = [lax.rem(z + m, 4) for m in range(1, 4)]
    z_peers = [me + 8 * (o - z) for o in z_other]
    has_before = me >= 2
    has_after = me < 30

    barrier = pltpu.get_barrier_semaphore()
    for peer in (sibling, x_peer, y_peer, *z_peers):
        pl.semaphore_signal(barrier, inc=1, device_id=(peer,), device_id_type=MESH)

    @pl.when(has_before)
    def _():
        pl.semaphore_signal(barrier, inc=1, device_id=(me - 2,), device_id_type=MESH)

    @pl.when(has_after)
    def _():
        pl.semaphore_signal(barrier, inc=1, device_id=(me + 2,), device_id_type=MESH)

    numbers = iter(range(LOADS))

    def fetch(source, slot):
        return start_copy(source, arena.at[pl.ds(slot * rows, source.shape[0])])

    def start_copy(source, target):
        copy = pltpu.make_async_copy(source, target, load.at[next(numbers)])
        copy.start()
        return copy

    def at(slot, count=1):
        return pl.ds(slot * rows, count * rows)

    def up_part(part):
        return far.up_weight.at[:, pl.ds(part * WIDE, WIDE)]

    def down_part(part):
        return far.down_weight.at[pl.ds(part * WIDE, WIDE)]

    ONE, TWO, THREE = 12, 14, 10
    low_three_load = fetch(far.low_three, 8)
    up_loads = [fetch(up_part(0), THREE)]
    out_grad_load = fetch(far.out_grad, 9)
    down_loads = [fetch(down_part(0), ONE)]
    up_loads.append(fetch(up_part(1), TWO))
    after_load = start_copy(far.after_two, sums.at[2])

    pl.semaphore_wait(barrier, 6 + jnp.where(has_before, 1, 0) + jnp.where(has_after, 1, 0))

    def remote(src, dst, send, recv, peer):
        return pltpu.make_async_remote_copy(
            src_ref=src, dst_ref=dst, send_sem=send, recv_sem=recv, device_id=(peer,), device_id_type=MESH
        )

    def along(c):
        even = lax.rem(c, 2) == 0
        return (
            jnp.where(even, x, y),
            jnp.where(even, x_peer, y_peer),
            jnp.where(even, y, x),
            jnp.where(even, y_peer, x_peer),
        )

    def add_blocks(count, dst, src):
        @pl.loop(0, count, unroll=4)
        def _(i):
            dst(i)[...] = dst(i)[...] + src(i)[...]

    def take_credit(c):
        if c >= LANDINGS:
            pl.semaphore_wait(credit, 1)

    def give(c):
        take_credit(c)
        remote(tiles.at[c % SLOTS, 1 - core], r0.at[c % LANDINGS], s0.at[c], d0.at[c], sibling).start()

    def make(c, left_at, right_at, depth):
        @pl.loop(0, 4)
        def _(zz):
            left = arena[pl.ds(left_at * rows, depth), pl.ds(pl.multiple_of(zz * TILE, TILE), TILE)]
            for part in range(2):
                cols = slice(part * (WIDE // 2), (part + 1) * (WIDE // 2))
                result = lax.dot_general(
                    left, arena[pl.ds(right_at * rows, depth), cols], TN, preferred_element_type=F32
                ).astype(BF16)
                for block in range(8):
                    yy, xx, cc = block // 4, (block // 2) % 2, block % 2
                    f, s = (xx, yy) if c % 2 == 0 else (yy, xx)
                    tiles[c % SLOTS, cc, f, s, zz, :, cols] = result[block * BLOCK : (block + 1) * BLOCK]

        give(c)

    def make_down(c, part):
        @pl.loop(0, 4)
        def _(zz):
            for quarter in range(4):
                yy, xx = quarter // 2, quarter % 2
                f, s = (xx, yy) if c % 2 == 0 else (yy, xx)
                left = arena[
                    pl.ds(pl.multiple_of(zz * rows, rows), rows), quarter * TILE : (quarter + 1) * TILE
                ]
                result = lax.dot_general(
                    left, arena[at(9), part * TILE : (part + 1) * TILE], TN, preferred_element_type=F32
                ).astype(BF16)
                for cc in range(2):
                    for group in range(4):
                        top = cc * 128 + group * BLOCK
                        tiles[c % SLOTS, cc, f, s, zz, :, group * TILE : (group + 1) * TILE] = result[top : top + BLOCK]

        give(c)

    def first(c):
        f, fp, _, _ = along(c)
        slot, place = c % SLOTS, c % LANDINGS
        copy = remote(tiles.at[slot, 1 - core], r0.at[place], s0.at[c], d0.at[c], sibling)
        copy.wait_recv()
        add_blocks(
            16,
            lambda i: r0.at[place, i // 8, (i // 4) % 2, i % 4],
            lambda i: tiles.at[slot, core, i // 8, (i // 4) % 2, i % 4],
        )
        remote(r0.at[place, 1 - f], r1.at[c], s1.at[c], d1.at[c], fp).start()
        copy.wait_send()

    def second(c):
        f, fp, s, sp = along(c)
        place = c % LANDINGS
        copy = remote(r0.at[place, 1 - f], r1.at[c], s1.at[c], d1.at[c], fp)
        copy.wait_recv()
        add_blocks(8, lambda i: r1.at[c, i // 4, i % 4], lambda i: r0.at[place, f, i // 4, i % 4])
        remote(r1.at[c, 1 - s], r2.at[c], s2.at[c], d2.at[c], sp).start()
        copy.wait_send()
        if c < total - LANDINGS:
            pl.semaphore_signal(credit, inc=1, device_id=(sibling,), device_id_type=MESH)

    def third(c):
        _, _, s, sp = along(c)
        copy = remote(r1.at[c, 1 - s], r2.at[c], s2.at[c], d2.at[c], sp)
        copy.wait_recv()
        add_blocks(4, lambda i: r2.at[c, i], lambda i: r1.at[c, s, i])
        for m in range(3):
            remote(r2.at[c, z_other[m]], r3.at[c, m], s3.at[c, m], d3.at[c, m], z_peers[m]).start()
        copy.wait_send()

    def last(c):
        number, part = PIECES[c]
        for m in range(3):
            remote(r2.at[c, z_other[m]], r3.at[c, m], s3.at[c, m], d3.at[c, m], z_peers[m]).wait()
        summed = r2[c, z].astype(F32) + r3[c, 0].astype(F32) + r3[c, 1].astype(F32) + r3[c, 2].astype(F32)
        out = outs[number]
        if number == DOWN:
            for group in range(4):
                out[group * BLOCK : (group + 1) * BLOCK, part * TILE : (part + 1) * TILE] = summed[
                    :, group * TILE : (group + 1) * TILE
                ]
        else:
            out[:, part * WIDE : (part + 1) * WIDE] = summed[: out.shape[0]]

    def each_tile(run):
        @pl.loop(0, WIDE // TILE, unroll=2)
        def _(n):
            run(pl.multiple_of(n * TILE, TILE))

    def product(pairs, add=False):
        def run(n):
            result = None
            for slot, weight in pairs:
                term = lax.dot_general(
                    arena[at(slot), :], arena[pl.ds(weight * rows + n, TILE), :], NT, preferred_element_type=F32
                )
                result = term if result is None else result + term
            if add:
                result += sums[0, :, pl.ds(n, TILE)]
            sums[0, :, pl.ds(n, TILE)] = result

        each_tile(run)

    def plain_product(slot, weight, add):
        def run(n):
            result = jnp.dot(arena[at(slot), :], arena[at(weight, 2), pl.ds(n, TILE)], preferred_element_type=F32)
            if add:
                result += sums[0, :, pl.ds(n, TILE)]
            sums[0, :, pl.ds(n, TILE)] = result

        each_tile(run)

    def low_product(slot, weight, target):
        def run(n):
            result = lax.dot_general(
                arena[at(slot), :], arena[pl.ds(weight * rows + n, TILE), :], NT, preferred_element_type=F32
            )
            arena[at(target), pl.ds(n, TILE)] = result.astype(BF16)

        each_tile(run)

    def each_step(run):
        @pl.loop(0, rows // STEP)
        def _(i):
            run(pl.multiple_of(i * STEP, STEP))

    vec[...] = jnp.zeros_like(vec)

    def add_gains(row, grad, unit):
        vec[row : row + 1] += jnp.sum(grad * unit, axis=0, keepdims=True)
        vec[row + 1 : row + 2] += jnp.sum(grad, axis=0, keepdims=True)

    def norm_back_rows(grad, unit, scale, gain):
        scaled = grad * gain
        return scale * (
            scaled - jnp.mean(scaled, axis=-1, keepdims=True) - unit * jnp.mean(scaled * unit, axis=-1, keepdims=True)
        )

    def attend_step(keys, values, query, grad, out, lse, allowed):
        query = query * jnp.asarray(0.125, BF16)
        inner = jnp.transpose(grad.astype(F32) * out.astype(F32))
        turned_keys = jnp.transpose(keys)
        parts = []
        dk = None
        dv = None
        for half in range(2):
            head_q = head_lanes(query, half)
            head_g = head_lanes(grad, half)
            delta = jnp.sum(inner[half * HALF : (half + 1) * HALF], axis=0, keepdims=True)
            scores = lax.dot_general(keys, head_q, NT, preferred_element_type=F32)
            probs = jnp.exp(jnp.where(allowed, scores - lse[half], NEG))
            grad_probs = lax.dot_general(values, head_g, NT, preferred_element_type=F32)
            grad_scores = (probs * (grad_probs - delta)).astype(BF16)
            part_k = jnp.dot(grad_scores, head_q, preferred_element_type=F32)
            part_v = jnp.dot(probs.astype(BF16), head_g, preferred_element_type=F32)
            dk = part_k if dk is None else dk + part_k
            dv = part_v if dv is None else dv + part_v
            parts.append(jnp.dot(turned_keys, grad_scores, preferred_element_type=F32))
        dq = jnp.concatenate([parts[0][:HALF], parts[1][HALF:]], 0)
        return (jnp.transpose(dq) * 0.125).astype(BF16), dk, dv

    position = [0]

    def take_steps(steps):
        for kind, c in steps:
            (first, second, third)[kind - 1](c)

    def tick():
        take_steps(PLAN[position[0]])
        position[0] += 1

    def loop_tick(base, i):
        for number, steps in enumerate(PLAN[base : base + 16]):
            if steps:
                pl.when(i == number)(functools.partial(take_steps, steps))

    def activate(part, up_at, down_at):
        def run(n):
            cols = pl.ds(n, TILE)
            pre = jnp.dot(arena[at(8), :], arena[at(up_at, 2), cols], preferred_element_type=F32)
            grad = lax.dot_general(
                arena[at(9), :], arena[pl.ds(down_at * rows + n, TILE), :], NT, preferred_element_type=F32
            )
            hidden, slope = gelu_and_slope(pre)
            arena[at(part), cols] = hidden.astype(BF16)
            arena[at(4 + part), cols] = (slope * grad).astype(BF16)

        each_tile(run)

    low_three_load.wait()
    out_grad_load.wait()
    places = ((THREE, ONE), (TWO, THREE), (ONE, TWO), (THREE, ONE))
    for part in range(4):
        up_loads[part].wait()
        down_loads[part].wait()
        activate(part, *places[part])
        if part == 0:
            down_loads.append(fetch(down_part(1), THREE))
            up_loads.append(fetch(up_part(2), ONE))
        if part == 1:
            down_loads.append(fetch(down_part(2), TWO))
            up_loads.append(fetch(up_part(3), THREE))
        if part == 2:
            down_loads.append(fetch(down_part(3), ONE))
            weight_two = fetch(up_part(1), TWO)
        if part == 3:
            weight_one = fetch(up_part(0), ONE)
        make(part, 8, 4 + part, rows)
        if part > 0:
            first(part - 1)
        tick()
    places = (ONE, TWO, THREE, ONE)
    loads = [weight_one, weight_two, fetch(up_part(2), THREE)]
    for part in range(4):
        make_down(4 + part, part)
        loads[part].wait()
        product([(4 + part, places[part])], add=part > 0)
        if part == 0:
            loads.append(fetch(up_part(3), ONE))
        first(3 + part)
        tick()
    weight_two = fetch(far.cross_output, TWO)
    weight_three = fetch(down_part(0), THREE)
    weight_one = fetch(down_part(1), ONE)
    low_two_load = fetch(far.low_two, 4)
    captions_load = fetch(far.captions, 5)
    cross_att_load = fetch(far.cross_att, 6)
    cross_q_load = fetch(far.cross_q, 7)
    after_load.wait()
    gains = near.gains

    def norm_three(n):
        here = pl.ds(n, STEP)
        unit, scale = normalise_rows(sums[2, here, :])
        grad = sums[0, here, :]
        add_gains(4, grad, unit)
        value = arena[pl.ds(9 * rows + n, STEP), :].astype(F32) + norm_back_rows(grad, unit, scale, gains[2:3])
        sums[1, here, :] = value
        arena[pl.ds(9 * rows + n, STEP), :] = value.astype(BF16)

    each_step(norm_three)
    first(7)
    tick()

    weight_two.wait()
    low_product(9, TWO, 8)
    weight_two = fetch(down_part(2), TWO)
    cross_att_load.wait()
    make(8, 6, 9, rows)
    tick()
    weight_three.wait()
    plain_product(0, THREE, False)
    weight_three = fetch(down_part(3), THREE)
    tick()
    weight_one.wait()
    plain_product(1, ONE, True)
    weight_one = fetch(far.cross_key, ONE)
    first(8)
    tick()
    weight_two.wait()
    plain_product(2, TWO, True)
    weight_two = fetch(far.cross_value, TWO)
    keys_load = fetch(far.text_keys, 2)
    tick()
    weight_three.wait()
    plain_product(3, THREE, True)
    weight_three = fetch(far.cross_query, THREE)
    values_load = fetch(far.text_values, 3)
    tick()

    def finish_block(n):
        here = pl.ds(n, STEP)
        arena[pl.ds(n, STEP), :] = (sums[2, here, :] + sums[0, here, :]).astype(BF16)

    each_step(finish_block)
    tick()
    loop_base = position[0]
    position[0] += 16
    block_copy = start_copy(arena.at[at(0)], block_output)
    after_load = start_copy(far.after_one, sums.at[2])

    text = far.text_keys.shape[0]
    cross_q_load.wait()
    keys_load.wait()
    values_load.wait()

    @pl.loop(0, 16)
    def _(i):
        h, t = lax.div(i, 2), lax.rem(i, 2)
        lanes = pl.ds(pl.multiple_of(h * LANES, LANES), LANES)
        own = pl.multiple_of(t * TILE, TILE)
        mine = pl.ds(7 * rows + own, TILE)
        allowed = near.key_code[...] == near.query_code[:, pl.ds(own, TILE)]
        lse = [near.cross_lse[h, half : half + 1, pl.ds(own, TILE)] for half in range(2)]
        dq, dk, dv = attend_step(
            arena[at(2), lanes], arena[at(3), lanes], arena[mine, lanes],
            arena[pl.ds(8 * rows + own, TILE), lanes], arena[pl.ds(6 * rows + own, TILE), lanes], lse, allowed,
        )
        arena[mine, lanes] = dq

        @pl.when(t == 0)
        def _():
            accum_k[:text] = dk
            accum_v[:text] = dv

        @pl.when(t == 1)
        def _():
            arena[at(2), lanes] = (accum_k[:text] + dk).astype(BF16)
            arena[at(3), lanes] = (accum_v[:text] + dv).astype(BF16)

        loop_tick(loop_base, i)

    block_copy.wait()
    self_att_load = fetch(far.self_att, 8)
    captions_load.wait()
    make(9, 5, 2, rows)
    tick()
    weight_one.wait()
    weight_two.wait()
    product([(2, ONE), (3, TWO)])
    weight_one = fetch(far.output_weight, ONE)
    make(10, 5, 3, rows)
    first(9)
    tick()

    c = 11
    for zz in range(4):
        for block in range(8):
            yy, xx, cc = block // 4, (block // 2) % 2, block % 2
            f, s = (xx, yy) if c % 2 == 0 else (yy, xx)
            top = (zz * 8 + block) * 16
            tiles[c % SLOTS, cc, f, s, zz, :16, :] = sums[0, top : top + 16, :].astype(BF16)
            tiles[c % SLOTS, cc, f, s, zz, 16:, :] = jnp.zeros((16, WIDE), BF16)
    give(c)
    tick()
    keys_load = fetch(far.near_keys, 1)
    weight_three.wait()
    product([(7, THREE)])
    near_low_load = fetch(far.near_low, 9)
    first(10)
    tick()
    low_two_load.wait()
    make(12, 4, 7, rows)
    values_load = fetch(far.near_values, 4)
    queries_load = fetch(far.queries, 0)
    first(11)
    tick()
    after_load.wait()

    def norm_two(n):
        here = pl.ds(n, STEP)
        unit, scale = normalise_rows(sums[2, here, :])
        grad = sums[0, here, :]
        add_gains(2, grad, unit)
        value = sums[1, here, :] + norm_back_rows(grad, unit, scale, gains[1:2])
        sums[1, here, :] = value
        arena[pl.ds(14 * rows + n, STEP), :] = value.astype(BF16)

    each_step(norm_two)
    first(12)
    tick()

    weight_one.wait()
    low_product(14, ONE, 7)
    weight_one = fetch(far.value_weight, ONE)
    self_att_load.wait()
    make(13, 8, 14, rows)
    tick()
    loop_base = position[0]
    position[0] += 16
    weight_two = fetch(far.key_weight, TWO)
    queries_load.wait()
    keys_load.wait()
    values_load.wait()

    span = 2 * rows + TILE

    @pl.loop(0, 16)
    def _(i):
        h, t = lax.div(i, 2), lax.rem(i, 2)
        lanes = pl.ds(pl.multiple_of(h * LANES, LANES), LANES)
        own = pl.multiple_of(t * TILE, TILE)
        mine = pl.ds(own, TILE)
        kpos = lax.broadcasted_iota(jnp.int32, (span, TILE), 0)
        qpos = lax.broadcasted_iota(jnp.int32, (TILE, TILE), 1)
        dpos = lax.broadcasted_iota(jnp.int32, (TILE, TILE), 0)
        allowed = kpos >= near.starts[:, mine] - own
        allowed = jnp.concatenate([allowed[: span - TILE], allowed[span - TILE :] & (dpos <= qpos)], 0)
        lse = [near.self_lse[h, half : half + 1, mine] for half in range(2)]
        dq, dk, dv = attend_step(
            arena[pl.ds(rows + own, span), lanes], arena[pl.ds(4 * rows + own, span), lanes], arena[mine, lanes],
            arena[pl.ds(7 * rows + own, TILE), lanes], arena[pl.ds(8 * rows + own, TILE), lanes], lse, allowed,
        )
        arena[mine, lanes] = dq

        @pl.when(t == 0)
        def _():
            accum_k[:span] = dk
            accum_v[:span] = dv

        @pl.when(t == 1)
        def _():
            for target, accum, part in ((1, accum_k, dk), (4, accum_v, dv)):
                arena[pl.ds(target * rows, TILE), lanes] = accum[:TILE].astype(BF16)
                arena[pl.ds(target * rows + TILE, span - TILE), lanes] = (accum[TILE:span] + part[: span - TILE]).astype(BF16)
                arena[pl.ds(target * rows + span, TILE), lanes] = part[span - TILE :].astype(BF16)

        loop_tick(loop_base, i)

    near_low_load.wait()
    make(14, 11, 0, rows)
    weight_two.wait()
    weight_one.wait()
    product([(2, TWO), (5, ONE)])

    def as_low(slot, extra):
        def run(n):
            value = sums[0, pl.ds(n, STEP), :]
            if extra is not None:
                value = value + jnp.where(core == 1, extra[pl.ds(n, STEP), :].astype(F32), 0.0)
            arena[pl.ds(slot * rows + n, STEP), :] = value.astype(BF16)

        each_step(run)

    as_low(7, None)
    swap = remote(arena.at[at(7)], back_one, bs.at[0], bd.at[0], sibling)
    swap.start()
    first(14)
    tick()
    product([(1, TWO), (4, ONE)])
    swap.wait()
    as_low(8, back_one)
    send_back = remote(arena.at[at(8)], back_two, bs.at[1], bd.at[1], me - 2)

    @pl.when(has_before)
    def _():
        send_back.start()

    tick()
    make(15, 9, 1, 3 * rows)
    tick()
    query_weight_load = fetch(far.query_weight, 1)
    make(16, 9, 4, 3 * rows)
    token_load = fetch(far.near_tokens, 9)
    first(15)
    tick()

    def block_gains(slot, grad_slot, factor):
        def run(n):
            unit, _ = normalise_rows(arena[pl.ds(slot * rows + n, STEP), :].astype(F32))
            if grad_slot is None:
                grad = sums[0, pl.ds(n, STEP), :]
            else:
                grad = arena[pl.ds(grad_slot * rows + n, STEP), :].astype(F32)
            if factor is not None:
                grad = grad * factor
            add_gains(0, grad, unit)

        each_step(run)

    token_load.wait()
    block_gains(9, 8, None)
    block_gains(10, 7, jnp.where(core == 1, 1.0, 0.0))
    first(16)
    tick()
    query_weight_load.wait()
    product([(0, 1), (3, TWO), (6, ONE)])
    tick()
    block_gains(11, None, None)

    def vec_step(number, peer):
        step = remote(vec, vec_in.at[number], vs.at[number], vd.at[number], peer)
        step.start()
        return step

    def norm_one(n):
        here = pl.ds(n, STEP)
        unit, scale = normalise_rows(arena[pl.ds(11 * rows + n, STEP), :].astype(F32))
        grad = sums[0, here, :]
        grad = grad + jnp.where(core == 0, back_one[here, :].astype(F32), 0.0)
        grad = grad + jnp.where(has_after, back_two[here, :].astype(F32), 0.0)
        sums[1, here, :] += norm_back_rows(grad, unit, scale, gains[0:1])

    step = vec_step(0, sibling)
    step.wait()
    vec[...] += vec_in[0]
    step = vec_step(1, x_peer)
    second(15)

    @pl.when(has_before)
    def _():
        send_back.wait_send()

    @pl.when(has_after)
    def _():
        send_back.wait_recv()

    second(16)
    each_step(norm_one)
    out_copy = start_copy(sums.at[1], input_grad)
    step.wait()
    vec[...] += vec_in[1]
    step = vec_step(2, y_peer)
    third(14)
    third(15)
    step.wait()
    vec[...] += vec_in[2]
    steps = [vec_step(3 + m, z_peers[m]) for m in range(3)]
    for c in range(total - 3):
        last(c)
    third(16)
    for step in steps:
        step.wait()
    vec_out[...] = vec[...] + vec_in[3] + vec_in[4] + vec_in[5]
    for c in range(total - 3, total):
        last(c)
    out_copy.wait()


def copy_kernel(number, *refs):
    sources, targets, staged = refs[:number], refs[number : 2 * number], refs[2 * number : 3 * number]
    sem_in, sem_out = refs[3 * number :]
    inward = [pltpu.make_async_copy(sources[i], staged[i], sem_in.at[i]) for i in range(number)]
    outward = [pltpu.make_async_copy(staged[i], targets[i], sem_out.at[i]) for i in range(number)]
    for copy in inward:
        copy.start()
    for i in range(number):
        inward[i].wait()
        outward[i].start()
    for copy in outward:
        copy.wait()


def copy_all(arrays):
    anywhere = pl.BlockSpec(memory_space=pl.ANY)
    return pl.pallas_call(
        functools.partial(copy_kernel, len(arrays)),
        in_specs=[anywhere] * len(arrays),
        out_specs=[anywhere] * len(arrays),
        out_shape=[jax.ShapeDtypeStruct(array.shape, array.dtype) for array in arrays],
        scratch_shapes=[pltpu.VMEM(array.shape, array.dtype) for array in arrays]
        + [pltpu.SemaphoreType.DMA((len(arrays),))] * 2,
        cost_estimate=pl.CostEstimate(flops=0, bytes_accessed=12 << 20, transcendentals=0),
    )(*arrays)


def layer_tail(far, near):
    rows, width = far.queries.shape
    count = 32
    sizes = {UP: (BLOCK, 4 * WIDE), DOWN: (4 * BLOCK, WIDE), CAPTION: (far.captions.shape[0] // count, WIDE)}
    total = len(PIECES)
    local = pl.BlockSpec(memory_space=pltpu.VMEM)
    anywhere = pl.BlockSpec(memory_space=pl.ANY)
    dma = pltpu.SemaphoreType.DMA
    scratch = Scratch(
        arena=pltpu.VMEM((16 * rows, width), BF16),
        sums=pltpu.VMEM((3, rows, width), F32),
        accum_k=pltpu.VMEM((3 * rows, LANES), F32),
        accum_v=pltpu.VMEM((3 * rows, LANES), F32),
        back_one=pltpu.VMEM((rows, width), BF16),
        back_two=pltpu.VMEM((rows, width), BF16),
        vec=pltpu.VMEM((8, width), F32),
        vec_in=pltpu.VMEM((6, 8, width), F32),
        tiles=pltpu.VMEM((SLOTS, 2, 2, 2, 4, BLOCK, WIDE), BF16),
        r0=pltpu.VMEM((LANDINGS, 2, 2, 4, BLOCK, WIDE), BF16),
        r1=pltpu.VMEM((total, 2, 4, BLOCK, WIDE), BF16),
        r2=pltpu.VMEM((total, 4, BLOCK, WIDE), BF16),
        r3=pltpu.VMEM((total, 3, BLOCK, WIDE), BF16),
        load=dma((LOADS,)), s0=dma((total,)), d0=dma((total,)), s1=dma((total,)), d1=dma((total,)),
        s2=dma((total,)), d2=dma((total,)), s3=dma((total, 3)), d3=dma((total, 3)), vs=dma((6,)), vd=dma((6,)),
        bs=dma((2,)), bd=dma((2,)), credit=pltpu.SemaphoreType.REGULAR,
    )
    results = pl.pallas_call(
        functools.partial(layer_kernel, rows),
        in_specs=[anywhere] * len(far) + [local] * len(near),
        out_specs=[local] * (len(Sums._fields) + 1) + [anywhere] * 2,
        out_shape=[jax.ShapeDtypeStruct(sizes.get(number, (BLOCK, WIDE)), F32) for number in range(len(Sums._fields))]
        + [
            jax.ShapeDtypeStruct((8, width), F32),
            jax.ShapeDtypeStruct((rows, width), BF16),
            jax.ShapeDtypeStruct((rows, width), F32),
        ],
        scratch_shapes=list(scratch),
        compiler_params=pltpu.CompilerParams(collective_id=0, has_side_effects=True, vmem_limit_bytes=63 << 20),
        cost_estimate=pl.CostEstimate(flops=1 << 34, bytes_accessed=64 << 20, transcendentals=0),
    )(*far, *near)
    small = results[len(Sums._fields)]
    copied = copy_all([*results[: len(Sums._fields)], *results[len(Sums._fields) + 1 :]])
    return Sums(*copied[:-2]), small, *copied[-2:]


def matmul(left, right):
    return jnp.dot(left, right, preferred_element_type=F32)


def left_product(left, right):
    return lax.dot_general(left, right, TN, preferred_element_type=F32)


def right_product(left, right):
    return lax.dot_general(left, right, NT, preferred_element_type=F32)


def normalise(value):
    mean = jnp.mean(value, axis=-1, keepdims=True)
    centred = value - mean
    scale = lax.rsqrt(jnp.mean(centred * centred, axis=-1, keepdims=True) + EPS)
    return centred * scale, scale


def norm_back(grad, unit, scale, gain):
    scaled = grad * gain
    return scale * (
        scaled
        - jnp.mean(scaled, axis=-1, keepdims=True)
        - unit * jnp.mean(scaled * unit, axis=-1, keepdims=True)
    )


def body(
    tokens, out_grad, caption_states,
    query_weight, key_weight, value_weight, output_weight,
    cross_query, cross_key, cross_value, cross_output,
    up_weight, down_weight,
    attn_gain, attn_bias, cross_gain, cross_bias, mlp_gain, mlp_bias,
    item_ids, caption_segments, item_rows, item_segments,
):
    device = lax.axis_index(AXIS)
    count = lax.axis_size(AXIS)
    rows = tokens.shape[0]
    tiles = rows // TILE
    odd = lax.rem(device, 2) == 1
    swap = [(i, i ^ 1) for i in range(count)]
    ahead = [(i, i + 2) for i in range(count - 2)]
    behind = [(i + 2, i) for i in range(count - 2)]

    inputs = tokens.astype(F32)
    low_one = (normalise(inputs)[0] * attn_gain + attn_bias).astype(BF16)
    queries = matmul(low_one, query_weight).astype(BF16)
    text_keys = matmul(caption_states, cross_key).astype(BF16)
    text_values = matmul(caption_states, cross_value).astype(BF16)
    block_two = lax.ppermute(tokens, AXIS, ahead)
    block_two, queries, text_keys, text_values = lax.optimization_barrier((block_two, queries, text_keys, text_values))
    block_one = lax.ppermute(jnp.where(odd, block_two, tokens), AXIS, swap)
    near_tokens = jnp.concatenate([block_two, block_one, tokens], 0)

    all_ids = jnp.concatenate([jnp.full((REACH * rows,), -1, jnp.int32), item_ids])
    near_ids = lax.dynamic_slice_in_dim(all_ids, device * rows, (REACH + 1) * rows)
    own_ids = near_ids[REACH * rows :]
    near_rows = (REACH + 1) * rows
    span = REACH * rows + TILE
    windows = jnp.stack([near_ids[t * TILE : t * TILE + span] for t in range(tiles)])
    firsts = own_ids[::TILE]
    before = jnp.sum((near_ids[None, :] < firsts[:, None]).astype(jnp.int32), axis=1)
    lasts = REACH * rows + TILE * (1 + jnp.arange(tiles, dtype=jnp.int32))
    numbers = lasts // TILE - before // TILE
    numbers = jnp.clip(numbers, 1, span // TILE)
    self_sizes = tuple(TILE * (i + 1) for i in range(span // TILE))
    self_ends = (REACH * rows + TILE, TILE)

    text = caption_states.shape[0]
    caption_len = caption_segments.shape[1]
    member = own_ids[:, None] == jnp.arange(item_rows.shape[0], dtype=jnp.int32)[None, :]
    codes = item_rows * caption_len + item_segments
    query_code = jnp.sum(jnp.where(member, codes[None, :], 0), axis=1)
    key_code = (jnp.arange(text, dtype=jnp.int32) // caption_len) * caption_len + caption_segments.reshape(-1)
    text_code = jnp.broadcast_to(key_code[None], (tiles, text))
    no_numbers = jnp.zeros((tiles,), jnp.int32)
    text_ends = (text, 0)

    near_unit, near_scale = normalise(near_tokens.astype(F32))
    near_low = (near_unit * attn_gain + attn_bias).astype(BF16)
    near_keys = matmul(near_low, key_weight).astype(BF16)
    near_values = matmul(near_low, value_weight).astype(BF16)
    self_att, self_lse = attend_forward(
        queries, near_keys, near_values, own_ids[:, None], windows[:, None, :], numbers, True, self_sizes, self_ends
    )
    after_one = inputs + matmul(self_att, output_weight)
    unit_two, scale_two = normalise(after_one)
    low_two = (unit_two * cross_gain + cross_bias).astype(BF16)
    cross_q = matmul(low_two, cross_query).astype(BF16)
    cross_att, cross_lse = cross_forward(
        cross_q, text_keys, text_values, query_code[:, None], key_code.reshape(-1, caption_len)
    )
    after_two = after_one + matmul(cross_att, cross_output)
    unit_three, scale_three = normalise(after_two)
    low_three = (unit_three * mlp_gain + mlp_bias).astype(BF16)
    width = tokens.shape[1]
    if count == 32:
        starts = jnp.sum((near_ids[None, :] < own_ids[:, None]).astype(jnp.int32), axis=1)
        sums, small, block_output, input_grad = layer_tail(
            Far(
                low_three=low_three, out_grad=out_grad, after_two=after_two,
                up_weight=up_weight, down_weight=down_weight,
                cross_att=cross_att, cross_q=cross_q, text_keys=text_keys, text_values=text_values,
                low_two=low_two, after_one=after_one, captions=caption_states,
                cross_output=cross_output, cross_key=cross_key, cross_value=cross_value, cross_query=cross_query,
                output_weight=output_weight,
                queries=queries, near_keys=near_keys, near_values=near_values, self_att=self_att,
                near_low=near_low, near_tokens=near_tokens,
                query_weight=query_weight, key_weight=key_weight, value_weight=value_weight,
            ),
            Near(
                starts=starts[None, :], self_lse=self_lse, query_code=query_code[None, :], key_code=key_code[:, None],
                cross_lse=cross_lse, gains=jnp.stack([attn_gain, cross_gain, mlp_gain]),
            ),
        )
        small = lax.dynamic_slice_in_dim(small, device * (width // count), width // count, 1)
    else:
        hidden_pre = matmul(low_three, up_weight)
        hidden, slope = gelu_and_slope(hidden_pre)
        hidden_low = hidden.astype(BF16)
        grad_pre = (slope * right_product(out_grad, down_weight)).astype(BF16)
        block_output = (after_two + matmul(hidden_low, down_weight)).astype(BF16)

        down_grad = left_product(hidden_low, out_grad).astype(BF16)
        up_grad = left_product(low_three, grad_pre).astype(BF16)
        z_, y_, x_, c_ = 0, 1, 2, 3
        one_way = (c_, x_, y_, z_) if len(factors(count)) == 4 else (0,)
        other_way = (c_, y_, x_, z_) if len(factors(count)) == 4 else (0,)
        grad_three = right_product(grad_pre, up_weight)
        mlp_gain_grad = jnp.sum(grad_three * unit_three, axis=0)
        mlp_bias_grad = jnp.sum(grad_three, axis=0)
        grad_two = out_grad.astype(F32) + norm_back(grad_three, unit_three, scale_three, mlp_gain)
        grad_two_low = grad_two.astype(BF16)

        cross_output_grad = left_product(cross_att, grad_two_low).astype(BF16)
        grad_cross = right_product(grad_two_low, cross_output).astype(BF16)
        grad_cq, grad_tk, grad_tv = attend_backward(
            cross_q, text_keys, text_values, grad_cross, cross_att, cross_lse,
            query_code[None, :], text_code[:, :, None], no_numbers, False, (text,), text_ends,
        )
        width = grad_tk.shape[1]
        cross_key_grad = left_product(caption_states, grad_tk).astype(BF16)
        cross_value_grad = left_product(caption_states, grad_tv).astype(BF16)
        caption_grad = (right_product(grad_tk, cross_key) + right_product(grad_tv, cross_value)).astype(BF16)
        cross_query_grad = left_product(low_two, grad_cq).astype(BF16)
        grad_norm_two = right_product(grad_cq, cross_query)
        cross_gain_grad = jnp.sum(grad_norm_two * unit_two, axis=0)
        cross_bias_grad = jnp.sum(grad_norm_two, axis=0)
        grad_one = grad_two + norm_back(grad_norm_two, unit_two, scale_two, cross_gain)
        grad_one_low = grad_one.astype(BF16)

        output_weight_grad = left_product(self_att, grad_one_low).astype(BF16)
        grad_self = right_product(grad_one_low, output_weight).astype(BF16)
        grad_q, grad_k, grad_v = attend_backward(
            queries, near_keys, near_values, grad_self, self_att, self_lse,
            own_ids[None, :], windows[:, :, None], numbers, True, self_sizes, self_ends,
        )
        grad_near = right_product(grad_k, key_weight) + right_product(grad_v, value_weight)
        grad_own = grad_near[REACH * rows :] + right_product(grad_q, query_weight)
        to_two = grad_near[:rows]
        to_one = grad_near[rows : REACH * rows].astype(BF16)
        from_swap = lax.ppermute(to_one, AXIS, swap).astype(F32)
        to_two = (to_two + jnp.where(odd, from_swap, 0.0)).astype(BF16)
        from_two = lax.ppermute(to_two, AXIS, behind).astype(F32)
        near_sum = jnp.concatenate([grad_near[: REACH * rows], grad_own], 0)
        attn_gain_grad = jnp.sum(near_sum * near_unit, axis=0)
        attn_bias_grad = jnp.sum(near_sum, axis=0)
        grad_norm_one = grad_own + from_two + jnp.where(odd, 0.0, from_swap)
        unit_one = near_unit[REACH * rows :]
        input_grad = grad_one + norm_back(grad_norm_one, unit_one, near_scale[REACH * rows :], attn_gain)
        query_grad = left_product(low_one, grad_q).astype(BF16)
        key_grad = left_product(near_low, grad_k).astype(BF16)
        value_grad = left_product(near_low, grad_v).astype(BF16)
        vectors = jnp.stack(
            [attn_gain_grad, attn_bias_grad, cross_gain_grad, cross_bias_grad, mlp_gain_grad, mlp_bias_grad]
        )
        grads = [
            down_grad, up_grad, cross_output_grad, cross_query_grad, cross_key_grad, cross_value_grad, output_weight_grad,
        ]
        sums = [
            reduce_scatter(grad, one_way if i % 2 else other_way, BF16, count)
            for i, grad in enumerate([*grads, query_grad, key_grad, value_grad, caption_grad])
        ]
        small = reduce_scatter(vectors.T, one_way, F32, count).T
        (down_out, up_out, cross_output_out, cross_query_out, cross_key_out, cross_value_out,
         output_out, query_out, key_out, value_out, caption_out) = sums
        sums = Sums(
            up=up_out, down=down_out, cross_output=cross_output_out, cross_key=cross_key_out,
            cross_value=cross_value_out, caption=caption_out, cross_query=cross_query_out, output=output_out,
            query=query_out, key=key_out, value=value_out,
        )
    return (
        block_output, input_grad, sums.caption,
        sums.query, sums.key, sums.value, sums.output,
        sums.cross_query, sums.cross_key, sums.cross_value, sums.cross_output,
        sums.up, sums.down,
        small[0], small[1], small[2], small[3], small[4], small[5],
    )


def solution(mesh):
    split = P(AXIS, None)
    return jax.shard_map(
        body,
        mesh=mesh,
        in_specs=(split, split) + (P(),) * 21,
        out_specs=(split,) * 13 + (P(AXIS),) * 6,
        check_vma=False,
    )
```
